32 devices in a mesh: section: 2 (over x), dp: 16 (over z, y, core).
Axes of the slice: x: 2, y: 2, z: 4, core: 2. Of those that a mesh axis runs over, the one named last changes fastest.
Arguments:
- embedded: bfloat16 [2, 16384, 512], P('section', 'dp'), may hold values from -6 to 6
- lengths: int32 [2, 32, 8], P('section', 'dp'), may hold values from 0 to 512, as said below
- cotangent: bfloat16 [2, 16384, 512], P('section', 'dp'), may hold values from -6 to 6
- attn_in: bfloat16 [2, 512, 1536], P('section', 'dp'), may hold values from -0.25 to 0.25
- attn_out: bfloat16 [2, 512, 512], P('section', 'dp'), may hold values from -1 to 1
- cross_weight: bfloat16 [2, 512, 1024], P('section', 'dp'), may hold values from -0.375 to 0.375
- up_weight: bfloat16 [2, 512, 2048], P('section', 'dp'), may hold values from -0.25 to 0.25
- down_weight: bfloat16 [2, 2048, 512], P('section', 'dp'), may hold values from -0.125 to 0.125
- norm_gain: float32 [2, 3, 512], P('section'), may hold values from 0.5 to 1.5
- norm_bias: float32 [2, 3, 512], P('section'), may hold values from -1.5 to 1.5
Outputs:
- result: bfloat16 [2, 16384, 512], P('section', 'dp')
- input_grads: bfloat16 [2, 16384, 512], P('section', 'dp')
- attn_in_grad: float32 [2, 512, 1536], P('section')
- attn_out_grad: float32 [2, 512, 512], P('section')
- cross_grad: float32 [2, 512, 1024], P('section')
- up_grad: float32 [2, 512, 2048], P('section')
- down_grad: float32 [2, 2048, 512], P('section')
- gain_grad: float32 [2, 3, 512], P('section')
- bias_grad: float32 [2, 3, 512], P('section')
The draws below stay inside these ranges and needn't reach their ends.
Inputs may be any that keep to these rules, and one draw needn't show every extreme that they name: `lengths`: each row's 8 entries sum to 512. Entry j of a source row is 0 exactly when entry j of the same target row is 0, and only entries after the first can be 0.
All inputs are finite; a program needn't handle non-finite values.
Results may differ from the reference program's by a relative error of at most 0.02.
Values may be sent and summed in bfloat16 or wider, within the bound.
A program may use at most 320 MiB of HBM per device.

```python
import math
from functools import partial
import jax
import jax.numpy as jnp
from jax import lax

D = 512
HEADS = 8
FF = 2048
ROW = 512
SEGS = 8
ROWS = 32
TOKENS = 16384


def draw_lengths(key, part):
    key = jax.random.fold_in(key, 17)
    order_key, pick_key = jax.random.split(key)
    row_keys = jax.random.split(order_key, 2 * ROWS)
    shuffled = jax.vmap(partial(jax.random.permutation, x=ROW - 1))(row_keys)
    cuts = jnp.sort(shuffled[:, :SEGS - 1], axis=1).astype(jnp.int32) + 1
    bounds = jnp.concatenate([jnp.zeros((2 * ROWS, 1), jnp.int32), cuts, jnp.full((2 * ROWS, 1), ROW, jnp.int32)], axis=1)
    spans = (bounds[:, 1:] - bounds[:, :-1]).reshape(2, ROWS, SEGS)
    chosen = jax.random.randint(pick_key, (), 0, ROWS)
    single = jnp.where(jnp.arange(SEGS) == 0, ROW, 0).astype(jnp.int32)
    row_index = jnp.arange(ROWS)
    return jnp.where((row_index == chosen)[None, :, None], single[None, None, :], spans).astype(jnp.int32)


def level_of(own_key, shape, cuts, low, high):
    factor_of, own = 1.0, jax.random.fold_in(own_key, 6)
    for axis_at, shards_of in cuts:
        draws = jnp.exp(jax.random.uniform(jax.random.fold_in(own, axis_at), (shards_of,), jnp.float32, low / len(cuts), high / len(cuts)))
        factor_of = factor_of * jnp.repeat(draws, shape[axis_at] // shards_of).reshape([-1 if axis == axis_at else 1 for axis in range(len(shape))])
    return factor_of


def scatter_about(stream_key, shape, scale, most, cuts=(), kind=jnp.bfloat16):
    values = scale * jax.random.normal(stream_key, shape, jnp.float32)
    if cuts:
        values = values * level_of(stream_key, shape, cuts, -0.22, 0.18)
    return jnp.clip(values, -most, most).astype(kind)


def setup_inputs(seed: int = 0) -> dict:
    keys = jax.random.split(jax.random.key(seed), 11)
    embedded = scatter_about(keys[0], (2, TOKENS, D), 1.0, 6.0, ((0, 2), (1, 16)))
    lengths = draw_lengths(jax.random.fold_in(keys[10], 71), 0)
    cotangent = scatter_about(keys[2], (2, TOKENS, D), 1.0, 6.0, ((0, 2), (1, 16)))
    attn_in = scatter_about(keys[3], (2, D, 3 * D), D ** -0.5, 0.25, ((0, 2), (1, 16)))
    attn_out = scatter_about(keys[4], (2, D, D), (D // 16) ** -0.5, 1.0, ((0, 2), (1, 16)))
    cross_weight = scatter_about(keys[5], (2, D, 2 * D), (D // 2) ** -0.5, 0.375, ((0, 2), (1, 16)))
    up_weight = scatter_about(keys[6], (2, D, FF), D ** -0.5, 0.25, ((0, 2), (1, 16)))
    down_weight = scatter_about(keys[7], (2, FF, D), FF ** -0.5, 0.125, ((0, 2), (1, 16)))
    norm_gain = jnp.clip(1.0 + 0.1 * jax.random.normal(keys[8], (2, 3, D), jnp.float32), 0.5, 1.5)
    norm_bias = scatter_about(keys[9], (2, 3, D), 0.3, 1.5, ((0, 2),), jnp.float32)
    return {"embedded": embedded, "lengths": lengths, "cotangent": cotangent, "attn_in": attn_in, "attn_out": attn_out, "cross_weight": cross_weight, "up_weight": up_weight, "down_weight": down_weight, "norm_gain": norm_gain, "norm_bias": norm_bias}


@jax.custom_vjp
def low(v):
    return lax.optimization_barrier(v.astype(jnp.bfloat16)).astype(jnp.float32)

@jax.custom_vjp
def low_back(v):
    return v

def low_keep(v):
    return (low(v), None)

def low_pass(kept, grad):
    return (grad,)

def back_keep(v):
    return (v, None)

def back_low(kept, grad):
    return (low(grad),)
low.defvjp(low_keep, low_pass)
low_back.defvjp(back_keep, back_low)
norm_eps = 1e-06
masked_score = -1e+30

def matmul_hi(left, right):
    return jnp.dot(left, right, precision=lax.Precision.HIGHEST, preferred_element_type=jnp.float32)

def layer_norm(values, gain, bias):
    center = lax.optimization_barrier(jnp.mean(values, axis=-1, keepdims=True))
    shifted = values - center
    spread = lax.optimization_barrier(jnp.mean(shifted * shifted, axis=-1, keepdims=True))
    return shifted * lax.rsqrt(spread + norm_eps) * gain + bias

def segment_ids(seg_lengths, width):
    seg_ends = jnp.cumsum(seg_lengths)
    positions = jnp.arange(width, dtype=jnp.int32)
    return lax.optimization_barrier(jnp.sum((positions[:, None] >= seg_ends[None, :]).astype(jnp.int32), axis=1))

def attend(queries, key_rows, value_rows, allowed):
    query_count = queries.shape[0]
    head_size = queries.shape[1] // HEADS
    query_heads = queries.reshape(query_count, HEADS, head_size)
    key_heads = key_rows.reshape(key_rows.shape[0], HEADS, head_size)
    value_heads = value_rows.reshape(value_rows.shape[0], HEADS, head_size)
    scores = jnp.einsum('qhd,khd->hqk', query_heads, key_heads, precision=lax.Precision.HIGHEST) * (1.0 / math.sqrt(head_size))
    scores = low_back(scores)
    masked = jnp.where(allowed[None], scores, masked_score)
    row_max = lax.optimization_barrier(jnp.max(masked, axis=-1, keepdims=True))
    raised = jnp.where(allowed[None], jnp.exp(masked - row_max), 0.0)
    attn_probs = low(raised / lax.optimization_barrier(jnp.sum(raised, axis=-1, keepdims=True)))
    attended = jnp.einsum('hqk,khd->qhd', attn_probs, value_heads, precision=lax.Precision.HIGHEST)
    return low(low_back(attended.reshape(query_count, -1)))

def self_block(inputs, allowed, in_weight, out_weight):
    model_width = out_weight.shape[0]
    qkv_rows = low(low_back(matmul_hi(inputs, in_weight)))
    attended = attend(qkv_rows[:, :model_width], qkv_rows[:, model_width:2 * model_width], qkv_rows[:, 2 * model_width:], allowed)
    return inputs + low_back(matmul_hi(attended, out_weight))

def feed_block(values, up_w, down_w):
    pre_act = low_back(matmul_hi(low(values), up_w))
    return values + low_back(matmul_hi(low(jax.nn.silu(pre_act)), down_w))

def one_row(params, source, target, source_len, target_len):
    in_w, out_w, cross_w, up_w, down_w, gain_rows, bias_rows = params
    model_width = out_w.shape[1]
    row_width = source.shape[0]
    source_ids = segment_ids(source_len, row_width)
    target_ids = segment_ids(target_len, row_width)
    positions = jnp.arange(row_width, dtype=jnp.int32)
    enc_mask = source_ids[:, None] == source_ids[None, :]
    first_out = layer_norm(self_block(source, enc_mask, in_w[0], out_w[0]), gain_rows[0, 0], bias_rows[0, 0])
    second = layer_norm(feed_block(first_out, up_w[0], down_w[0]), gain_rows[0, 1], bias_rows[0, 1])
    memory = layer_norm(second, gain_rows[0, 2], bias_rows[0, 2])
    key_values = low(low_back(matmul_hi(low(memory), cross_w[0])))
    dec_mask = (target_ids[:, None] == target_ids[None, :]) & (positions[None, :] <= positions[:, None])
    first_dec = layer_norm(self_block(target, dec_mask, in_w[1], out_w[1]), gain_rows[1, 0], bias_rows[1, 0])
    queries = low(low_back(matmul_hi(low(first_dec), cross_w[1][:, :model_width])))
    cross_mask = target_ids[:, None] == source_ids[None, :]
    crossed = attend(queries, key_values[:, :model_width], key_values[:, model_width:], cross_mask)
    second_dec = layer_norm(first_dec + low_back(matmul_hi(crossed, cross_w[1][:, model_width:])), gain_rows[1, 1], bias_rows[1, 1])
    third_out = layer_norm(feed_block(second_dec, up_w[1], down_w[1]), gain_rows[1, 2], bias_rows[1, 2])
    return (memory, third_out)

def reference(embedded, lengths, cotangent, attn_in, attn_out, cross_weight, up_weight, down_weight, norm_gain, norm_bias):
    group = math.gcd(ROWS, max(1, 4096 // ROW))
    blocks = ROWS // group
    source = embedded[0].astype(jnp.float32).reshape(blocks, group, ROW, D)
    target = embedded[1].astype(jnp.float32).reshape(blocks, group, ROW, D)
    src_lengths = lengths[0].reshape(blocks, group, SEGS)
    tgt_lengths = lengths[1].reshape(blocks, group, SEGS)
    params = (attn_in.astype(jnp.float32), attn_out.astype(jnp.float32), cross_weight.astype(jnp.float32), up_weight.astype(jnp.float32), down_weight.astype(jnp.float32), norm_gain, norm_bias)

    def forward(weights, source_all, target_all):

        def block_step(carry, pieces):
            src_block, tgt_block, src_len, tgt_len = pieces

            def rows_fn(inner_weights, src_rows, tgt_rows):
                return jax.vmap(lambda a, b, c, e: one_row(inner_weights, a, b, c, e))(src_rows, tgt_rows, src_len, tgt_len)
            return (carry, jax.checkpoint(rows_fn)(weights, src_block, tgt_block))
        unused, outputs = lax.scan(block_step, None, (source_all, target_all, src_lengths, tgt_lengths))
        return outputs
    (memory, third_out), pullback = jax.vjp(forward, params, source, target)
    cot_memory = cotangent[0].astype(jnp.float32).reshape(blocks, group, ROW, D)
    cot_decoder = cotangent[1].astype(jnp.float32).reshape(blocks, group, ROW, D)
    grads, grad_source, grad_target = pullback((cot_memory, cot_decoder))
    result = jnp.stack([memory.reshape(TOKENS, D), third_out.reshape(TOKENS, D)]).astype(jnp.bfloat16)
    input_grads = jnp.stack([grad_source.reshape(TOKENS, D), grad_target.reshape(TOKENS, D)]).astype(jnp.bfloat16)
    return (result, input_grads, grads[0], grads[1], grads[2], grads[3], grads[4], grads[5], grads[6])
```

```python
import functools
import math

import jax
import jax.numpy as jnp
from jax import lax
from jax.experimental import pallas as pl
from jax.experimental.pallas import tpu as pltpu
from jax.sharding import PartitionSpec as P

HEADS = 8

norm_eps = 1e-06
masked_score = -1e30
F32 = jnp.float32
BF16 = jnp.bfloat16
MESH = pl.DeviceIdType.MESH
LINE = 4
CALL_ROWS = 2
TILE = 512


def matmul_nn(left, right):
    return jnp.dot(left, right, preferred_element_type=F32)


def matmul_tn(left, right):
    return lax.dot_general(left, right, (((0,), (0,)), ((), ())), preferred_element_type=F32)


def matmul_nt(left, right):
    return lax.dot_general(left, right, (((1,), (1,)), ((), ())), preferred_element_type=F32)


class Slots:
    def __init__(self, rows, ff_tiles):
        self.rows = rows
        self.count = 0
        self.qkv = self.take(3 * rows)
        self.cq = self.take(rows)
        self.kv = self.take(2 * rows)
        self.pre = self.take(ff_tiles * rows)
        self.hid = self.take(ff_tiles * rows)
        self.att = self.take(rows)
        self.oc = self.take(rows)
        self.first = self.take(rows)
        self.second = self.take(rows)
        self.mem = self.take(rows)
        self.gmem = self.take(rows)
        self.gdown = self.take(rows)
        self.gout = self.take(rows)
        self.gcross = self.take(rows)
        self.stage = self.take(rows)
        self.dout = self.take(1)
        self.xhat = self.take(3 * rows)

    def take(self, n):
        at = self.count
        self.count += n
        return at


class Body:
    def __init__(self, inner, rows, dp, ff_tiles, refs):
        self.inner = inner
        self.rows = rows
        self.ff_tiles = ff_tiles
        self.at = Slots(rows, ff_tiles)
        names = ["emb", "cot", "lengths", "gain", "bias"]
        names += ["w_in", "w_out", "w_cross", "w_up", "w_down"]
        if not inner:
            names += ["w_memory"]
        names += ["result", "grad_in", "grads", "small", "spill"]
        names += ["act", "probs", "res", "tmp", "mask", "rstd", "gacc", "own_len", "src_len"]
        names += ["local_sem", "x_send", "x_recv"]
        if not inner:
            names += ["grad_sem"]
        if inner:
            names += ["wt", "wd", "x_shard", "x_grad", "r1", "r2", "r3", "gbuf", "grcv"]
            names += ["gz_s", "gz_r", "gy_s", "gy_r", "gc_s", "gc_r"]
            names += ["a1_s", "a1_r", "a2_s", "a2_r", "a3_s", "a3_r"]
            names += ["a4_s", "a4_r", "a5_s", "a5_r", "a6_s", "a6_r", "own_sem", "gs_s", "gs_r"]
        assert len(names) == len(refs), (len(names), len(refs))
        for name, ref in zip(names, refs):
            setattr(self, name, ref)
        self.sec = lax.axis_index("section")
        self.i = lax.axis_index("dp")
        self.across = (1 - self.sec, self.i)
        if inner:
            self.c = lax.rem(self.i, 2)
            self.y = lax.rem(self.i // 2, 2)
            self.z = self.i // 4
            self.core_dev = (self.sec, self.z * 4 + self.y * 2 + (1 - self.c))
            self.y_dev = (self.sec, self.z * 4 + (1 - self.y) * 2 + self.c)
            self.z_other = [lax.rem(self.z + d, LINE) for d in range(1, LINE)]
            self.z_dev = [(self.sec, zz * 4 + self.y * 2 + self.c) for zz in self.z_other]
        self.pending = []
        self.encoding = True
        self.t_in = 0
        self.t_out = 3
        self.t_cross = 4
        self.t_up = 6
        self.t_down = 6 + ff_tiles
        self.t_all = 6 + 2 * ff_tiles
        self.t_mem = self.t_all
        self.w_memory_at = 6
        self.w_up_at = 8


    def remote(self, src, dst, send, recv, dev):
        return pltpu.make_async_remote_copy(
            src_ref=src, dst_ref=dst, send_sem=send, recv_sem=recv, device_id=dev, device_id_type=MESH
        )

    def send(self, src, dst, send, recv, dev):
        copy = self.remote(src, dst, send, recv, dev)
        copy.start()
        self.pending.append(copy)

    def drain(self):
        for copy in self.pending:
            copy.wait_send()
        self.pending = []

    def barrier(self):
        sem = pltpu.get_barrier_semaphore()
        devs = [self.across]
        if self.inner:
            devs += [self.core_dev, self.y_dev] + self.z_dev
        for dev in devs:
            pl.semaphore_signal(sem, inc=1, device_id=dev, device_id_type=MESH)
        pl.semaphore_wait(sem, len(devs))


    def weight(self, k):
        if self.inner:
            return self.wt[k].reshape(TILE, TILE)
        if k < 3:
            return self.w_in[:, k * TILE : (k + 1) * TILE]
        if k == 3:
            return self.w_out[...]
        if k < 6:
            return self.w_cross[:, (k - 4) * TILE : (k - 3) * TILE]
        if k < 8:
            return self.w_memory[:, (k - 6) * TILE : (k - 5) * TILE]
        return self.w_up[:, (k - 8) * TILE : (k - 7) * TILE]

    def weight_down(self, t):
        if self.inner:
            return self.wd[t].reshape(TILE, TILE)
        return self.w_down[t * TILE : (t + 1) * TILE, :]

    def chunk_source(self, k):
        shard = TILE // 16
        z, y, c = self.z, self.y, self.c
        down_at = self.w_up_at + self.ff_tiles
        if k < 3:
            src = self.w_in.at[:, pl.ds(k * TILE, TILE)]
        elif k == 3:
            src = self.w_out.at[...]
        elif k < 6:
            src = self.w_cross.at[:, pl.ds((k - 4) * TILE, TILE)]
        elif k < 8:
            src = self.x_shard.at[:, pl.ds((k - 6) * TILE, TILE)]
        elif k < down_at:
            src = self.w_up.at[:, pl.ds((k - 8) * TILE, TILE)]
        else:
            src = self.w_down.at[pl.ds((k - down_at) * shard, shard), :]
        if k < down_at:
            whole = self.wt.at[k]
            own = whole.at[z, y, c]
            line = whole.at[:, y, c]
            plane = whole.at[:, :, c]
        else:
            band = pl.ds((k - down_at) * shard, shard)
            own = self.wd.at[z, y, c, band]
            line = self.wd.at[:, y, c, band]
            plane = self.wd.at[:, :, c, band]
        return src, own, line, plane

    def gather1(self, k):
        src, own, line, plane = self.chunk_source(k)
        own[...] = src[...]
        for d in range(LINE - 1):
            self.send(src, own, self.gz_s.at[k, d], self.gz_r.at[k, d], self.z_dev[d])

    def gather2(self, k):
        src, own, line, plane = self.chunk_source(k)
        for d in range(LINE - 1):
            self.remote(src, own, self.gz_s.at[k, d], self.gz_r.at[k, d], self.z_dev[d]).wait_recv()
        self.send(line, line, self.gy_s.at[k], self.gy_r.at[k], self.y_dev)

    def gather3(self, k):
        src, own, line, plane = self.chunk_source(k)
        self.remote(line, line, self.gy_s.at[k], self.gy_r.at[k], self.y_dev).wait_recv()
        self.send(plane, plane, self.gc_s.at[k], self.gc_r.at[k], self.core_dev)

    def gather4(self, k):
        src, own, line, plane = self.chunk_source(k)
        self.remote(plane, plane, self.gc_s.at[k], self.gc_r.at[k], self.core_dev).wait_recv()

    def pipeline(self, items, stages):
        for step in range(len(items) + len(stages) - 1):
            for back in reversed(range(len(stages))):
                n = step - back
                if 0 <= n < len(items):
                    stages[back](items[n])
            yield step


    def tile_slot(self, k):
        at, rows = self.at, self.rows
        if k < 3:
            return at.qkv + k * rows
        if k == 3:
            return at.gout
        if k == 4:
            return at.cq
        if k == 5:
            return at.gcross
        if k < self.t_down:
            return at.pre + (k - self.t_up) * rows
        if k < self.t_all:
            return at.hid + (k - self.t_down) * rows
        return at.kv + (k - self.t_mem) * rows

    def from_partner(self, k):
        return self.encoding and k in (self.t_cross, self.t_cross + 1)

    def block_at(self, c, y=0, z=0):
        return c * (TILE // 2) + y * (TILE // 4) + z * (TILE // 16)

    def reduce1(self, k):
        if self.from_partner(k):
            return
        slot = self.tile_slot(k)
        half = TILE // 2
        src = self.act.at[slot, pl.ds(self.block_at(1 - self.c), half)]
        self.send(src, self.r1.at[k], self.a1_s.at[k], self.a1_r.at[k], self.core_dev)

    def reduce2(self, k):
        if self.from_partner(k):
            return
        slot = self.tile_slot(k)
        half, quarter = TILE // 2, TILE // 4
        own = pl.ds(pl.multiple_of(self.block_at(self.c), half), half)
        src = self.act.at[slot, own]
        self.remote(src, self.r1.at[k], self.a1_s.at[k], self.a1_r.at[k], self.core_dev).wait_recv()
        total = self.act[slot, own].astype(F32) + self.r1[k].astype(F32)
        self.act[slot, own] = total.astype(BF16)
        src = self.act.at[slot, pl.ds(self.block_at(self.c, 1 - self.y), quarter)]
        self.send(src, self.r2.at[k], self.a2_s.at[k], self.a2_r.at[k], self.y_dev)

    def reduce3(self, k):
        if self.from_partner(k):
            return
        slot = self.tile_slot(k)
        quarter, part = TILE // 4, TILE // 16
        own = pl.ds(pl.multiple_of(self.block_at(self.c, self.y), quarter), quarter)
        src = self.act.at[slot, own]
        self.remote(src, self.r2.at[k], self.a2_s.at[k], self.a2_r.at[k], self.y_dev).wait_recv()
        total = self.act[slot, own].astype(F32) + self.r2[k].astype(F32)
        self.act[slot, own] = total.astype(BF16)
        for d in range(LINE - 1):
            src = self.act.at[slot, pl.ds(self.block_at(self.c, self.y, self.z_other[d]), part)]
            self.send(src, self.r3.at[k, d], self.a3_s.at[k, d], self.a3_r.at[k, d], self.z_dev[d])

    def reduce4(self, k):
        if self.from_partner(k):
            return self.reduce4_memory(k)
        slot = self.tile_slot(k)
        part = TILE // 16
        own = pl.ds(pl.multiple_of(self.block_at(self.c, self.y, self.z), part), part)
        src = self.act.at[slot, own]
        total = self.act[slot, own].astype(F32)
        for d in range(LINE - 1):
            self.remote(
                src, self.r3.at[k, d], self.a3_s.at[k, d], self.a3_r.at[k, d], self.z_dev[d]
            ).wait_recv()
            total = total + self.r3[k, d].astype(F32)
        self.act[slot, own] = total.astype(BF16)
        if k < self.t_all:
            self.spread(k, src)
        else:
            j = k - self.t_mem
            dst = self.x_grad.at[j]
            self.send(src, dst, self.x_send.at[6 + j], self.x_recv.at[6 + j], self.across)

    def spread(self, k, src):
        part = TILE // 16
        dst = self.grads.at[k, pl.ds(self.block_at(self.c, self.y, self.z), part)]
        pltpu.make_async_copy(src, dst, self.own_sem.at[k]).start()
        for d in range(LINE - 1):
            self.send(src, dst, self.a4_s.at[k, d], self.a4_r.at[k, d], self.z_dev[d])

    def reduce4_memory(self, k):
        j = k - self.t_cross
        src = self.x_grad.at[j]
        self.remote(src, src, self.x_send.at[6 + j], self.x_recv.at[6 + j], self.across).wait_recv()
        self.spread(k, src)

    def reduce5(self, k):
        if k >= self.t_all:
            return
        quarter, part = TILE // 4, TILE // 16
        own = self.grads.at[k, pl.ds(self.block_at(self.c, self.y, self.z), part)]
        pltpu.make_async_copy(own, own, self.own_sem.at[k]).wait()
        for d in range(LINE - 1):
            self.remote(
                own, own, self.a4_s.at[k, d], self.a4_r.at[k, d], self.z_dev[d]
            ).wait_recv()
        line = self.grads.at[k, pl.ds(self.block_at(self.c, self.y), quarter)]
        self.send(line, line, self.a5_s.at[k], self.a5_r.at[k], self.y_dev)

    def reduce6(self, k):
        if k >= self.t_all:
            return
        half, quarter = TILE // 2, TILE // 4
        line = self.grads.at[k, pl.ds(self.block_at(self.c, self.y), quarter)]
        self.remote(line, line, self.a5_s.at[k], self.a5_r.at[k], self.y_dev).wait_recv()
        plane = self.grads.at[k, pl.ds(self.block_at(self.c), half)]
        self.send(plane, plane, self.a6_s.at[k], self.a6_r.at[k], self.core_dev)

    def reduce7(self, k):
        if k >= self.t_all:
            return
        plane = self.grads.at[k, pl.ds(self.block_at(self.c), TILE // 2)]
        self.remote(plane, plane, self.a6_s.at[k], self.a6_r.at[k], self.core_dev).wait_recv()

    def small1(self):
        for j in range(6):
            self.gbuf[0, pl.ds(j, 1), :] = jnp.sum(self.gacc[j], axis=0, keepdims=True)
        self.gbuf[0, pl.ds(6, 2), :] = jnp.zeros((2, TILE), F32)
        self.send(self.gbuf.at[0], self.grcv.at[0], self.gs_s.at[0], self.gs_r.at[0], self.core_dev)

    def small2(self):
        self.remote(
            self.gbuf.at[0], self.grcv.at[0], self.gs_s.at[0], self.gs_r.at[0], self.core_dev
        ).wait_recv()
        self.gbuf[1] = self.gbuf[0] + self.grcv[0]
        self.send(self.gbuf.at[1], self.grcv.at[1], self.gs_s.at[1], self.gs_r.at[1], self.y_dev)

    def small3(self):
        self.remote(
            self.gbuf.at[1], self.grcv.at[1], self.gs_s.at[1], self.gs_r.at[1], self.y_dev
        ).wait_recv()
        self.gbuf[2] = self.gbuf[1] + self.grcv[1]
        for d in range(LINE - 1):
            self.send(
                self.gbuf.at[2],
                self.grcv.at[2 + self.z],
                self.gs_s.at[2 + d],
                self.gs_r.at[2 + d],
                self.z_dev[d],
            )
        self.grcv[2 + self.z] = self.gbuf[2]

    def small4(self):
        for d in range(LINE - 1):
            self.remote(
                self.gbuf.at[2],
                self.grcv.at[2 + self.z],
                self.gs_s.at[2 + d],
                self.gs_r.at[2 + d],
                self.z_dev[d],
            ).wait_recv()
        total = self.grcv[2]
        for n in range(1, LINE):
            total = total + self.grcv[2 + n]
        self.small[...] = total


    def fill_mask(self, r, key_len, causal):
        lane = lax.broadcasted_iota(jnp.int32, (8, 128), 1)
        sub = lax.broadcasted_iota(jnp.int32, (8, 128), 0)

        def ends_of(ref):
            spans = jnp.broadcast_to(ref[pl.ds(r, 1), :], (8, 128))
            return jnp.sum(jnp.where(lane <= sub, spans, 0).astype(F32), axis=1, keepdims=True)

        ends = ends_of(self.own_len)
        flat = jnp.sum(jnp.where(lane == sub, ends, 0.0), axis=0, keepdims=True)
        flat = jnp.where(lane[:1] < 8, flat, 1e9)
        pos = lax.broadcasted_iota(jnp.int32, (TILE, 128), 0).astype(F32)
        query_ids = jnp.sum(jnp.where(pos >= flat, 1.0, 0.0), axis=1, keepdims=True)
        key_ends = ends_of(key_len)
        pos = lax.broadcasted_iota(jnp.int32, (8, TILE), 1).astype(F32)
        key_ids = jnp.sum(jnp.where(pos >= key_ends, 1.0, 0.0), axis=0, keepdims=True)
        step = 128
        for b in range(TILE // step):
            allowed = query_ids[b * step : (b + 1) * step] == key_ids
            if causal:
                q_pos = lax.broadcasted_iota(jnp.int32, (step, TILE), 0) + b * step
                k_pos = lax.broadcasted_iota(jnp.int32, (step, TILE), 1)
                allowed = allowed & (k_pos <= q_pos)
            self.mask[b * step : (b + 1) * step, :] = jnp.where(allowed, 0.0, masked_score)


    def attend(self, q, k, v, out, r):
        act = self.act
        low = lax.broadcasted_iota(jnp.int32, (1, 128), 1) < 64

        def pair(hp, carry):
            cols = pl.ds(pl.multiple_of(hp * 128, 128), 128)
            qs, ks, vs = act[q, :, cols], act[k, :, cols], act[v, :, cols]
            outs = []
            for j in range(2):
                qm = jnp.where(low if j == 0 else ~low, qs, jnp.zeros_like(qs))
                scores = matmul_nt(qm, ks) + self.mask[...]
                top = jnp.max(scores, axis=-1, keepdims=True)
                raised = jnp.exp(scores - top)
                total = jnp.sum(raised, axis=-1, keepdims=True)
                probs = (raised * (1.0 / total)).astype(BF16)
                self.probs[r, hp * 2 + j] = probs
                outs.append(matmul_nn(probs, vs))
            act[out, :, cols] = jnp.where(low, outs[0], outs[1]).astype(BF16)
            return carry

        lax.fori_loop(0, HEADS // 2, pair, 0)

    def attend_back(self, q, k, v, out, dout, r, first, last):
        act = self.act
        low = lax.broadcasted_iota(jnp.int32, (1, 128), 1) < 64

        def pair(hp, carry):
            cols = pl.ds(pl.multiple_of(hp * 128, 128), 128)
            qs, ks, vs = act[q, :, cols], act[k, :, cols], act[v, :, cols]
            do = act[dout, :, cols]
            prod = do.astype(F32) * act[out, :, cols].astype(F32)
            none = jnp.zeros_like(do)
            dq = dk = dv = None
            for j in range(2):
                mine = low if j == 0 else ~low
                dom = jnp.where(mine, do, none)
                delta = jnp.sum(jnp.where(mine, prod, 0.0), axis=-1, keepdims=True)
                probs = self.probs[r, hp * 2 + j]
                ds = (probs.astype(F32) * (matmul_nt(dom, vs) - delta)).astype(BF16)
                a = matmul_nn(ds, jnp.where(mine, ks, none))
                b = matmul_tn(ds, jnp.where(mine, qs, none))
                c = matmul_tn(probs, dom)
                dq, dk, dv = (a, b, c) if j == 0 else (dq + a, dk + b, dv + c)
            act[q, :, cols] = (dq * 0.125).astype(BF16)
            act[k, :, cols] = dk.astype(BF16)
            act[v, :, cols] = dv.astype(BF16)
            return carry

        lax.fori_loop(first, last, pair, 0)


    def blocks(self, body):
        step = 128

        def one(b, carry):
            body(pl.ds(pl.multiple_of(b * step, step), step))
            return carry

        lax.fori_loop(0, TILE // step, one, 0)

    def norm(self, values, n, r, rows):
        center = jnp.mean(values, axis=-1, keepdims=True)
        shifted = values - center
        scale = lax.rsqrt(jnp.mean(shifted * shifted, axis=-1, keepdims=True) + norm_eps)
        hat = shifted * scale
        self.act[self.at.xhat + n * self.rows + r, rows] = hat.astype(BF16)
        self.rstd[r, rows, pl.ds(n, 1)] = scale
        return hat * self.gain[pl.ds(n, 1), :] + self.bias[pl.ds(n, 1), :]

    def norm_back(self, grad, n, r, rows):
        hat = self.act[self.at.xhat + n * self.rows + r, rows].astype(F32)
        scale = self.rstd[r, rows, pl.ds(n, 1)]
        count = grad.shape[0] // 8
        self.gacc[n] += jnp.sum((grad * hat).reshape(count, 8, TILE), axis=0)
        self.gacc[3 + n] += jnp.sum(grad.reshape(count, 8, TILE), axis=0)
        up = grad * self.gain[pl.ds(n, 1), :]
        first = jnp.mean(up, axis=-1, keepdims=True)
        second = jnp.mean(up * hat, axis=-1, keepdims=True)
        return (up - first - hat * second) * scale


    def self_in(self, r):
        x = self.emb[pl.ds(r * TILE, TILE), :]
        for j in range(3):
            rows = matmul_nn(x, self.weight(j)).astype(BF16)
            if j == 0:
                rows = rows * jnp.asarray(0.125, BF16)
            self.act[self.at.qkv + j * self.rows + r] = rows

    def self_attend(self, r, causal):
        at = self.at
        self.fill_mask(r, self.own_len, causal)
        q, k, v = (at.qkv + j * self.rows + r for j in range(3))
        self.attend(q, k, v, at.att + r, r)

    def self_out(self, r):
        at = self.at
        self.tmp[...] = matmul_nn(self.act[at.att + r], self.weight(3))

        def block(rows):
            x = self.emb[pl.ds(pl.multiple_of(r * TILE + rows.start, 128), rows.size), :]
            out = self.norm(x.astype(F32) + self.tmp[rows], 0, r, rows)
            self.res[r, rows] = out
            self.act[at.first + r, rows] = out.astype(BF16)

        self.blocks(block)

    def feed(self, x_slot, r):
        at = self.at
        x = self.act[x_slot]
        total = None
        for t in range(self.ff_tiles):
            pre = matmul_nn(x, self.weight(self.w_up_at + t))
            hid = (pre / (1.0 + jnp.exp(-pre))).astype(BF16)
            self.act[at.pre + t * self.rows + r] = pre.astype(BF16)
            self.act[at.hid + t * self.rows + r] = hid
            part = matmul_nn(hid, self.weight_down(t))
            total = part if total is None else total + part
        self.tmp[...] = total

    def feed_back(self, r):
        at = self.at
        grad = self.act[at.gdown + r]
        total = None
        for t in range(self.ff_tiles):
            dh = matmul_nt(grad, self.weight_down(t))
            pre = self.act[at.pre + t * self.rows + r].astype(F32)
            s = 1.0 / (1.0 + jnp.exp(-pre))
            dp = (dh * (s * (1.0 + pre * (1.0 - s)))).astype(BF16)
            self.act[at.pre + t * self.rows + r] = dp
            part = matmul_nt(dp, self.weight(self.w_up_at + t))
            total = part if total is None else total + part
        self.tmp[...] = total

    def self_back_out(self, r):
        at = self.at
        self.act[at.dout] = matmul_nt(self.act[at.gout + r], self.weight(3)).astype(BF16)

    def self_back_attend(self, r, first, last):
        at = self.at
        q, k, v = (at.qkv + j * self.rows + r for j in range(3))
        self.attend_back(q, k, v, at.att + r, at.dout, r, first, last)

    def self_back_in(self, r):
        at = self.at
        total = self.res[r]
        for j in range(3):
            total = total + matmul_nt(self.act[at.qkv + j * self.rows + r], self.weight(j))
        self.act[at.stage + r] = total.astype(BF16)

    def both(self, slot):
        return self.act[pl.ds(slot, self.rows)].reshape(self.rows * TILE, TILE)

    def weight_grad(self, k, left, right):
        self.act[self.tile_slot(k)] = matmul_tn(left, right).astype(BF16)

    def feed_grads(self, x_slot):
        at, rows = self.at, self.rows
        x = self.both(x_slot)
        grad = self.both(at.gdown)
        for t in range(self.ff_tiles):
            self.weight_grad(self.t_down + t, self.both(at.hid + t * rows), grad)
        for t in range(self.ff_tiles):
            self.weight_grad(self.t_up + t, x, self.both(at.pre + t * rows))

    def self_grads(self):
        at = self.at
        x = self.emb[...]
        for j in range(3):
            self.weight_grad(self.t_in + j, x, self.both(at.qkv + j * self.rows))
        self.weight_grad(self.t_out, self.both(at.att), self.both(at.gout))


    def store(self, slot, out, r, sem):
        return pltpu.make_async_copy(
            self.act.at[slot], out.at[pl.ds(r * TILE, TILE), :], self.local_sem.at[sem]
        )

    def spilled(self, r, back):
        a, b = self.probs.at[r], self.spill.at[r]
        return pltpu.make_async_copy(*((b, a) if back else (a, b)), self.local_sem.at[4 + r])

    def upstream(self, slot, r):
        return pltpu.make_async_copy(
            self.cot.at[pl.ds(r * TILE, TILE), :], self.act.at[slot], self.local_sem.at[6 + r]
        )

    def x_copy(self, slot, r, sem):
        ref = self.act.at[slot + r]
        return self.remote(ref, ref, self.x_send.at[sem + r], self.x_recv.at[sem + r], self.across)

    def length_copy(self):
        return self.remote(
            self.own_len, self.src_len, self.x_send.at[4], self.x_recv.at[4], self.across
        )

    def shard_copy(self):
        return self.remote(
            self.w_cross, self.x_shard, self.x_send.at[5], self.x_recv.at[5], self.across
        )


    def run(self):
        self.gacc[...] = jnp.zeros(self.gacc.shape, F32)
        self.own_len[...] = jnp.zeros(self.own_len.shape, jnp.int32)
        self.own_len[pl.ds(0, self.rows), pl.ds(0, self.lengths.shape[1])] = self.lengths[...]
        self.barrier()

        @pl.when(self.sec == 0)
        def first():
            self.encoding = True
            self.encoder()

        @pl.when(self.sec == 1)
        def second():
            self.encoding = False
            self.decoder()

    def encoder(self):
        at, rows = self.at, self.rows
        self.length_copy().start()
        for r in range(rows):
            self.upstream(at.cq + r, r).start()
        steps = iter(())
        if self.inner:
            self.shard_copy().start()
            up = [self.w_up_at + t for t in range(2 * self.ff_tiles)]
            steps = self.pipeline(
                [0, 1, 2, 3] + up, [self.gather1, self.gather2, self.gather3, self.gather4]
            )
            for step in range(7):
                next(steps)
        for r in range(rows):
            self.self_in(r)
            next(steps, None)
            self.self_attend(r, False)
            next(steps, None)
            next(steps, None)
            self.self_out(r)
            next(steps, None)
        for step in steps:
            pass
        for r in range(rows):
            self.feed(at.first + r, r)

            def block(b):
                second = self.norm(self.res[r, b] + self.tmp[b], 1, r, b)
                self.act[at.mem + r, b] = self.norm(second, 2, r, b).astype(BF16)

            self.blocks(block)
            self.x_copy(at.mem, r, 0).start()
            self.store(at.mem + r, self.result, r, r).start()
        steps = iter(())
        for r in range(rows):
            self.x_copy(at.gmem, r, 2).wait_recv()
            self.upstream(at.cq + r, r).wait()

            def block(b):
                up = self.act[at.cq + r, b]
                grad = up.astype(F32) + self.act[at.gmem + r, b].astype(F32)
                grad = self.norm_back(self.norm_back(grad, 2, r, b), 1, r, b)
                self.res[r, b] = grad
                self.act[at.gdown + r, b] = grad.astype(BF16)

            self.blocks(block)
            self.feed_back(r)

            def block(b):
                grad = self.norm_back(self.res[r, b] + self.tmp[b], 0, r, b)
                self.res[r, b] = grad
                self.act[at.gout + r, b] = grad.astype(BF16)

            self.blocks(block)
            if r == rows - 1:
                self.feed_grads(at.first)
                if self.inner:
                    self.small1()
                    feed = list(range(self.t_down, self.t_all)) + list(range(self.t_up, self.t_down))
                    steps = self.reduce_steps(feed + [4, 5, 3, 0, 1, 2])
            next(steps, None)
            self.self_back_out(r)
            for n in range(HEADS // 2):
                self.self_back_attend(r, n, n + 1)
                next(steps, None)
            self.self_back_in(r)
            next(steps, None)
            self.store(at.stage + r, self.grad_in, r, 2 + r).start()
        if self.inner:
            self.small2()
        self.self_grads()
        if self.inner:
            self.small3()
        for step in steps:
            pass
        if self.inner:
            self.small4()
        self.length_copy().wait_send()
        if self.inner:
            self.shard_copy().wait_send()
            self.drain()
        for r in range(rows):
            self.x_copy(at.mem, r, 0).wait_send()
            self.store(at.mem + r, self.result, r, r).wait()
            self.store(at.stage + r, self.grad_in, r, 2 + r).wait()
        if not self.inner:
            self.keep_grads()

    def reduce_steps(self, tiles):
        first = [self.reduce1, self.reduce2, self.reduce3, self.reduce4]
        yield from self.pipeline(tiles, first + [self.reduce5, self.reduce6, self.reduce7])

    def keep_grads(self):
        tiles = list(range(self.t_all))
        if self.encoding:
            tiles = [k for k in tiles if not self.from_partner(k)]
        else:
            tiles += [self.t_mem, self.t_mem + 1]
        copies = [
            pltpu.make_async_copy(
                self.act.at[self.tile_slot(k)], self.grads.at[k], self.grad_sem.at[k]
            )
            for k in tiles
        ]
        for copy in copies:
            copy.start()
        for copy in copies:
            copy.wait()
        for j in range(6):
            self.small[pl.ds(j, 1), :] = jnp.sum(self.gacc[j], axis=0, keepdims=True)
        self.small[pl.ds(6, 2), :] = jnp.zeros((2, TILE), F32)

    def decoder(self):
        at, rows = self.at, self.rows
        for r in range(rows):
            self.upstream(at.gcross + r, r).start()
        steps = iter(())
        if self.inner:
            up = [self.w_up_at + t for t in range(2 * self.ff_tiles)]
            steps = self.pipeline(
                [0, 1, 2, 3, 4, 5, 6, 7] + up,
                [self.gather1, self.gather2, self.gather3, self.gather4],
            )
            self.shard_copy().wait_recv()
            for step in range(7):
                next(steps)
        for r in range(rows):
            self.self_in(r)
            next(steps, None)
            self.self_attend(r, True)
            self.spilled(r, False).start()
            next(steps, None)
            next(steps, None)
            self.self_out(r)
            next(steps, None)
        for step in steps:
            pass
        for r in range(rows):
            queries = matmul_nn(self.act[at.first + r], self.weight(4)).astype(BF16)
            self.act[at.cq + r] = queries * jnp.asarray(0.125, BF16)
        self.length_copy().wait_recv()
        for r in range(rows):
            self.fill_mask(r, self.src_len, False)
            self.spilled(r, False).wait()
            self.x_copy(at.mem, r, 0).wait_recv()
            for j in range(2):
                self.act[at.kv + j * rows + r] = matmul_nn(
                    self.act[at.mem + r], self.weight(self.w_memory_at + j)
                ).astype(BF16)
            k, v = at.kv + r, at.kv + rows + r
            self.attend(at.cq + r, k, v, at.oc + r, r)
            self.tmp[...] = matmul_nn(self.act[at.oc + r], self.weight(5))

            def block(b):
                out = self.norm(self.res[r, b] + self.tmp[b], 1, r, b)
                self.res[r, b] = out
                self.act[at.second + r, b] = out.astype(BF16)

            self.blocks(block)
            self.feed(at.second + r, r)
            self.upstream(at.gcross + r, r).wait()

            def block(b):
                out = self.norm(self.res[r, b] + self.tmp[b], 2, r, b)
                self.act[at.stage + r, b] = out.astype(BF16)
                up = self.act[at.gcross + r, b]
                grad = self.norm_back(up.astype(F32), 2, r, b)
                self.res[r, b] = grad
                self.act[at.gdown + r, b] = grad.astype(BF16)

            self.blocks(block)
            self.store(at.stage + r, self.result, r, r).start()
            self.feed_back(r)

            def block(b):
                grad = self.norm_back(self.res[r, b] + self.tmp[b], 1, r, b)
                self.res[r, b] = grad
                self.act[at.gcross + r, b] = grad.astype(BF16)

            self.blocks(block)
            self.act[at.dout] = matmul_nt(self.act[at.gcross + r], self.weight(5)).astype(BF16)
            self.attend_back(at.cq + r, k, v, at.oc + r, at.dout, r, 0, HEADS // 2)
            self.spilled(r, True).start()
            total = matmul_nt(self.act[k], self.weight(self.w_memory_at))
            total = total + matmul_nt(self.act[v], self.weight(self.w_memory_at + 1))
            self.act[at.gmem + r] = total.astype(BF16)
            self.x_copy(at.gmem, r, 2).start()
            self.tmp[...] = matmul_nt(self.act[at.cq + r], self.weight(4))

            def block(b):
                grad = self.norm_back(self.res[r, b] + self.tmp[b], 0, r, b)
                self.res[r, b] = grad
                self.act[at.gout + r, b] = grad.astype(BF16)

            self.blocks(block)
        self.feed_grads(at.second)
        for j in range(2):
            self.weight_grad(self.t_mem + j, self.both(at.mem), self.both(at.kv + j * rows))
        self.weight_grad(self.t_cross, self.both(at.first), self.both(at.cq))
        self.weight_grad(self.t_cross + 1, self.both(at.oc), self.both(at.gcross))
        steps = iter(())
        if self.inner:
            feed = list(range(self.t_down, self.t_all)) + list(range(self.t_up, self.t_down))
            self.small1()
            steps = self.reduce_steps([self.t_mem, self.t_mem + 1] + feed + [4, 5, 3, 0, 1, 2])
        for r in range(rows):
            next(steps, None)
            self.self_back_out(r)
            self.spilled(r, True).wait()
            for n in range(HEADS // 2):
                self.self_back_attend(r, n, n + 1)
                if n % 2:
                    next(steps, None)
            self.store(at.stage + r, self.result, r, r).wait()
            self.self_back_in(r)
            next(steps, None)
            self.store(at.stage + r, self.grad_in, r, 2 + r).start()
        if self.inner:
            self.small2()
        self.self_grads()
        if self.inner:
            self.small3()
        for step in steps:
            pass
        if self.inner:
            self.small4()
        if self.inner:
            self.drain()
        for r in range(rows):
            self.x_copy(at.gmem, r, 2).wait_send()
            self.store(at.stage + r, self.grad_in, r, 2 + r).wait()
        if not self.inner:
            self.keep_grads()


def both_layers(inner, dp, call, emb, cot, lengths, gain, bias, weights):
    rows = lengths.shape[0]
    model = emb.shape[1]
    ff_tiles = weights[3].shape[1] // TILE
    tiles = 6 + 2 * ff_tiles
    sums = tiles + 2
    vmem = pl.BlockSpec(memory_space=pltpu.VMEM)
    anywhere = pl.BlockSpec(memory_space=pl.ANY)
    dma = pltpu.SemaphoreType.DMA
    square = (TILE, TILE)
    scratch = [
        pltpu.VMEM((Slots(rows, ff_tiles).count,) + square, BF16),
        pltpu.VMEM((rows, HEADS) + square, BF16),
        pltpu.VMEM((rows,) + square, F32),
        pltpu.VMEM(square, F32),
        pltpu.VMEM(square, F32),
        pltpu.VMEM((rows, TILE, 128), F32),
        pltpu.VMEM((6, 8, model), F32),
        pltpu.VMEM((8, 128), jnp.int32),
        pltpu.VMEM((8, 128), jnp.int32),
        dma((8,)),
        dma((8,)),
        dma((8,)),
    ]
    if inner:
        part = TILE // 16
        chunks = 8 + 2 * ff_tiles
        scratch += [
            pltpu.VMEM((8 + ff_tiles, LINE, 2, 2, part, TILE), BF16),
            pltpu.VMEM((LINE, 2, 2, weights[4].shape[0], TILE), BF16),
            pltpu.VMEM((part, 2 * TILE), BF16),
            pltpu.VMEM((2, part, TILE), BF16),
            pltpu.VMEM((sums, TILE // 2, TILE), BF16),
            pltpu.VMEM((sums, TILE // 4, TILE), BF16),
            pltpu.VMEM((sums, LINE - 1, part, TILE), BF16),
            pltpu.VMEM((3, 8, model), F32),
            pltpu.VMEM((2 + LINE, 8, model), F32),
        ]
        line = (LINE - 1,)
        scratch += [dma((chunks,) + line)] * 2 + [dma((chunks,))] * 4
        scratch += [dma((sums,))] * 4 + [dma((sums,) + line)] * 4
        scratch += [dma((sums,))] * 4 + [dma((sums,)), dma((2 + LINE,)), dma((2 + LINE,))]
    else:
        scratch += [dma((sums,))]

    def kernel(*refs):
        Body(inner, rows, dp, ff_tiles, refs).run()

    return pl.pallas_call(
        kernel,
        out_shape=(
            jax.ShapeDtypeStruct(emb.shape, BF16),
            jax.ShapeDtypeStruct(emb.shape, BF16),
            jax.ShapeDtypeStruct((tiles if inner else sums,) + square, BF16),
            jax.ShapeDtypeStruct((8, model), F32),
            jax.ShapeDtypeStruct((rows, HEADS) + square, BF16),
        ),
        in_specs=[vmem, anywhere] + [vmem] * (3 + len(weights)),
        out_specs=(anywhere, anywhere, anywhere, vmem, anywhere),
        scratch_shapes=scratch,
        compiler_params=pltpu.CompilerParams(
            collective_id=call, has_side_effects=True, vmem_limit_bytes=62 * 2**20
        ),
        name="layers",
    )(emb, cot, lengths, gain, bias, *weights)


def passed_along(shard, axis, by):
    count = lax.axis_size(axis)
    pairs = [(i, i + by) for i in range(count) if 0 <= i + by < count]
    return lax.ppermute(shard, axis, pairs)


def local(
    embedded,
    lengths,
    cotangent,
    attn_in,
    attn_out,
    cross_weight,
    up_weight,
    down_weight,
    norm_gain,
    norm_bias,
):
    dp = lax.axis_size("dp")
    rows = lengths.shape[1]
    model = embedded.shape[2]
    ff_tiles = up_weight.shape[2] // TILE
    shards = tuple(w[0] for w in (attn_in, attn_out, cross_weight, up_weight, down_weight))
    inner = dp == 4 * LINE and rows <= CALL_ROWS
    args = (embedded[0], cotangent[0], lengths[0], norm_gain[0], norm_bias[0])
    if inner:
        result, grad_in, grads, small, spill = both_layers(inner, dp, 0, *args, shards)
        cross = jnp.concatenate([grads[4], grads[5]], axis=1).astype(F32)
    else:
        weights = tuple(lax.all_gather(w, "dp", axis=0, tiled=True) for w in shards)
        weights += (passed_along(weights[2], "section", 1),)
        parts = []
        for call in range(0, rows, CALL_ROWS):
            span = slice(call * TILE, min(rows, call + CALL_ROWS) * TILE)
            lens = args[2][call : call + CALL_ROWS]
            parts.append(
                both_layers(
                    inner, dp, call // CALL_ROWS, args[0][span], args[1][span], lens, *args[3:], weights
                )
            )
        result = jnp.concatenate([part[0] for part in parts], axis=0)
        grad_in = jnp.concatenate([part[1] for part in parts], axis=0)
        grads = sum(part[2].astype(F32) for part in parts)
        grads, small = lax.psum((grads, sum(part[3] for part in parts)), "dp")
        cross = jnp.concatenate([grads[4], grads[5]], axis=1)
        memory = jnp.concatenate([grads[-2], grads[-1]], axis=1)
        is_first = lax.axis_index("section") == 0
        cross = jnp.where(is_first, passed_along(memory, "section", -1), cross)
    up_at, down_at = 6, 6 + ff_tiles
    in_grad = jnp.concatenate([grads[j] for j in range(3)], axis=1).astype(F32)
    up_grad = jnp.concatenate([grads[up_at + t] for t in range(ff_tiles)], axis=1).astype(F32)
    down_grad = grads[down_at : down_at + ff_tiles].reshape(ff_tiles * TILE, model).astype(F32)
    return (
        result[None],
        grad_in[None],
        in_grad[None],
        grads[3].astype(F32)[None],
        cross[None],
        up_grad[None],
        down_grad[None],
        small[None, 0:3],
        small[None, 3:6],
    )


def solution(mesh):
    rows = P("section", "dp", None)
    whole = P("section", None, None)
    in_specs = (rows,) * 8 + (whole,) * 2
    out_specs = (rows,) * 2 + (whole,) * 7
    return jax.shard_map(local, mesh=mesh, in_specs=in_specs, out_specs=out_specs, check_vma=False)
```

```python
import functools

import jax
import jax.numpy as jnp
from jax import lax
from jax.experimental import pallas as pl
from jax.experimental.pallas import tpu as pltpu
from jax.sharding import PartitionSpec as P

HEADS = 8

norm_eps = 1e-06
masked_score = -1e30
F32 = jnp.float32
BF16 = jnp.bfloat16
MESH = pl.DeviceIdType.MESH
down_columns = 256
query_scale = 0.125
LINE = 4
CALL_ROWS = 2
TILE = 512


def matmul_nn(left, right):
    return jnp.dot(left, right, preferred_element_type=F32)


def matmul_tn(left, right):
    return lax.dot_general(left, right, (((0,), (0,)), ((), ())), preferred_element_type=F32)


def matmul_nt(left, right):
    return lax.dot_general(left, right, (((1,), (1,)), ((), ())), preferred_element_type=F32)


class Steps:
    def __init__(self, body=None, items=(), stages=()):
        self.body = body
        self.items = items
        self.stages = stages
        self.count = len(items) + stages[-1][0] if items else 0
        self.next = 0

    def run(self, n):
        if n >= self.count:
            return
        for offset, act in reversed(self.stages):
            if 0 <= n - offset < len(self.items):
                item = self.items[n - offset]
                act(item)
                self.body.done.append((act, item))

    def until(self, n):
        while self.next < n:
            self.run(self.next)
            self.next += 1

    def more(self, n):
        self.until(self.next + n)

    def finish(self):
        self.until(self.count)


class Slots:
    def __init__(self, rows, ff_tiles):
        self.rows = rows
        self.count = 0
        self.qkv = self.take(3 * rows)
        self.cq = self.take(rows)
        self.kv = self.take(2 * rows)
        self.pre = self.take(ff_tiles * rows)
        self.hid = self.take(ff_tiles * rows)
        self.att = self.take(rows)
        self.oc = self.take(rows)
        self.first = self.take(rows)
        self.second = self.take(rows)
        self.mem = self.take(rows)
        self.gmem = self.take(rows)
        self.gdown = self.take(rows)
        self.gout = self.take(rows)
        self.gcross = self.take(rows)
        self.stage = self.take(rows)
        self.dout = self.take(1)
        self.xhat = self.take(3 * rows)

    def take(self, n):
        at = self.count
        self.count += n
        return at


class Body:
    def __init__(self, inner, rows, dp, ff_tiles, refs):
        self.inner = inner
        self.rows = rows
        self.ff_tiles = ff_tiles
        self.at = Slots(rows, ff_tiles)
        names = ["emb", "cot", "lengths", "gain", "bias"]
        names += ["w_in", "w_out", "w_cross", "w_up", "w_down"]
        if not inner:
            names += ["w_memory"]
        names += ["result", "grad_in", "g_in", "g_out", "g_cross", "g_up", "g_down"]
        if not inner:
            names += ["g_memory"]
        names += ["g_gain", "g_bias", "spill"]
        names += ["act", "probs", "res", "mask", "rstd", "gacc", "own_len", "src_len"]
        names += ["local_sem", "x_send", "x_recv"]
        if not inner:
            names += ["grad_sem"]
        if inner:
            names += ["wt", "wd", "x_shard", "x_grad", "r1", "r2", "r3", "gbuf", "grcv"]
            names += ["gz_s", "gz_r", "gy_s", "gy_r", "gc_s", "gc_r"]
            names += ["a1_s", "a1_r", "a2_s", "a2_r", "a3_s", "a3_r"]
            names += ["a4_s", "a4_r", "a5_s", "a5_r", "a6_s", "a6_r", "own_sem", "gs_s", "gs_r"]
        assert len(names) == len(refs), (len(names), len(refs))
        for name, ref in zip(names, refs):
            setattr(self, name, ref)
        self.sec = lax.axis_index("section")
        self.i = lax.axis_index("dp")
        self.across = (1 - self.sec, self.i)
        if inner:
            self.c = lax.rem(self.i, 2)
            self.y = lax.rem(self.i // 2, 2)
            self.z = self.i // 4
            self.core_dev = (self.sec, self.z * 4 + self.y * 2 + (1 - self.c))
            self.y_dev = (self.sec, self.z * 4 + (1 - self.y) * 2 + self.c)
            self.z_other = [lax.rem(self.z + d, LINE) for d in range(1, LINE)]
            self.z_dev = [(self.sec, zz * 4 + self.y * 2 + self.c) for zz in self.z_other]
        self.done = []
        self.draining = False
        self.encoding = True
        self.t_in = 0
        self.t_out = 3
        self.t_cross = 4
        self.t_up = 6
        self.t_down = 6 + ff_tiles
        self.t_all = 6 + 2 * ff_tiles
        self.t_mem = self.t_all
        self.w_memory_at = 6
        self.w_up_at = 8
        self.down_bands = TILE // down_columns
        self.feed_chunks = [self.w_up_at + n for n in range(ff_tiles + self.down_bands)]


    def remote(self, src, dst, send, recv, dev):
        return pltpu.make_async_remote_copy(
            src_ref=src, dst_ref=dst, send_sem=send, recv_sem=recv, device_id=dev, device_id_type=MESH
        )

    def send(self, src, dst, send, recv, dev):
        copy = self.remote(src, dst, send, recv, dev)
        if self.draining:
            copy.wait_send()
        else:
            copy.start()

    def drain(self):
        self.draining = True
        for act, item in self.done:
            act(item)
        self.draining = False
        self.done = []

    def barrier(self):
        sem = pltpu.get_barrier_semaphore()
        devs = [self.across]
        if self.inner:
            devs += [self.core_dev, self.y_dev] + self.z_dev
        for dev in devs:
            pl.semaphore_signal(sem, inc=1, device_id=dev, device_id_type=MESH)
        pl.semaphore_wait(sem, len(devs))


    def weight(self, k):
        if self.inner:
            return self.wt[k].reshape(TILE, TILE)
        if k < 3:
            return self.w_in[:, k * TILE : (k + 1) * TILE]
        if k == 3:
            return self.w_out[...]
        if k < 6:
            return self.w_cross[:, (k - 4) * TILE : (k - 3) * TILE]
        if k < 8:
            return self.w_memory[:, (k - 6) * TILE : (k - 5) * TILE]
        return self.w_up[:, (k - 8) * TILE : (k - 7) * TILE]

    def weight_up(self, t):
        if self.inner:
            return self.wt[self.w_up_at + t].reshape(TILE, TILE)
        start = t * TILE
        return self.w_up[:, pl.ds(start if isinstance(start, int) else pl.multiple_of(start, TILE), TILE)]

    def weight_down(self, t, cols=slice(None)):
        if self.inner:
            tile = self.wd[t, :, :, :, cols]
            return tile.reshape(TILE, tile.shape[-1])
        return self.w_down[t * TILE : (t + 1) * TILE, cols]

    def chunk_source(self, k):
        z, y, c = self.z, self.y, self.c
        down_at = self.w_up_at + self.ff_tiles
        if k < 3:
            src = self.w_in.at[:, pl.ds(k * TILE, TILE)]
        elif k == 3:
            src = self.w_out.at[...]
        elif k < 6:
            src = self.w_cross.at[:, pl.ds((k - 4) * TILE, TILE)]
        elif k < 8:
            src = self.x_shard.at[:, pl.ds((k - 6) * TILE, TILE)]
        elif k < down_at:
            src = self.w_up.at[:, pl.ds((k - 8) * TILE, TILE)]
        else:
            cols = pl.ds((k - down_at) * down_columns, down_columns)
            src = self.w_down.at[:, cols]
        if k < down_at:
            whole = self.wt.at[k]
            own = whole.at[z, y, c]
            line = whole.at[:, y, c]
            plane = whole.at[:, :, c]
        else:
            own = self.wd.at[z, y, c, :, cols]
            line = self.wd.at[:, y, c, :, cols]
            plane = self.wd.at[:, :, c, :, cols]
        return src, own, line, plane

    def gather1(self, k):
        src, own, line, plane = self.chunk_source(k)
        if not self.draining:
            own[...] = src[...]
        for d in range(LINE - 1):
            self.send(src, own, self.gz_s.at[k, d], self.gz_r.at[k, d], self.z_dev[d])

    def gather2(self, k):
        src, own, line, plane = self.chunk_source(k)
        for d in range(0 if self.draining else LINE - 1):
            self.remote(src, own, self.gz_s.at[k, d], self.gz_r.at[k, d], self.z_dev[d]).wait_recv()
        self.send(line, line, self.gy_s.at[k], self.gy_r.at[k], self.y_dev)

    def gather3(self, k):
        src, own, line, plane = self.chunk_source(k)
        if not self.draining:
            self.remote(line, line, self.gy_s.at[k], self.gy_r.at[k], self.y_dev).wait_recv()
        self.send(plane, plane, self.gc_s.at[k], self.gc_r.at[k], self.core_dev)

    def gather4(self, k):
        src, own, line, plane = self.chunk_source(k)
        if not self.draining:
            self.remote(plane, plane, self.gc_s.at[k], self.gc_r.at[k], self.core_dev).wait_recv()

    def gather_steps(self, chunks):
        stages = [(0, self.gather1), (2, self.gather2), (4, self.gather3), (5, self.gather4)]
        return Steps(self, chunks, stages)


    def tile_slot(self, k):
        at, rows = self.at, self.rows
        if k < 3:
            return at.qkv + k * rows
        if k == 3:
            return at.gout
        if k == 4:
            return at.cq
        if k == 5:
            return at.gcross
        if k < self.t_down:
            return at.pre + (k - self.t_up) * rows
        if k < self.t_all:
            return at.hid + (k - self.t_down) * rows
        return at.kv + (k - self.t_mem) * rows

    def whole_grad(self, k, start=0, size=TILE):
        rows = pl.ds(start, size)

        def columns(ref, n):
            return ref.at[rows, pl.ds(n * TILE, TILE)]

        if k < 3:
            return columns(self.g_in, k)
        if k == 3:
            return columns(self.g_out, 0)
        if k < 6:
            return columns(self.g_cross, k - self.t_cross)
        if k < self.t_down:
            return columns(self.g_up, k - self.t_up)
        if k < self.t_all:
            return self.g_down.at[pl.ds((k - self.t_down) * TILE + start, size), :]
        return columns(self.g_memory, k - self.t_mem)

    def from_partner(self, k):
        return self.encoding and k in (self.t_cross, self.t_cross + 1)

    def block_at(self, c, y=0, z=0):
        return c * (TILE // 2) + y * (TILE // 4) + z * (TILE // 16)

    def reduce1(self, k):
        if self.from_partner(k):
            return
        slot = self.tile_slot(k)
        half = TILE // 2
        src = self.act.at[slot, pl.ds(self.block_at(1 - self.c), half)]
        self.send(src, self.r1.at[k], self.a1_s.at[k], self.a1_r.at[k], self.core_dev)

    def reduce2(self, k):
        if self.from_partner(k):
            return
        slot = self.tile_slot(k)
        half, quarter = TILE // 2, TILE // 4
        own = pl.ds(pl.multiple_of(self.block_at(self.c), half), half)
        src = self.act.at[slot, own]
        if not self.draining:
            self.remote(
                src, self.r1.at[k], self.a1_s.at[k], self.a1_r.at[k], self.core_dev
            ).wait_recv()
            total = self.act[slot, own].astype(F32) + self.r1[k].astype(F32)
            self.act[slot, own] = total.astype(BF16)
        src = self.act.at[slot, pl.ds(self.block_at(self.c, 1 - self.y), quarter)]
        self.send(src, self.r2.at[k], self.a2_s.at[k], self.a2_r.at[k], self.y_dev)

    def reduce3(self, k):
        if self.from_partner(k):
            return
        slot = self.tile_slot(k)
        quarter, part = TILE // 4, TILE // 16
        own = pl.ds(pl.multiple_of(self.block_at(self.c, self.y), quarter), quarter)
        src = self.act.at[slot, own]
        if not self.draining:
            self.remote(
                src, self.r2.at[k], self.a2_s.at[k], self.a2_r.at[k], self.y_dev
            ).wait_recv()
            total = self.act[slot, own].astype(F32) + self.r2[k].astype(F32)
            self.act[slot, own] = total.astype(BF16)
        for d in range(LINE - 1):
            src = self.act.at[slot, pl.ds(self.block_at(self.c, self.y, self.z_other[d]), part)]
            self.send(src, self.r3.at[k, d], self.a3_s.at[k, d], self.a3_r.at[k, d], self.z_dev[d])

    def reduce4(self, k):
        if self.from_partner(k):
            return self.reduce4_memory(k)
        slot = self.tile_slot(k)
        part = TILE // 16
        own = pl.ds(pl.multiple_of(self.block_at(self.c, self.y, self.z), part), part)
        src = self.act.at[slot, own]
        if not self.draining:
            total = self.act[slot, own].astype(F32)
            for d in range(LINE - 1):
                self.remote(
                    src, self.r3.at[k, d], self.a3_s.at[k, d], self.a3_r.at[k, d], self.z_dev[d]
                ).wait_recv()
                total = total + self.r3[k, d].astype(F32)
            self.act[slot, own] = total.astype(BF16)
        if k < self.t_all:
            self.spread(k, src)
        else:
            j = k - self.t_mem
            dst = self.x_grad.at[j]
            self.send(src, dst, self.x_send.at[6 + j], self.x_recv.at[6 + j], self.across)

    def spread(self, k, src):
        part = TILE // 16
        dst = self.whole_grad(k, self.block_at(self.c, self.y, self.z), part)
        if not self.draining:
            pltpu.make_async_copy(src, dst, self.own_sem.at[k]).start()
        for d in range(LINE - 1):
            self.send(src, dst, self.a4_s.at[k, d], self.a4_r.at[k, d], self.z_dev[d])

    def reduce4_memory(self, k):
        j = k - self.t_cross
        src = self.x_grad.at[j]
        if not self.draining:
            self.remote(
                src, src, self.x_send.at[6 + j], self.x_recv.at[6 + j], self.across
            ).wait_recv()
        self.spread(k, src)

    def reduce5(self, k):
        if k >= self.t_all:
            return
        quarter, part = TILE // 4, TILE // 16
        own = self.whole_grad(k, self.block_at(self.c, self.y, self.z), part)
        if not self.draining:
            pltpu.make_async_copy(own, own, self.own_sem.at[k]).wait()
        for d in range(0 if self.draining else LINE - 1):
            self.remote(
                own, own, self.a4_s.at[k, d], self.a4_r.at[k, d], self.z_dev[d]
            ).wait_recv()
        line = self.whole_grad(k, self.block_at(self.c, self.y), quarter)
        self.send(line, line, self.a5_s.at[k], self.a5_r.at[k], self.y_dev)

    def reduce6(self, k):
        if k >= self.t_all:
            return
        half, quarter = TILE // 2, TILE // 4
        line = self.whole_grad(k, self.block_at(self.c, self.y), quarter)
        if not self.draining:
            self.remote(line, line, self.a5_s.at[k], self.a5_r.at[k], self.y_dev).wait_recv()
        plane = self.whole_grad(k, self.block_at(self.c), half)
        self.send(plane, plane, self.a6_s.at[k], self.a6_r.at[k], self.core_dev)

    def reduce7(self, k):
        if k >= self.t_all:
            return
        plane = self.whole_grad(k, self.block_at(self.c), TILE // 2)
        if not self.draining:
            self.remote(plane, plane, self.a6_s.at[k], self.a6_r.at[k], self.core_dev).wait_recv()

    def small_steps(self):
        stages = [(0, self.small1), (1, self.small2), (2, self.small3), (3, self.small4)]
        return Steps(self, [0], stages)

    def small1(self, item):
        if not self.draining:
            for j in range(6):
                self.gbuf[0, pl.ds(j, 1), :] = jnp.sum(self.gacc[j], axis=0, keepdims=True)
            self.gbuf[0, pl.ds(6, 2), :] = jnp.zeros((2, TILE), F32)
        self.send(self.gbuf.at[0], self.grcv.at[0], self.gs_s.at[0], self.gs_r.at[0], self.core_dev)

    def small2(self, item):
        if not self.draining:
            self.remote(
                self.gbuf.at[0], self.grcv.at[0], self.gs_s.at[0], self.gs_r.at[0], self.core_dev
            ).wait_recv()
            self.gbuf[1] = self.gbuf[0] + self.grcv[0]
        self.send(self.gbuf.at[1], self.grcv.at[1], self.gs_s.at[1], self.gs_r.at[1], self.y_dev)

    def small3(self, item):
        if not self.draining:
            self.remote(
                self.gbuf.at[1], self.grcv.at[1], self.gs_s.at[1], self.gs_r.at[1], self.y_dev
            ).wait_recv()
            self.gbuf[2] = self.gbuf[1] + self.grcv[1]
        for d in range(LINE - 1):
            self.send(
                self.gbuf.at[2],
                self.grcv.at[2 + self.z],
                self.gs_s.at[2 + d],
                self.gs_r.at[2 + d],
                self.z_dev[d],
            )
        if not self.draining:
            self.grcv[2 + self.z] = self.gbuf[2]

    def small4(self, item):
        if self.draining:
            return
        for d in range(LINE - 1):
            self.remote(
                self.gbuf.at[2],
                self.grcv.at[2 + self.z],
                self.gs_s.at[2 + d],
                self.gs_r.at[2 + d],
                self.z_dev[d],
            ).wait_recv()
        total = self.grcv[2]
        for n in range(1, LINE):
            total = total + self.grcv[2 + n]
        self.g_gain[...] = total[0:3]
        self.g_bias[...] = total[3:6]


    def fill_mask(self, r, key_len, causal):
        lane = lax.broadcasted_iota(jnp.int32, (8, 128), 1)
        sub = lax.broadcasted_iota(jnp.int32, (8, 128), 0)

        def ends_of(ref):
            spans = jnp.broadcast_to(ref[pl.ds(r, 1), :], (8, 128))
            return jnp.sum(jnp.where(lane <= sub, spans, 0).astype(F32), axis=1, keepdims=True)

        ends = ends_of(key_len)
        flat = jnp.sum(jnp.where(lane == sub, ends, 0.0), axis=0, keepdims=True)
        flat = jnp.where(lane[:1] < 8, flat, 1e9)
        pos = lax.broadcasted_iota(jnp.int32, (TILE, 128), 0).astype(F32)
        key_ids = jnp.sum(jnp.where(pos >= flat, 1.0, 0.0), axis=1, keepdims=True)
        query_ends = ends_of(self.own_len)
        pos = lax.broadcasted_iota(jnp.int32, (8, TILE), 1).astype(F32)
        query_ids = jnp.sum(jnp.where(pos >= query_ends, 1.0, 0.0), axis=0, keepdims=True)
        step = 128
        for b in range(TILE // step):
            allowed = key_ids[b * step : (b + 1) * step] == query_ids
            if causal:
                k_pos = lax.broadcasted_iota(jnp.int32, (step, TILE), 0) + b * step
                q_pos = lax.broadcasted_iota(jnp.int32, (step, TILE), 1)
                allowed = allowed & (k_pos <= q_pos)
            self.mask[b * step : (b + 1) * step, :] = jnp.where(allowed, 0.0, masked_score)


    def attend(self, q, k, v, out, r, first=0, count=HEADS // 2):
        act = self.act
        low = lax.broadcasted_iota(jnp.int32, (1, 128), 1) < 64

        def pair(n, carry):
            hp = first + n
            cols = pl.ds(pl.multiple_of(hp * 128, 128), 128)
            qs, ks, vs = act[q, :, cols], act[k, :, cols], act[v, :, cols]
            scores = []
            for j in range(2):
                qm = jnp.where(low if j == 0 else ~low, qs, jnp.zeros_like(qs))
                s = matmul_nt(ks, qm) + self.mask[...]
                scores.append((s, jnp.max(s, axis=0, keepdims=True)))
            weights = []
            for j, (s, top) in enumerate(scores):
                raised = jnp.exp(s - top)
                raised = raised * (1.0 / jnp.sum(raised, axis=0, keepdims=True))
                weights.append(raised.astype(BF16))
                self.probs[r, hp * 2 + j] = weights[j]
            for j, probs in enumerate(weights):
                o = matmul_tn(vs, probs)[64 * j : 64 * j + 64]
                rows = pl.ds(pl.multiple_of(hp * 128 + 64 * j, 64), 64)
                act[out, rows, :] = o.astype(BF16)
            return carry

        lax.fori_loop(0, count, pair, 0)

    def attend_back(self, q, k, v, out, dout, r, first=0, count=HEADS // 2):
        act = self.act
        low = lax.broadcasted_iota(jnp.int32, (1, 128), 1) < 64

        def pair(n, carry):
            hp = first + n
            cols = pl.ds(pl.multiple_of(hp * 128, 128), 128)
            qs, ks, vs = act[q, :, cols], act[k, :, cols], act[v, :, cols]
            grads = []
            for j in range(2):
                rows = pl.ds(pl.multiple_of(hp * 128 + 64 * j, 64), 64)
                do = act[dout, rows, :]
                prod = do.astype(F32) * act[out, rows, :].astype(F32)
                delta = jnp.sum(prod, axis=0, keepdims=True)
                none = jnp.zeros_like(do)
                do = jnp.concatenate([do, none] if j == 0 else [none, do], axis=0)
                grads.append((do, delta, matmul_nn(vs, do)))
            scores = []
            for j, (do, delta, dp) in enumerate(grads):
                probs = self.probs[r, hp * 2 + j]
                scores.append((probs, (probs.astype(F32) * (dp - delta)).astype(BF16)))
            dq, dk, dv = [], None, None
            for j, (probs, ds) in enumerate(scores):
                qm = jnp.where(low if j == 0 else ~low, qs, jnp.zeros_like(qs))
                a, b = matmul_nt(probs, grads[j][0]), matmul_nn(ds, qm)
                dv, dk = (a, b) if j == 0 else (dv + a, dk + b)
                dq.append(matmul_tn(ks, ds)[64 * j : 64 * j + 64])
            dq = (jnp.concatenate(dq, axis=0) * 0.125).astype(BF16)
            act[q, :, cols] = dq.T
            act[k, :, cols] = dk.astype(BF16)
            act[v, :, cols] = dv.astype(BF16)
            return carry

        lax.fori_loop(0, count, pair, 0)


    def blocks(self, body):
        step = 128

        def one(b, carry):
            body(pl.ds(pl.multiple_of(b * step, step), step))
            return carry

        lax.fori_loop(0, TILE // step, one, 0, unroll=True)

    def norm(self, values, n, r, rows):
        center = jnp.mean(values, axis=-1, keepdims=True)
        shifted = values - center
        scale = lax.rsqrt(jnp.mean(shifted * shifted, axis=-1, keepdims=True) + norm_eps)
        hat = shifted * scale
        self.act[self.at.xhat + n * self.rows + r, rows] = hat.astype(BF16)
        self.rstd[r, rows, pl.ds(n, 1)] = scale
        return hat * self.gain[pl.ds(n, 1), :] + self.bias[pl.ds(n, 1), :]

    def norm_back(self, grad, n, r, rows):
        hat = self.act[self.at.xhat + n * self.rows + r, rows].astype(F32)
        scale = self.rstd[r, rows, pl.ds(n, 1)]
        count = grad.shape[0] // 8
        self.gacc[n] += jnp.sum((grad * hat).reshape(count, 8, TILE), axis=0)
        self.gacc[3 + n] += jnp.sum(grad.reshape(count, 8, TILE), axis=0)
        up = grad * self.gain[pl.ds(n, 1), :]
        first = jnp.mean(up, axis=-1, keepdims=True)
        second = jnp.mean(up * hat, axis=-1, keepdims=True)
        return (up - first - hat * second) * scale


    def row(self, r):
        start = r * TILE
        return pl.ds(start if isinstance(start, int) else pl.multiple_of(start, TILE), TILE)

    def loop(self, count, body):
        def one(n, carry):
            body(n)
            return carry

        lax.fori_loop(0, count, one, 0)

    def self_in(self, r):
        x = self.emb[self.row(r), :]
        for j in range(3):
            rows = matmul_nn(x, self.weight(j))
            if j == 0:
                rows = rows * query_scale
            self.act[self.at.qkv + j * self.rows + r] = rows.astype(BF16)

    def self_forward(self, causal, steps):
        at, rows = self.at, self.rows
        base = steps.next
        steps.next += 3 * rows

        def one(r):
            self.self_in(r)
            for n in range(rows):
                pl.when(r == n)(functools.partial(steps.run, base + 3 * n))
            self.fill_mask(r, self.own_len, causal)
            q, k, v = (at.qkv + j * rows + r for j in range(3))

            def half(h):
                self.attend(q, k, v, at.att + r, r, 2 * h, 2)
                for n in range(rows):
                    for m in range(2):
                        pl.when((r == n) & (h == m))(
                            functools.partial(steps.run, base + 3 * n + 1 + m)
                        )

            self.loop(HEADS // 4, half)
            if not self.encoding:
                self.spilled(r, False).start()
            self.self_out(r)

        self.loop(rows, one)

    def self_out(self, r):
        at = self.at
        x = self.emb[self.row(r), :].astype(F32)
        self.res[r] = x + matmul_tn(self.act[at.att + r], self.weight(3))

        def block(rows):
            out = self.norm(self.res[r, rows], 0, r, rows)
            self.res[r, rows] = out
            self.act[at.first + r, rows] = out.astype(BF16)

        self.blocks(block)

    def feed_up(self, x_slot, r, t):
        at = self.at
        pre = matmul_nn(self.act[x_slot], self.weight_up(t))
        hid = (pre / (1.0 + jnp.exp(-pre))).astype(BF16)
        self.act[at.pre + t * self.rows + r] = pre.astype(BF16)
        self.act[at.hid + t * self.rows + r] = hid

    def feed_down(self, r, j):
        cols = slice(j * down_columns, (j + 1) * down_columns)
        total = self.res[r, :, cols]
        for t in range(self.ff_tiles):
            hid = self.act[self.at.hid + t * self.rows + r]
            total = total + matmul_nn(hid, self.weight_down(t, cols))
        self.res[r, :, cols] = total

    def feed_back(self, r):
        at = self.at
        grad = self.act[at.gdown + r]
        total = None
        for t in range(self.ff_tiles):
            dh = matmul_nt(grad, self.weight_down(t))
            pre = self.act[at.pre + t * self.rows + r].astype(F32)
            s = 1.0 / (1.0 + jnp.exp(-pre))
            dp = (dh * (s * (1.0 + pre * (1.0 - s)))).astype(BF16)
            self.act[at.pre + t * self.rows + r] = dp
            part = matmul_nt(dp, self.weight_up(t))
            total = part if total is None else total + part
        self.res[r] += total

    def self_back(self, r, step):
        at = self.at
        self.act[at.dout] = matmul_nt(self.weight(3), self.act[at.gout + r]).astype(BF16)
        step(0)
        q, k, v = (at.qkv + j * self.rows + r for j in range(3))

        def half(h):
            self.attend_back(q, k, v, at.att + r, at.dout, r, 2 * h, 2)
            for m in range(2):
                pl.when(h == m)(functools.partial(step, 1 + m))

        self.loop(HEADS // 4, half)
        total = self.res[r]
        for j in range(3):
            total = total + matmul_nt(self.act[at.qkv + j * self.rows + r], self.weight(j))
        self.act[at.stage + r] = total.astype(BF16)
        step(3)
        self.store(at.stage + r, self.grad_in, r, 2 + r).start()

    def both(self, slot):
        return self.act[pl.ds(slot, self.rows)].reshape(self.rows * TILE, TILE)

    def weight_grad(self, slot, left, right):
        self.act[slot] = matmul_tn(left, right).astype(BF16)

    def out_grad(self, k, left, right):
        total = matmul_nn(self.act[left], self.act[right])
        for r in range(1, self.rows):
            total = total + matmul_nn(self.act[left + r], self.act[right + r])
        self.act[self.tile_slot(k)] = total.astype(BF16)

    def down_grads(self):
        at, rows = self.at, self.rows
        grad = self.both(at.gdown)

        def part(t):
            slot = at.hid + t * rows
            self.weight_grad(slot, self.both(slot), grad)

        self.loop(self.ff_tiles, part)

    def up_grads(self, x_slot):
        at, rows = self.at, self.rows
        x = self.both(x_slot)

        def part(t):
            slot = at.pre + t * rows
            self.weight_grad(slot, x, self.both(slot))

        self.loop(self.ff_tiles, part)

    def self_grads(self):
        at = self.at
        x = self.emb[...]

        def part(j):
            slot = at.qkv + j * self.rows
            self.weight_grad(slot, x, self.both(slot))

        self.loop(3, part)
        self.out_grad(self.t_out, at.att, at.gout)


    def store(self, slot, out, r, sem):
        return pltpu.make_async_copy(
            self.act.at[slot], out.at[self.row(r), :], self.local_sem.at[sem]
        )

    def spilled(self, r, back):
        a, b = self.probs.at[r], self.spill.at[r]
        return pltpu.make_async_copy(*((b, a) if back else (a, b)), self.local_sem.at[4 + r])

    def upstream(self, slot, r):
        return pltpu.make_async_copy(
            self.cot.at[self.row(r), :], self.act.at[slot], self.local_sem.at[6 + r]
        )

    def x_copy(self, slot, r, sem):
        ref = self.act.at[slot + r]
        return self.remote(ref, ref, self.x_send.at[sem + r], self.x_recv.at[sem + r], self.across)

    def length_copy(self):
        return self.remote(
            self.own_len, self.src_len, self.x_send.at[4], self.x_recv.at[4], self.across
        )

    def shard_copy(self):
        return self.remote(
            self.w_cross, self.x_shard, self.x_send.at[5], self.x_recv.at[5], self.across
        )


    def run(self):
        self.gacc[...] = jnp.zeros(self.gacc.shape, F32)
        self.own_len[...] = jnp.zeros(self.own_len.shape, jnp.int32)
        self.own_len[pl.ds(0, self.rows), pl.ds(0, self.lengths.shape[1])] = self.lengths[...]
        self.barrier()

        @pl.when(self.sec == 0)
        def first():
            self.encoding = True
            self.encoder()

        @pl.when(self.sec == 1)
        def second():
            self.encoding = False
            self.decoder()

    def encoder(self):
        at, rows = self.at, self.rows
        self.length_copy().start()
        for r in range(rows):
            self.upstream(at.cq + r, r).start()
        steps = Steps()
        if self.inner:
            self.shard_copy().start()
            steps = self.gather_steps([0, 1, 2, 3] + self.feed_chunks)
            steps.until(9)
        self.self_forward(False, steps)
        base = max(steps.next, 10)
        steps.until(base)

        def up(t):
            for n in range(1, self.ff_tiles):
                if base <= 9 + n:
                    pl.when(t == n)(functools.partial(steps.run, 9 + n))
            for r in range(rows):
                self.feed_up(at.first + r, r, t)

        steps.next = max(base, 9 + self.ff_tiles)
        self.loop(self.ff_tiles, up)
        last = self.down_bands - 1
        for j in range(last):
            steps.until(10 + self.ff_tiles + j)
            self.loop(rows, functools.partial(self.feed_down, j=j))
        steps.finish()

        def send(r):
            self.feed_down(r, last)

            def block(b):
                second = self.norm(self.res[r, b], 1, r, b)
                self.act[at.mem + r, b] = self.norm(second, 2, r, b).astype(BF16)

            self.blocks(block)
            pl.when(r > 0)(lambda: self.x_copy(at.mem, r - 1, 0).wait_send())
            self.x_copy(at.mem, r, 0).start()
            self.store(at.mem + r, self.result, r, r).start()

        self.loop(rows, send)
        steps = Steps()
        if self.inner:
            feed = list(range(self.t_down, self.t_all)) + list(range(self.t_up, self.t_down))
            steps = self.reduce_steps(feed + [4, 5, 3, 0, 1, 2])

        def back(r):
            self.x_copy(at.gmem, r, 2).wait_recv()
            self.upstream(at.cq + r, r).wait()

            def block(b):
                up = self.act[at.cq + r, b]
                grad = up.astype(F32) + self.act[at.gmem + r, b].astype(F32)
                grad = self.norm_back(self.norm_back(grad, 2, r, b), 1, r, b)
                self.res[r, b] = grad
                self.act[at.gdown + r, b] = grad.astype(BF16)

            self.blocks(block)

            @pl.when(r == rows - 1)
            def down():
                self.down_grads()
                steps.more(3)

            self.feed_back(r)

            def block(b):
                grad = self.norm_back(self.res[r, b], 0, r, b)
                self.res[r, b] = grad
                self.act[at.gout + r, b] = grad.astype(BF16)

            self.blocks(block)

            @pl.when(r == rows - 1)
            def up():
                self.up_grads(at.first)
                steps.more(2)

            base = steps.next
            steps.next += 4

            def step(n):
                pl.when(r == rows - 1)(functools.partial(steps.run, base + n))

            self.self_back(r, step)

        self.loop(rows, back)
        small = Steps()
        if self.inner:
            small = self.small_steps()
            small.more(1)
        self.self_grads()
        small.more(1)
        steps.more(2)
        small.more(1)
        steps.finish()
        small.finish()
        self.length_copy().wait_send()
        if self.inner:
            self.shard_copy().wait_send()
            self.drain()
        self.x_copy(at.mem, rows - 1, 0).wait_send()
        for r in range(rows):
            self.store(at.mem + r, self.result, r, r).wait()
            self.store(at.stage + r, self.grad_in, r, 2 + r).wait()
        if not self.inner:
            self.keep_grads()

    def reduce_steps(self, tiles):
        stages = [(0, self.reduce1), (1, self.reduce2), (3, self.reduce3), (5, self.reduce4)]
        stages += [(7, self.reduce5), (9, self.reduce6), (10, self.reduce7)]
        return Steps(self, tiles, stages)

    def keep_grads(self):
        tiles = list(range(self.t_all))
        if self.encoding:
            tiles = [k for k in tiles if not self.from_partner(k)]
        else:
            tiles += [self.t_mem, self.t_mem + 1]
        copies = [
            pltpu.make_async_copy(
                self.act.at[self.tile_slot(k)], self.whole_grad(k), self.grad_sem.at[k]
            )
            for k in tiles
        ]
        for copy in copies:
            copy.start()
        for copy in copies:
            copy.wait()
        for j in range(3):
            self.g_gain[pl.ds(j, 1), :] = jnp.sum(self.gacc[j], axis=0, keepdims=True)
            self.g_bias[pl.ds(j, 1), :] = jnp.sum(self.gacc[3 + j], axis=0, keepdims=True)

    def decoder(self):
        at, rows = self.at, self.rows
        for r in range(rows):
            self.upstream(at.gcross + r, r).start()
        steps = Steps()
        if self.inner:
            steps = self.gather_steps(list(range(8)) + self.feed_chunks)
            self.shard_copy().wait_recv()
            steps.until(9)
        self.self_forward(True, steps)
        steps.until(13)

        def ask(r):
            queries = matmul_nn(self.act[at.first + r], self.weight(4)) * query_scale
            self.act[at.cq + r] = queries.astype(BF16)

        self.loop(rows, ask)
        self.length_copy().wait_recv()
        base = steps.next
        steps.next = steps.count

        def middle(r):
            def step(n, count):
                @pl.when(r == 0)
                def some():
                    for m in range(base + n, base + n + count):
                        steps.run(m)

            self.fill_mask(r, self.src_len, False)
            self.spilled(r, False).wait()
            self.x_copy(at.mem, r, 0).wait_recv()
            for j in range(2):
                self.act[at.kv + j * rows + r] = matmul_nn(
                    self.act[at.mem + r], self.weight(self.w_memory_at + j)
                ).astype(BF16)
            step(0, 2)
            k, v = at.kv + r, at.kv + rows + r
            self.attend(at.cq + r, k, v, at.oc + r, r)
            step(2, steps.count)
            self.res[r] += matmul_tn(self.act[at.oc + r], self.weight(5))

            def block(b):
                out = self.norm(self.res[r, b], 1, r, b)
                self.res[r, b] = out
                self.act[at.second + r, b] = out.astype(BF16)

            self.blocks(block)
            for t in range(self.ff_tiles):
                self.feed_up(at.second + r, r, t)
            for j in range(self.down_bands):
                self.feed_down(r, j)
            self.upstream(at.gcross + r, r).wait()

            def block(b):
                out = self.norm(self.res[r, b], 2, r, b)
                self.act[at.stage + r, b] = out.astype(BF16)
                up = self.act[at.gcross + r, b]
                grad = self.norm_back(up.astype(F32), 2, r, b)
                self.res[r, b] = grad
                self.act[at.gdown + r, b] = grad.astype(BF16)

            self.blocks(block)
            self.store(at.stage + r, self.result, r, r).start()
            self.feed_back(r)

            def block(b):
                grad = self.norm_back(self.res[r, b], 1, r, b)
                self.res[r, b] = grad
                self.act[at.gcross + r, b] = grad.astype(BF16)

            self.blocks(block)
            self.act[at.dout] = matmul_nt(self.weight(5), self.act[at.gcross + r]).astype(BF16)
            self.attend_back(at.cq + r, k, v, at.oc + r, at.dout, r)
            total = matmul_nt(self.act[k], self.weight(self.w_memory_at))
            total = total + matmul_nt(self.act[v], self.weight(self.w_memory_at + 1))
            self.act[at.gmem + r] = total.astype(BF16)
            self.x_copy(at.gmem, r, 2).start()
            self.spilled(r, True).start()
            self.res[r] += matmul_nt(self.act[at.cq + r], self.weight(4))

            def block(b):
                grad = self.norm_back(self.res[r, b], 0, r, b)
                self.res[r, b] = grad
                self.act[at.gout + r, b] = grad.astype(BF16)

            self.blocks(block)

        self.loop(rows, middle)
        steps, small = Steps(), Steps()
        x = self.both(at.mem)

        def memory_grad(j):
            slot = at.kv + j * rows
            self.weight_grad(slot, x, self.both(slot))

        self.loop(2, memory_grad)
        if self.inner:
            feed = list(range(self.t_down, self.t_all)) + list(range(self.t_up, self.t_down))
            steps = self.reduce_steps([self.t_mem, self.t_mem + 1] + feed + [4, 5, 3, 0, 1, 2])
            small = self.small_steps()
        steps.more(2)
        self.down_grads()
        steps.more(3)
        small.more(1)
        self.up_grads(at.second)
        steps.more(2)
        self.weight_grad(at.cq, self.both(at.first), self.both(at.cq))
        self.out_grad(self.t_cross + 1, at.oc, at.gcross)
        base = steps.next
        steps.next += 2 * rows

        def back(r):
            self.spilled(r, True).wait()
            self.store(at.stage + r, self.result, r, r).wait()

            def step(n):
                if n % 2 == 0:
                    for m in range(rows):
                        pl.when(r == m)(functools.partial(steps.run, base + 2 * m + n // 2))

            self.self_back(r, step)

        self.loop(rows, back)
        small.more(1)
        self.self_grads()
        small.more(1)
        steps.finish()
        small.finish()
        if self.inner:
            self.drain()
        for r in range(rows):
            self.x_copy(at.gmem, r, 2).wait_send()
            self.store(at.stage + r, self.grad_in, r, 2 + r).wait()
        if not self.inner:
            self.keep_grads()


def both_layers(inner, dp, call, emb, cot, lengths, gain, bias, weights):
    rows = lengths.shape[0]
    model = emb.shape[1]
    ff_tiles = weights[3].shape[1] // TILE
    tiles = 6 + 2 * ff_tiles
    sums = tiles + 2
    vmem = pl.BlockSpec(memory_space=pltpu.VMEM)
    anywhere = pl.BlockSpec(memory_space=pl.ANY)
    dma = pltpu.SemaphoreType.DMA
    square = (TILE, TILE)
    scratch = [
        pltpu.VMEM((Slots(rows, ff_tiles).count,) + square, BF16),
        pltpu.VMEM((rows, HEADS) + square, BF16),
        pltpu.VMEM((rows,) + square, F32),
        pltpu.VMEM(square, F32),
        pltpu.VMEM((rows, TILE, 128), F32),
        pltpu.VMEM((6, 8, model), F32),
        pltpu.VMEM((8, 128), jnp.int32),
        pltpu.VMEM((8, 128), jnp.int32),
        dma((8,)),
        dma((8,)),
        dma((8,)),
    ]
    if inner:
        part = TILE // 16
        chunks = 8 + ff_tiles + TILE // down_columns
        scratch += [
            pltpu.VMEM((8 + ff_tiles, LINE, 2, 2, part, TILE), BF16),
            pltpu.VMEM((LINE, 2, 2, weights[4].shape[0], TILE), BF16),
            pltpu.VMEM((part, 2 * TILE), BF16),
            pltpu.VMEM((2, part, TILE), BF16),
            pltpu.VMEM((sums, TILE // 2, TILE), BF16),
            pltpu.VMEM((sums, TILE // 4, TILE), BF16),
            pltpu.VMEM((sums, LINE - 1, part, TILE), BF16),
            pltpu.VMEM((3, 8, model), F32),
            pltpu.VMEM((2 + LINE, 8, model), F32),
        ]
        line = (LINE - 1,)
        scratch += [dma((chunks,) + line)] * 2 + [dma((chunks,))] * 4
        scratch += [dma((sums,))] * 4 + [dma((sums,) + line)] * 4
        scratch += [dma((sums,))] * 4 + [dma((sums,)), dma((2 + LINE,)), dma((2 + LINE,))]
    else:
        scratch += [dma((sums,))]

    hidden = ff_tiles * TILE
    grads = [(model, 3 * TILE), square, (model, 2 * TILE), (model, hidden), (hidden, model)]
    if not inner:
        grads += [(model, 2 * TILE)]

    def kernel(*refs):
        Body(inner, rows, dp, ff_tiles, refs).run()

    return pl.pallas_call(
        kernel,
        out_shape=(
            jax.ShapeDtypeStruct(emb.shape, BF16),
            jax.ShapeDtypeStruct(emb.shape, BF16),
            *(jax.ShapeDtypeStruct(shape, BF16) for shape in grads),
            jax.ShapeDtypeStruct(gain.shape, F32),
            jax.ShapeDtypeStruct(bias.shape, F32),
            jax.ShapeDtypeStruct((rows, HEADS) + square, BF16),
        ),
        in_specs=[vmem, anywhere] + [vmem] * (3 + len(weights)),
        out_specs=(anywhere,) * (2 + len(grads)) + (vmem, vmem, anywhere),
        scratch_shapes=scratch,
        compiler_params=pltpu.CompilerParams(
            collective_id=call, has_side_effects=True, vmem_limit_bytes=62 * 2**20
        ),
        name="layers",
    )(emb, cot, lengths, gain, bias, *weights)


def passed_along(shard, axis, by):
    count = lax.axis_size(axis)
    pairs = [(i, i + by) for i in range(count) if 0 <= i + by < count]
    return lax.ppermute(shard, axis, pairs)


def local(
    embedded,
    lengths,
    cotangent,
    attn_in,
    attn_out,
    cross_weight,
    up_weight,
    down_weight,
    norm_gain,
    norm_bias,
):
    dp = lax.axis_size("dp")
    rows = lengths.shape[1]
    shards = tuple(w[0] for w in (attn_in, attn_out, cross_weight, up_weight, down_weight))
    inner = dp == 4 * LINE and rows <= CALL_ROWS
    args = (embedded[0], cotangent[0], lengths[0], norm_gain[0], norm_bias[0])
    if inner:
        result, grad_in, *grads, gain, bias, spill = both_layers(inner, dp, 0, *args, shards)
        grads = [grad.astype(F32) for grad in grads]
    else:
        weights = tuple(lax.all_gather(w, "dp", axis=0, tiled=True) for w in shards)
        weights += (passed_along(weights[2], "section", 1),)
        parts = []
        for call in range(0, rows, CALL_ROWS):
            span = slice(call * TILE, min(rows, call + CALL_ROWS) * TILE)
            lens = args[2][call : call + CALL_ROWS]
            parts.append(
                both_layers(
                    inner, dp, call // CALL_ROWS, args[0][span], args[1][span], lens, *args[3:], weights
                )
            )
        result = jnp.concatenate([part[0] for part in parts], axis=0)
        grad_in = jnp.concatenate([part[1] for part in parts], axis=0)
        sums = [sum(part[n].astype(F32) for part in parts) for n in range(2, 10)]
        *grads, memory, gain, bias = lax.psum(tuple(sums), "dp")
        is_first = lax.axis_index("section") == 0
        grads[2] = jnp.where(is_first, passed_along(memory, "section", -1), grads[2])
    return tuple(out[None] for out in (result, grad_in, *grads, gain, bias))


def solution(mesh):
    rows = P("section", "dp", None)
    whole = P("section", None, None)
    in_specs = (rows,) * 8 + (whole,) * 2
    out_specs = (rows,) * 2 + (whole,) * 7
    return jax.shard_map(local, mesh=mesh, in_specs=in_specs, out_specs=out_specs, check_vma=False)
```

```python
import functools

import jax
import jax.numpy as jnp
from jax import lax
from jax.experimental import pallas as pl
from jax.experimental.pallas import tpu as pltpu
from jax.sharding import PartitionSpec as P

HEADS = 8

norm_eps = 1e-06
masked_score = -1e30
F32 = jnp.float32
BF16 = jnp.bfloat16
MESH = pl.DeviceIdType.MESH
down_columns = 128
query_scale = 0.125
LINE = 4
CALL_ROWS = 2
TILE = 512


def matmul_nn(left, right):
    return jnp.dot(left, right, preferred_element_type=F32)


def matmul_tn(left, right):
    return lax.dot_general(left, right, (((0,), (0,)), ((), ())), preferred_element_type=F32)


def matmul_nt(left, right):
    return lax.dot_general(left, right, (((1,), (1,)), ((), ())), preferred_element_type=F32)


class Steps:
    def __init__(self, body=None, items=(), stages=()):
        self.body = body
        self.items = items
        self.stages = stages
        self.count = len(items) + stages[-1][0] if items else 0
        self.next = 0

    def run(self, n):
        if n >= self.count:
            return
        for offset, act in reversed(self.stages):
            if 0 <= n - offset < len(self.items):
                item = self.items[n - offset]
                act(item)
                self.body.done.append((act, item))

    def until(self, n):
        while self.next < n:
            self.run(self.next)
            self.next += 1

    def more(self, n):
        self.until(self.next + n)

    def finish(self):
        self.until(self.count)


class Slots:
    def __init__(self, rows, ff_tiles):
        self.rows = rows
        self.count = 0
        self.qkv = self.take(3 * rows)
        self.cq = self.take(rows)
        self.kv = self.take(2 * rows)
        self.pre = self.take(ff_tiles * rows)
        self.hid = self.take(ff_tiles * rows)
        self.att = self.take(rows)
        self.oc = self.take(rows)
        self.first = self.take(rows)
        self.second = self.take(rows)
        self.mem = self.take(rows)
        self.gmem = self.take(rows)
        self.gdown = self.take(rows)
        self.gout = self.take(rows)
        self.gcross = self.take(rows)
        self.stage = self.take(rows)
        self.dout = self.take(1)
        self.xhat = self.take(3 * rows)

    def take(self, n):
        at = self.count
        self.count += n
        return at


class Body:
    def __init__(self, inner, rows, dp, ff_tiles, refs):
        self.inner = inner
        self.rows = rows
        self.ff_tiles = ff_tiles
        self.at = Slots(rows, ff_tiles)
        names = ["emb_in", "cot", "lengths", "gain", "bias"]
        names += ["w_in", "w_out", "w_cross", "w_up", "w_down"]
        if not inner:
            names += ["w_memory"]
        names += ["result", "grad_in", "g_in", "g_out", "g_cross", "g_up", "g_down"]
        if not inner:
            names += ["g_memory"]
        names += ["g_gain", "g_bias", "spill"]
        names += ["emb", "emb_sem", "act", "probs", "res", "mask", "rstd", "gacc", "own_len", "src_len"]
        names += ["local_sem", "x_send", "x_recv"]
        if not inner:
            names += ["grad_sem"]
        if inner:
            names += ["wt", "wd", "x_shard", "x_grad", "r1", "r2", "r3", "gbuf", "grcv"]
            names += ["gown_sem", "gz_s", "gz_r", "gy_s", "gy_r", "gc_s", "gc_r"]
            names += ["a1_s", "a1_r", "a2_s", "a2_r", "a3_s", "a3_r"]
            names += ["a4_s", "a4_r", "a5_s", "a5_r", "a6_s", "a6_r", "own_sem", "gs_s", "gs_r"]
        assert len(names) == len(refs), (len(names), len(refs))
        for name, ref in zip(names, refs):
            setattr(self, name, ref)
        self.sec = lax.axis_index("section")
        self.i = lax.axis_index("dp")
        self.across = (1 - self.sec, self.i)
        if inner:
            self.c = lax.rem(self.i, 2)
            self.y = lax.rem(self.i // 2, 2)
            self.z = self.i // 4
            self.core_dev = (self.sec, self.z * 4 + self.y * 2 + (1 - self.c))
            self.y_dev = (self.sec, self.z * 4 + (1 - self.y) * 2 + self.c)
            self.z_other = [lax.rem(self.z + d, LINE) for d in range(1, LINE)]
            self.z_dev = [(self.sec, zz * 4 + self.y * 2 + self.c) for zz in self.z_other]
        self.done = []
        self.draining = False
        self.encoding = True
        self.t_in = 0
        self.t_out = 3
        self.t_cross = 4
        self.t_up = 6
        self.t_down = 6 + ff_tiles
        self.t_all = 6 + 2 * ff_tiles
        self.t_mem = self.t_all
        self.w_memory_at = 6
        self.w_up_at = 8
        self.down_bands = TILE // down_columns
        self.feed_chunks = [self.w_up_at + n for n in range(ff_tiles + self.down_bands)]


    def remote(self, src, dst, send, recv, dev):
        return pltpu.make_async_remote_copy(
            src_ref=src, dst_ref=dst, send_sem=send, recv_sem=recv, device_id=dev, device_id_type=MESH
        )

    def send(self, src, dst, send, recv, dev):
        copy = self.remote(src, dst, send, recv, dev)
        if self.draining:
            copy.wait_send()
        else:
            copy.start()

    def drain(self):
        self.draining = True
        for act, item in self.done:
            act(item)
        self.draining = False
        self.done = []

    def barrier(self):
        sem = pltpu.get_barrier_semaphore()
        devs = [self.across]
        if self.inner:
            devs += [self.core_dev, self.y_dev] + self.z_dev
        for dev in devs:
            pl.semaphore_signal(sem, inc=1, device_id=dev, device_id_type=MESH)
        pl.semaphore_wait(sem, len(devs))


    def weight(self, k):
        if self.inner:
            return self.wt[k].reshape(TILE, TILE)
        if k < 3:
            return self.w_in[:, k * TILE : (k + 1) * TILE]
        if k == 3:
            return self.w_out[...]
        if k < 6:
            return self.w_cross[:, (k - 4) * TILE : (k - 3) * TILE]
        if k < 8:
            return self.w_memory[:, (k - 6) * TILE : (k - 5) * TILE]
        return self.w_up[:, (k - 8) * TILE : (k - 7) * TILE]

    def weight_up(self, t):
        if self.inner:
            return self.wt[self.w_up_at + t].reshape(TILE, TILE)
        start = t * TILE
        return self.w_up[:, pl.ds(start if isinstance(start, int) else pl.multiple_of(start, TILE), TILE)]

    def weight_down(self, t, cols=slice(None)):
        if self.inner:
            tile = self.wd[t, :, :, :, cols]
            return tile.reshape(TILE, tile.shape[-1])
        return self.w_down[t * TILE : (t + 1) * TILE, cols]

    def chunk_source(self, k):
        z, y, c = self.z, self.y, self.c
        down_at = self.w_up_at + self.ff_tiles
        if k < 3:
            src = self.w_in.at[:, pl.ds(k * TILE, TILE)]
        elif k == 3:
            src = self.w_out.at[...]
        elif k < 6:
            src = self.w_cross.at[:, pl.ds((k - 4) * TILE, TILE)]
        elif k < 8:
            src = self.x_shard.at[:, pl.ds((k - 6) * TILE, TILE)]
        elif k < down_at:
            src = self.w_up.at[:, pl.ds((k - 8) * TILE, TILE)]
        else:
            cols = pl.ds((k - down_at) * down_columns, down_columns)
            src = self.w_down.at[:, cols]
        if k < down_at:
            whole = self.wt.at[k]
            own = whole.at[z, y, c]
            line = whole.at[:, y, c]
            plane = whole.at[:, :, c]
        else:
            own = self.wd.at[z, y, c, :, cols]
            line = self.wd.at[:, y, c, :, cols]
            plane = self.wd.at[:, :, c, :, cols]
        return src, own, line, plane

    def gather1(self, k):
        src, own, line, plane = self.chunk_source(k)
        if not self.draining:
            pltpu.make_async_copy(src, own, self.gown_sem.at[k]).start()
        for d in range(LINE - 1):
            self.send(src, own, self.gz_s.at[k, d], self.gz_r.at[k, d], self.z_dev[d])

    def gather2(self, k):
        src, own, line, plane = self.chunk_source(k)
        if not self.draining:
            pltpu.make_async_copy(src, own, self.gown_sem.at[k]).wait()
        for d in range(0 if self.draining else LINE - 1):
            self.remote(src, own, self.gz_s.at[k, d], self.gz_r.at[k, d], self.z_dev[d]).wait_recv()
        self.send(line, line, self.gy_s.at[k], self.gy_r.at[k], self.y_dev)

    def gather3(self, k):
        src, own, line, plane = self.chunk_source(k)
        if not self.draining:
            self.remote(line, line, self.gy_s.at[k], self.gy_r.at[k], self.y_dev).wait_recv()
        self.send(plane, plane, self.gc_s.at[k], self.gc_r.at[k], self.core_dev)

    def gather4(self, k):
        src, own, line, plane = self.chunk_source(k)
        if not self.draining:
            self.remote(plane, plane, self.gc_s.at[k], self.gc_r.at[k], self.core_dev).wait_recv()

    def gather_steps(self, chunks):
        stages = [(0, self.gather1), (2, self.gather2), (4, self.gather3), (5, self.gather4)]
        return Steps(self, chunks, stages)


    def tile_slot(self, k):
        at, rows = self.at, self.rows
        if k < 3:
            return at.qkv + k * rows
        if k == 3:
            return at.gout
        if k == 4:
            return at.cq
        if k == 5:
            return at.gcross
        if k < self.t_down:
            return at.pre + (k - self.t_up) * rows
        if k < self.t_all:
            return at.hid + (k - self.t_down) * rows
        return at.kv + (k - self.t_mem) * rows

    def whole_grad(self, k, start=0, size=TILE):
        rows = pl.ds(start, size)

        def columns(ref, n):
            return ref.at[rows, pl.ds(n * TILE, TILE)]

        if k < 3:
            return columns(self.g_in, k)
        if k == 3:
            return columns(self.g_out, 0)
        if k < 6:
            return columns(self.g_cross, k - self.t_cross)
        if k < self.t_down:
            return columns(self.g_up, k - self.t_up)
        if k < self.t_all:
            return self.g_down.at[pl.ds((k - self.t_down) * TILE + start, size), :]
        return columns(self.g_memory, k - self.t_mem)

    def from_partner(self, k):
        return self.encoding and k in (self.t_cross, self.t_cross + 1)

    def block_at(self, c, y=0, z=0):
        return c * (TILE // 2) + y * (TILE // 4) + z * (TILE // 16)

    def reduce1(self, k):
        if self.from_partner(k):
            return
        slot = self.tile_slot(k)
        half = TILE // 2
        src = self.act.at[slot, pl.ds(self.block_at(1 - self.c), half)]
        self.send(src, self.r1.at[k], self.a1_s.at[k], self.a1_r.at[k], self.core_dev)

    def reduce2(self, k):
        if self.from_partner(k):
            return
        slot = self.tile_slot(k)
        half, quarter = TILE // 2, TILE // 4
        own = pl.ds(pl.multiple_of(self.block_at(self.c), half), half)
        src = self.act.at[slot, own]
        if not self.draining:
            self.remote(
                src, self.r1.at[k], self.a1_s.at[k], self.a1_r.at[k], self.core_dev
            ).wait_recv()
            total = self.act[slot, own].astype(F32) + self.r1[k].astype(F32)
            self.act[slot, own] = total.astype(BF16)
        src = self.act.at[slot, pl.ds(self.block_at(self.c, 1 - self.y), quarter)]
        self.send(src, self.r2.at[k], self.a2_s.at[k], self.a2_r.at[k], self.y_dev)

    def reduce3(self, k):
        if self.from_partner(k):
            return
        slot = self.tile_slot(k)
        quarter, part = TILE // 4, TILE // 16
        own = pl.ds(pl.multiple_of(self.block_at(self.c, self.y), quarter), quarter)
        src = self.act.at[slot, own]
        if not self.draining:
            self.remote(
                src, self.r2.at[k], self.a2_s.at[k], self.a2_r.at[k], self.y_dev
            ).wait_recv()
            total = self.act[slot, own].astype(F32) + self.r2[k].astype(F32)
            self.act[slot, own] = total.astype(BF16)
        for d in range(LINE - 1):
            src = self.act.at[slot, pl.ds(self.block_at(self.c, self.y, self.z_other[d]), part)]
            self.send(src, self.r3.at[k, d], self.a3_s.at[k, d], self.a3_r.at[k, d], self.z_dev[d])

    def reduce4(self, k):
        if self.from_partner(k):
            return self.reduce4_memory(k)
        slot = self.tile_slot(k)
        part = TILE // 16
        own = pl.ds(pl.multiple_of(self.block_at(self.c, self.y, self.z), part), part)
        src = self.act.at[slot, own]
        if not self.draining:
            total = self.act[slot, own].astype(F32)
            for d in range(LINE - 1):
                self.remote(
                    src, self.r3.at[k, d], self.a3_s.at[k, d], self.a3_r.at[k, d], self.z_dev[d]
                ).wait_recv()
                total = total + self.r3[k, d].astype(F32)
            self.act[slot, own] = total.astype(BF16)
        if k < self.t_all:
            self.spread(k, src)
        else:
            j = k - self.t_mem
            dst = self.x_grad.at[j]
            self.send(src, dst, self.x_send.at[6 + j], self.x_recv.at[6 + j], self.across)

    def spread(self, k, src):
        part = TILE // 16
        dst = self.whole_grad(k, self.block_at(self.c, self.y, self.z), part)
        if not self.draining:
            pltpu.make_async_copy(src, dst, self.own_sem.at[k]).start()
        for d in range(LINE - 1):
            self.send(src, dst, self.a4_s.at[k, d], self.a4_r.at[k, d], self.z_dev[d])

    def reduce4_memory(self, k):
        j = k - self.t_cross
        src = self.x_grad.at[j]
        if not self.draining:
            self.remote(
                src, src, self.x_send.at[6 + j], self.x_recv.at[6 + j], self.across
            ).wait_recv()
        self.spread(k, src)

    def reduce5(self, k):
        if k >= self.t_all:
            return
        quarter, part = TILE // 4, TILE // 16
        own = self.whole_grad(k, self.block_at(self.c, self.y, self.z), part)
        if not self.draining:
            pltpu.make_async_copy(own, own, self.own_sem.at[k]).wait()
        for d in range(0 if self.draining else LINE - 1):
            self.remote(
                own, own, self.a4_s.at[k, d], self.a4_r.at[k, d], self.z_dev[d]
            ).wait_recv()
        line = self.whole_grad(k, self.block_at(self.c, self.y), quarter)
        self.send(line, line, self.a5_s.at[k], self.a5_r.at[k], self.y_dev)

    def reduce6(self, k):
        if k >= self.t_all:
            return
        half, quarter = TILE // 2, TILE // 4
        line = self.whole_grad(k, self.block_at(self.c, self.y), quarter)
        if not self.draining:
            self.remote(line, line, self.a5_s.at[k], self.a5_r.at[k], self.y_dev).wait_recv()
        plane = self.whole_grad(k, self.block_at(self.c), half)
        self.send(plane, plane, self.a6_s.at[k], self.a6_r.at[k], self.core_dev)

    def reduce7(self, k):
        if k >= self.t_all:
            return
        plane = self.whole_grad(k, self.block_at(self.c), TILE // 2)
        if not self.draining:
            self.remote(plane, plane, self.a6_s.at[k], self.a6_r.at[k], self.core_dev).wait_recv()

    def small_steps(self):
        stages = [(0, self.small1), (1, self.small2), (2, self.small3), (3, self.small4)]
        return Steps(self, [0], stages)

    def small1(self, item):
        if not self.draining:
            for j in range(6):
                self.gbuf[0, pl.ds(j, 1), :] = jnp.sum(self.gacc[j], axis=0, keepdims=True)
            self.gbuf[0, pl.ds(6, 2), :] = jnp.zeros((2, TILE), F32)
        self.send(self.gbuf.at[0], self.grcv.at[0], self.gs_s.at[0], self.gs_r.at[0], self.core_dev)

    def small2(self, item):
        if not self.draining:
            self.remote(
                self.gbuf.at[0], self.grcv.at[0], self.gs_s.at[0], self.gs_r.at[0], self.core_dev
            ).wait_recv()
            self.gbuf[1] = self.gbuf[0] + self.grcv[0]
        self.send(self.gbuf.at[1], self.grcv.at[1], self.gs_s.at[1], self.gs_r.at[1], self.y_dev)

    def small3(self, item):
        if not self.draining:
            self.remote(
                self.gbuf.at[1], self.grcv.at[1], self.gs_s.at[1], self.gs_r.at[1], self.y_dev
            ).wait_recv()
            self.gbuf[2] = self.gbuf[1] + self.grcv[1]
        for d in range(LINE - 1):
            self.send(
                self.gbuf.at[2],
                self.grcv.at[2 + self.z],
                self.gs_s.at[2 + d],
                self.gs_r.at[2 + d],
                self.z_dev[d],
            )
        if not self.draining:
            self.grcv[2 + self.z] = self.gbuf[2]

    def small4(self, item):
        if self.draining:
            return
        for d in range(LINE - 1):
            self.remote(
                self.gbuf.at[2],
                self.grcv.at[2 + self.z],
                self.gs_s.at[2 + d],
                self.gs_r.at[2 + d],
                self.z_dev[d],
            ).wait_recv()
        total = self.grcv[2]
        for n in range(1, LINE):
            total = total + self.grcv[2 + n]
        self.g_gain[...] = total[0:3]
        self.g_bias[...] = total[3:6]


    def fill_mask(self, r, key_len, causal):
        lane = lax.broadcasted_iota(jnp.int32, (8, 128), 1)
        sub = lax.broadcasted_iota(jnp.int32, (8, 128), 0)

        def ends_of(ref):
            spans = jnp.broadcast_to(ref[pl.ds(r, 1), :], (8, 128))
            return jnp.sum(jnp.where(lane <= sub, spans, 0).astype(F32), axis=1, keepdims=True)

        ends = ends_of(key_len)
        flat = jnp.sum(jnp.where(lane == sub, ends, 0.0), axis=0, keepdims=True)
        flat = jnp.where(lane[:1] < 8, flat, 1e9)
        pos = lax.broadcasted_iota(jnp.int32, (TILE, 128), 0).astype(F32)
        key_ids = jnp.sum(jnp.where(pos >= flat, 1.0, 0.0), axis=1, keepdims=True)
        query_ends = ends_of(self.own_len)
        pos = lax.broadcasted_iota(jnp.int32, (8, TILE), 1).astype(F32)
        query_ids = jnp.sum(jnp.where(pos >= query_ends, 1.0, 0.0), axis=0, keepdims=True)
        step = 128
        for b in range(TILE // step):
            allowed = key_ids[b * step : (b + 1) * step] == query_ids
            if causal:
                k_pos = lax.broadcasted_iota(jnp.int32, (step, TILE), 0) + b * step
                q_pos = lax.broadcasted_iota(jnp.int32, (step, TILE), 1)
                allowed = allowed & (k_pos <= q_pos)
            self.mask[b * step : (b + 1) * step, :] = jnp.where(allowed, 0.0, masked_score)


    def attend(self, q, k, v, out, r, first=0, count=HEADS // 2):
        act = self.act
        low = lax.broadcasted_iota(jnp.int32, (1, 128), 1) < 64

        def pair(n, carry):
            hp = first + n
            cols = pl.ds(pl.multiple_of(hp * 128, 128), 128)
            qs, ks, vs = act[q, :, cols], act[k, :, cols], act[v, :, cols]
            scores = []
            for j in range(2):
                qm = jnp.where(low if j == 0 else ~low, qs, jnp.zeros_like(qs))
                s = matmul_nt(ks, qm) + self.mask[...]
                scores.append((s, jnp.max(s, axis=0, keepdims=True)))
            weights = []
            for j, (s, top) in enumerate(scores):
                raised = jnp.exp(s - top)
                raised = raised * (1.0 / jnp.sum(raised, axis=0, keepdims=True))
                weights.append(raised.astype(BF16))
                self.probs[r, hp * 2 + j] = weights[j]
            for j, probs in enumerate(weights):
                o = matmul_tn(vs, probs)[64 * j : 64 * j + 64]
                rows = pl.ds(pl.multiple_of(hp * 128 + 64 * j, 64), 64)
                act[out, rows, :] = o.astype(BF16)
            return carry

        lax.fori_loop(0, count, pair, 0)

    def attend_back(self, q, k, v, out, dout, r, first=0, count=HEADS // 2):
        act = self.act
        low = lax.broadcasted_iota(jnp.int32, (1, 128), 1) < 64

        def pair(n, carry):
            hp = first + n
            cols = pl.ds(pl.multiple_of(hp * 128, 128), 128)
            qs, ks, vs = act[q, :, cols], act[k, :, cols], act[v, :, cols]
            grads = []
            for j in range(2):
                rows = pl.ds(pl.multiple_of(hp * 128 + 64 * j, 64), 64)
                do = act[dout, rows, :]
                prod = do.astype(F32) * act[out, rows, :].astype(F32)
                delta = jnp.sum(prod, axis=0, keepdims=True)
                none = jnp.zeros_like(do)
                do = jnp.concatenate([do, none] if j == 0 else [none, do], axis=0)
                grads.append((do, delta, matmul_nn(vs, do)))
            scores = []
            for j, (do, delta, dp) in enumerate(grads):
                probs = self.probs[r, hp * 2 + j]
                scores.append((probs, (probs.astype(F32) * (dp - delta)).astype(BF16)))
            dq, dk, dv = [], None, None
            for j, (probs, ds) in enumerate(scores):
                qm = jnp.where(low if j == 0 else ~low, qs, jnp.zeros_like(qs))
                a, b = matmul_nt(probs, grads[j][0]), matmul_nn(ds, qm)
                dv, dk = (a, b) if j == 0 else (dv + a, dk + b)
                dq.append(matmul_tn(ks, ds)[64 * j : 64 * j + 64])
            dq = (jnp.concatenate(dq, axis=0) * 0.125).astype(BF16)
            act[q, :, cols] = dq.T
            act[k, :, cols] = dk.astype(BF16)
            act[v, :, cols] = dv.astype(BF16)
            return carry

        lax.fori_loop(0, count, pair, 0)


    def blocks(self, body):
        step = 128

        def one(b, carry):
            body(pl.ds(pl.multiple_of(b * step, step), step))
            return carry

        lax.fori_loop(0, TILE // step, one, 0, unroll=True)

    def norm(self, values, n, r, rows):
        center = jnp.mean(values, axis=-1, keepdims=True)
        shifted = values - center
        scale = lax.rsqrt(jnp.mean(shifted * shifted, axis=-1, keepdims=True) + norm_eps)
        hat = shifted * scale
        self.act[self.at.xhat + n * self.rows + r, rows] = hat.astype(BF16)
        self.rstd[r, rows, pl.ds(n, 1)] = scale
        return hat * self.gain[pl.ds(n, 1), :] + self.bias[pl.ds(n, 1), :]

    def norm_back(self, grad, n, r, rows):
        hat = self.act[self.at.xhat + n * self.rows + r, rows].astype(F32)
        scale = self.rstd[r, rows, pl.ds(n, 1)]
        count = grad.shape[0] // 8
        self.gacc[n] += jnp.sum((grad * hat).reshape(count, 8, TILE), axis=0)
        self.gacc[3 + n] += jnp.sum(grad.reshape(count, 8, TILE), axis=0)
        up = grad * self.gain[pl.ds(n, 1), :]
        first = jnp.mean(up, axis=-1, keepdims=True)
        second = jnp.mean(up * hat, axis=-1, keepdims=True)
        return (up - first - hat * second) * scale


    def row(self, r):
        start = r * TILE
        return pl.ds(start if isinstance(start, int) else pl.multiple_of(start, TILE), TILE)

    def loop(self, count, body):
        def one(n, carry):
            body(n)
            return carry

        lax.fori_loop(0, count, one, 0)

    def self_in(self, r):
        x = self.emb[self.row(r), :]
        for j in range(3):
            rows = matmul_nn(x, self.weight(j))
            if j == 0:
                rows = rows * query_scale
            self.act[self.at.qkv + j * self.rows + r] = rows.astype(BF16)

    def self_forward(self, causal, steps):
        at, rows = self.at, self.rows
        base = steps.next
        steps.next += 3 * rows

        def one(r):
            self.self_in(r)
            for n in range(rows):
                pl.when(r == n)(functools.partial(steps.run, base + 3 * n))
            self.fill_mask(r, self.own_len, causal)
            q, k, v = (at.qkv + j * rows + r for j in range(3))

            def half(h):
                self.attend(q, k, v, at.att + r, r, 2 * h, 2)
                for n in range(rows):
                    for m in range(2):
                        pl.when((r == n) & (h == m))(
                            functools.partial(steps.run, base + 3 * n + 1 + m)
                        )

            self.loop(HEADS // 4, half)
            if not self.encoding:
                self.spilled(r, False).start()
            self.self_out(r)

        self.loop(rows, one)

    def self_out(self, r):
        at = self.at
        x = self.emb[self.row(r), :].astype(F32)
        self.res[r] = x + matmul_tn(self.act[at.att + r], self.weight(3))

        def block(rows):
            out = self.norm(self.res[r, rows], 0, r, rows)
            self.res[r, rows] = out
            self.act[at.first + r, rows] = out.astype(BF16)

        self.blocks(block)

    def feed_up(self, x_slot, r, t):
        at = self.at
        pre = matmul_nn(self.act[x_slot], self.weight_up(t))
        hid = (pre / (1.0 + jnp.exp(-pre))).astype(BF16)
        self.act[at.pre + t * self.rows + r] = pre.astype(BF16)
        self.act[at.hid + t * self.rows + r] = hid

    def feed_down(self, r, j=None):
        cols = slice(None) if j is None else slice(j * down_columns, (j + 1) * down_columns)
        total = self.res[r, :, cols]
        for t in range(self.ff_tiles):
            hid = self.act[self.at.hid + t * self.rows + r]
            total = total + matmul_nn(hid, self.weight_down(t, cols))
        self.res[r, :, cols] = total

    def feed_back(self, r):
        at = self.at
        grad = self.act[at.gdown + r]
        total = None
        for t in range(self.ff_tiles):
            dh = matmul_nt(grad, self.weight_down(t))
            pre = self.act[at.pre + t * self.rows + r].astype(F32)
            s = 1.0 / (1.0 + jnp.exp(-pre))
            dp = (dh * (s * (1.0 + pre * (1.0 - s)))).astype(BF16)
            self.act[at.pre + t * self.rows + r] = dp
            part = matmul_nt(dp, self.weight_up(t))
            total = part if total is None else total + part
        self.res[r] += total

    def self_back(self, r, step):
        at = self.at
        self.act[at.dout] = matmul_nt(self.weight(3), self.act[at.gout + r]).astype(BF16)
        step(0)
        q, k, v = (at.qkv + j * self.rows + r for j in range(3))

        def half(h):
            self.attend_back(q, k, v, at.att + r, at.dout, r, 2 * h, 2)
            for m in range(2):
                pl.when(h == m)(functools.partial(step, 1 + m))

        self.loop(HEADS // 4, half)
        total = self.res[r]
        for j in range(3):
            total = total + matmul_nt(self.act[at.qkv + j * self.rows + r], self.weight(j))
        self.act[at.stage + r] = total.astype(BF16)
        step(3)
        self.store(at.stage + r, self.grad_in, r, 2 + r).start()

    def both(self, slot):
        return self.act[pl.ds(slot, self.rows)].reshape(self.rows * TILE, TILE)

    def weight_grad(self, slot, left, right):
        self.act[slot] = matmul_tn(left, right).astype(BF16)

    def out_grad(self, k, left, right):
        total = matmul_nn(self.act[left], self.act[right])
        for r in range(1, self.rows):
            total = total + matmul_nn(self.act[left + r], self.act[right + r])
        self.act[self.tile_slot(k)] = total.astype(BF16)

    def down_grads(self, steps):
        at, rows = self.at, self.rows
        grad = self.both(at.gdown)
        base = steps.next
        steps.next += self.ff_tiles

        def part(t):
            slot = at.hid + t * rows
            self.weight_grad(slot, self.both(slot), grad)
            for n in range(self.ff_tiles):
                pl.when(t == n)(functools.partial(steps.run, base + n))

        self.loop(self.ff_tiles, part)

    def up_grads(self, x_slot):
        at, rows = self.at, self.rows
        x = self.both(x_slot)

        def part(t):
            slot = at.pre + t * rows
            self.weight_grad(slot, x, self.both(slot))

        self.loop(self.ff_tiles, part)

    def self_grads(self):
        at = self.at
        x = self.emb[...]

        def part(j):
            slot = at.qkv + j * self.rows
            self.weight_grad(slot, x, self.both(slot))

        self.loop(3, part)
        self.out_grad(self.t_out, at.att, at.gout)


    def store(self, slot, out, r, sem):
        return pltpu.make_async_copy(
            self.act.at[slot], out.at[self.row(r), :], self.local_sem.at[sem]
        )

    def spilled(self, r, back):
        a, b = self.probs.at[r], self.spill.at[r]
        return pltpu.make_async_copy(*((b, a) if back else (a, b)), self.local_sem.at[4 + r])

    def upstream(self, slot, r):
        return pltpu.make_async_copy(
            self.cot.at[self.row(r), :], self.act.at[slot], self.local_sem.at[6 + r]
        )

    def x_copy(self, slot, r, sem):
        ref = self.act.at[slot + r]
        return self.remote(ref, ref, self.x_send.at[sem + r], self.x_recv.at[sem + r], self.across)

    def length_copy(self):
        return self.remote(
            self.own_len, self.src_len, self.x_send.at[4], self.x_recv.at[4], self.across
        )

    def shard_copy(self):
        return self.remote(
            self.w_cross, self.x_shard, self.x_send.at[5], self.x_recv.at[5], self.across
        )


    def run(self):
        rows_in = pltpu.make_async_copy(self.emb_in, self.emb, self.emb_sem.at[0])
        rows_in.start()
        self.gacc[...] = jnp.zeros(self.gacc.shape, F32)
        self.own_len[...] = jnp.zeros(self.own_len.shape, jnp.int32)
        self.own_len[pl.ds(0, self.rows), pl.ds(0, self.lengths.shape[1])] = self.lengths[...]
        self.barrier()
        rows_in.wait()

        @pl.when(self.sec == 0)
        def first():
            self.encoding = True
            self.encoder()

        @pl.when(self.sec == 1)
        def second():
            self.encoding = False
            self.decoder()

    def encoder(self):
        at, rows = self.at, self.rows
        self.length_copy().start()
        for r in range(rows):
            self.upstream(at.cq + r, r).start()
        steps = Steps()
        if self.inner:
            self.shard_copy().start()
            steps = self.gather_steps([0, 1, 2, 3] + self.feed_chunks)
            steps.until(9)
        self.self_forward(False, steps)
        base = max(steps.next, 10)
        steps.until(base)

        def up(t):
            for n in range(1, self.ff_tiles):
                if base <= 9 + n:
                    pl.when(t == n)(functools.partial(steps.run, 9 + n))
            for r in range(rows):
                self.feed_up(at.first + r, r, t)

        steps.next = max(base, 9 + self.ff_tiles)
        self.loop(self.ff_tiles, up)
        last = self.down_bands - 1
        for j in range(last):
            steps.until(10 + self.ff_tiles + j)
            self.loop(rows, functools.partial(self.feed_down, j=j))
        steps.finish()

        def send(r):
            self.feed_down(r, last)

            def block(b):
                second = self.norm(self.res[r, b], 1, r, b)
                self.act[at.mem + r, b] = self.norm(second, 2, r, b).astype(BF16)

            self.blocks(block)
            pl.when(r > 0)(lambda: self.x_copy(at.mem, r - 1, 0).wait_send())
            self.x_copy(at.mem, r, 0).start()
            self.store(at.mem + r, self.result, r, r).start()

        self.loop(rows, send)
        steps = Steps()
        if self.inner:
            feed = list(range(self.t_down, self.t_all)) + list(range(self.t_up, self.t_down))
            steps = self.reduce_steps(feed + [4, 5, 3, 0, 1, 2])

        def back(r):
            self.x_copy(at.gmem, r, 2).wait_recv()
            self.upstream(at.cq + r, r).wait()

            def block(b):
                up = self.act[at.cq + r, b]
                grad = up.astype(F32) + self.act[at.gmem + r, b].astype(F32)
                grad = self.norm_back(self.norm_back(grad, 2, r, b), 1, r, b)
                self.res[r, b] = grad
                self.act[at.gdown + r, b] = grad.astype(BF16)

            self.blocks(block)

            @pl.when(r == rows - 1)
            def down():
                self.down_grads(steps)

            self.feed_back(r)

            def block(b):
                grad = self.norm_back(self.res[r, b], 0, r, b)
                self.res[r, b] = grad
                self.act[at.gout + r, b] = grad.astype(BF16)

            self.blocks(block)

            @pl.when(r == rows - 1)
            def up():
                self.up_grads(at.first)
                steps.more(1)

            base = steps.next
            steps.next += 4

            def step(n):
                pl.when(r == rows - 1)(functools.partial(steps.run, base + n))

            self.self_back(r, step)

        self.loop(rows, back)
        small = Steps()
        if self.inner:
            small = self.small_steps()
            small.more(1)
        self.self_grads()
        small.more(1)
        steps.more(2)
        small.more(1)
        steps.finish()
        small.finish()
        self.length_copy().wait_send()
        if self.inner:
            self.shard_copy().wait_send()
            self.drain()
        self.x_copy(at.mem, rows - 1, 0).wait_send()
        for r in range(rows):
            self.store(at.mem + r, self.result, r, r).wait()
            self.store(at.stage + r, self.grad_in, r, 2 + r).wait()
        if not self.inner:
            self.keep_grads()

    def reduce_steps(self, tiles):
        stages = [(0, self.reduce1), (2, self.reduce2), (4, self.reduce3), (6, self.reduce4)]
        stages += [(8, self.reduce5), (10, self.reduce6), (11, self.reduce7)]
        return Steps(self, tiles, stages)

    def keep_grads(self):
        tiles = list(range(self.t_all))
        if self.encoding:
            tiles = [k for k in tiles if not self.from_partner(k)]
        else:
            tiles += [self.t_mem, self.t_mem + 1]
        copies = [
            pltpu.make_async_copy(
                self.act.at[self.tile_slot(k)], self.whole_grad(k), self.grad_sem.at[k]
            )
            for k in tiles
        ]
        for copy in copies:
            copy.start()
        for copy in copies:
            copy.wait()
        for j in range(3):
            self.g_gain[pl.ds(j, 1), :] = jnp.sum(self.gacc[j], axis=0, keepdims=True)
            self.g_bias[pl.ds(j, 1), :] = jnp.sum(self.gacc[3 + j], axis=0, keepdims=True)

    def decoder(self):
        at, rows = self.at, self.rows
        for r in range(rows):
            self.upstream(at.gcross + r, r).start()
        steps = Steps()
        if self.inner:
            steps = self.gather_steps(list(range(8)) + self.feed_chunks)
            self.shard_copy().wait_recv()
            steps.until(9)
        self.self_forward(True, steps)
        steps.until(13)

        def ask(r):
            queries = matmul_nn(self.act[at.first + r], self.weight(4)) * query_scale
            self.act[at.cq + r] = queries.astype(BF16)

        self.loop(rows, ask)
        steps.finish()
        self.length_copy().wait_recv()

        def middle(r):
            self.fill_mask(r, self.src_len, False)
            self.spilled(r, False).wait()
            self.x_copy(at.mem, r, 0).wait_recv()
            for j in range(2):
                self.act[at.kv + j * rows + r] = matmul_nn(
                    self.act[at.mem + r], self.weight(self.w_memory_at + j)
                ).astype(BF16)
            k, v = at.kv + r, at.kv + rows + r
            self.attend(at.cq + r, k, v, at.oc + r, r)
            self.res[r] += matmul_tn(self.act[at.oc + r], self.weight(5))

            def block(b):
                out = self.norm(self.res[r, b], 1, r, b)
                self.res[r, b] = out
                self.act[at.second + r, b] = out.astype(BF16)

            self.blocks(block)
            for t in range(self.ff_tiles):
                self.feed_up(at.second + r, r, t)
            self.feed_down(r)
            self.upstream(at.gcross + r, r).wait()

            def block(b):
                out = self.norm(self.res[r, b], 2, r, b)
                self.act[at.stage + r, b] = out.astype(BF16)
                up = self.act[at.gcross + r, b]
                grad = self.norm_back(up.astype(F32), 2, r, b)
                self.res[r, b] = grad
                self.act[at.gdown + r, b] = grad.astype(BF16)

            self.blocks(block)
            self.store(at.stage + r, self.result, r, r).start()
            self.feed_back(r)

            def block(b):
                grad = self.norm_back(self.res[r, b], 1, r, b)
                self.res[r, b] = grad
                self.act[at.gcross + r, b] = grad.astype(BF16)

            self.blocks(block)
            self.act[at.dout] = matmul_nt(self.weight(5), self.act[at.gcross + r]).astype(BF16)
            self.attend_back(at.cq + r, k, v, at.oc + r, at.dout, r)
            total = matmul_nt(self.act[k], self.weight(self.w_memory_at))
            total = total + matmul_nt(self.act[v], self.weight(self.w_memory_at + 1))
            self.act[at.gmem + r] = total.astype(BF16)
            self.x_copy(at.gmem, r, 2).start()
            self.spilled(r, True).start()
            self.res[r] += matmul_nt(self.act[at.cq + r], self.weight(4))

            def block(b):
                grad = self.norm_back(self.res[r, b], 0, r, b)
                self.res[r, b] = grad
                self.act[at.gout + r, b] = grad.astype(BF16)

            self.blocks(block)

        self.loop(rows, middle)
        steps, small = Steps(), Steps()
        x = self.both(at.mem)

        def memory_grad(j):
            slot = at.kv + j * rows
            self.weight_grad(slot, x, self.both(slot))

        self.loop(2, memory_grad)
        if self.inner:
            feed = list(range(self.t_down, self.t_all)) + list(range(self.t_up, self.t_down))
            steps = self.reduce_steps([self.t_mem, self.t_mem + 1] + feed + [4, 5, 3, 0, 1, 2])
            small = self.small_steps()
        steps.more(2)
        self.down_grads(steps)
        small.more(1)
        self.up_grads(at.second)
        steps.more(1)
        self.weight_grad(at.cq, self.both(at.first), self.both(at.cq))
        self.out_grad(self.t_cross + 1, at.oc, at.gcross)
        base = steps.next
        steps.next += 2 * rows

        def back(r):
            self.spilled(r, True).wait()
            self.store(at.stage + r, self.result, r, r).wait()

            def step(n):
                if n % 2 == 0:
                    for m in range(rows):
                        pl.when(r == m)(functools.partial(steps.run, base + 2 * m + n // 2))

            self.self_back(r, step)

        self.loop(rows, back)
        small.more(1)
        self.self_grads()
        small.more(1)
        steps.finish()
        small.finish()
        if self.inner:
            self.drain()
        for r in range(rows):
            self.x_copy(at.gmem, r, 2).wait_send()
            self.store(at.stage + r, self.grad_in, r, 2 + r).wait()
        if not self.inner:
            self.keep_grads()


def both_layers(inner, dp, call, emb, cot, lengths, gain, bias, weights):
    rows = lengths.shape[0]
    model = emb.shape[1]
    ff_tiles = weights[3].shape[1] // TILE
    tiles = 6 + 2 * ff_tiles
    sums = tiles + 2
    vmem = pl.BlockSpec(memory_space=pltpu.VMEM)
    anywhere = pl.BlockSpec(memory_space=pl.ANY)
    dma = pltpu.SemaphoreType.DMA
    square = (TILE, TILE)
    scratch = [
        pltpu.VMEM(emb.shape, BF16),
        dma((1,)),
        pltpu.VMEM((Slots(rows, ff_tiles).count,) + square, BF16),
        pltpu.VMEM((rows, HEADS) + square, BF16),
        pltpu.VMEM((rows,) + square, F32),
        pltpu.VMEM(square, F32),
        pltpu.VMEM((rows, TILE, 128), F32),
        pltpu.VMEM((6, 8, model), F32),
        pltpu.VMEM((8, 128), jnp.int32),
        pltpu.VMEM((8, 128), jnp.int32),
        dma((8,)),
        dma((8,)),
        dma((8,)),
    ]
    if inner:
        part = TILE // 16
        chunks = 8 + ff_tiles + TILE // down_columns
        scratch += [
            pltpu.VMEM((8 + ff_tiles, LINE, 2, 2, part, TILE), BF16),
            pltpu.VMEM((LINE, 2, 2, weights[4].shape[0], TILE), BF16),
            pltpu.VMEM((part, 2 * TILE), BF16),
            pltpu.VMEM((2, part, TILE), BF16),
            pltpu.VMEM((sums, TILE // 2, TILE), BF16),
            pltpu.VMEM((sums, TILE // 4, TILE), BF16),
            pltpu.VMEM((sums, LINE - 1, part, TILE), BF16),
            pltpu.VMEM((3, 8, model), F32),
            pltpu.VMEM((2 + LINE, 8, model), F32),
        ]
        line = (LINE - 1,)
        scratch += [dma((chunks,))] + [dma((chunks,) + line)] * 2 + [dma((chunks,))] * 4
        scratch += [dma((sums,))] * 4 + [dma((sums,) + line)] * 4
        scratch += [dma((sums,))] * 4 + [dma((sums,)), dma((2 + LINE,)), dma((2 + LINE,))]
    else:
        scratch += [dma((sums,))]

    hidden = ff_tiles * TILE
    grads = [(model, 3 * TILE), square, (model, 2 * TILE), (model, hidden), (hidden, model)]
    if not inner:
        grads += [(model, 2 * TILE)]

    def kernel(*refs):
        Body(inner, rows, dp, ff_tiles, refs).run()

    return pl.pallas_call(
        kernel,
        out_shape=(
            jax.ShapeDtypeStruct(emb.shape, BF16),
            jax.ShapeDtypeStruct(emb.shape, BF16),
            *(jax.ShapeDtypeStruct(shape, BF16) for shape in grads),
            jax.ShapeDtypeStruct(gain.shape, F32),
            jax.ShapeDtypeStruct(bias.shape, F32),
            jax.ShapeDtypeStruct((rows, HEADS) + square, BF16),
        ),
        in_specs=[anywhere] * 2 + [vmem] * 3 + [anywhere if inner else vmem] * len(weights),
        out_specs=(anywhere,) * (2 + len(grads)) + (vmem, vmem, anywhere),
        scratch_shapes=scratch,
        compiler_params=pltpu.CompilerParams(
            collective_id=call, has_side_effects=True, vmem_limit_bytes=62 * 2**20
        ),
        name="layers",
    )(emb, cot, lengths, gain, bias, *weights)


def passed_along(shard, axis, by):
    count = lax.axis_size(axis)
    pairs = [(i, i + by) for i in range(count) if 0 <= i + by < count]
    return lax.ppermute(shard, axis, pairs)


def local(
    embedded,
    lengths,
    cotangent,
    attn_in,
    attn_out,
    cross_weight,
    up_weight,
    down_weight,
    norm_gain,
    norm_bias,
):
    dp = lax.axis_size("dp")
    rows = lengths.shape[1]
    shards = tuple(w[0] for w in (attn_in, attn_out, cross_weight, up_weight, down_weight))
    inner = dp == 4 * LINE and rows <= CALL_ROWS
    args = (embedded[0], cotangent[0], lengths[0], norm_gain[0], norm_bias[0])
    if inner:
        result, grad_in, *grads, gain, bias, spill = both_layers(inner, dp, 0, *args, shards)
        grads = [grad.astype(F32) for grad in grads]
    else:
        weights = tuple(lax.all_gather(w, "dp", axis=0, tiled=True) for w in shards)
        weights += (passed_along(weights[2], "section", 1),)
        parts = []
        for call in range(0, rows, CALL_ROWS):
            span = slice(call * TILE, min(rows, call + CALL_ROWS) * TILE)
            lens = args[2][call : call + CALL_ROWS]
            parts.append(
                both_layers(
                    inner, dp, call // CALL_ROWS, args[0][span], args[1][span], lens, *args[3:], weights
                )
            )
        result = jnp.concatenate([part[0] for part in parts], axis=0)
        grad_in = jnp.concatenate([part[1] for part in parts], axis=0)
        sums = [sum(part[n].astype(F32) for part in parts) for n in range(2, 10)]
        *grads, memory, gain, bias = lax.psum(tuple(sums), "dp")
        is_first = lax.axis_index("section") == 0
        grads[2] = jnp.where(is_first, passed_along(memory, "section", -1), grads[2])
    return tuple(out[None] for out in (result, grad_in, *grads, gain, bias))


def solution(mesh):
    rows = P("section", "dp", None)
    whole = P("section", None, None)
    in_specs = (rows,) * 8 + (whole,) * 2
    out_specs = (rows,) * 2 + (whole,) * 7
    return jax.shard_map(local, mesh=mesh, in_specs=in_specs, out_specs=out_specs, check_vma=False)
```

```python
import functools

import jax
import jax.numpy as jnp
from jax import lax
from jax.experimental import pallas as pl
from jax.experimental.pallas import tpu as pltpu
from jax.sharding import PartitionSpec as P

HEADS = 8

norm_eps = 1e-06
masked_score = -1e30
F32 = jnp.float32
BF16 = jnp.bfloat16
MESH = pl.DeviceIdType.MESH
far_count = 1
down_columns = 128
query_scale = 0.125
LINE = 4
CALL_ROWS = 2
TILE = 512


def matmul_nn(left, right):
    return jnp.dot(left, right, preferred_element_type=F32)


def matmul_tn(left, right):
    return lax.dot_general(left, right, (((0,), (0,)), ((), ())), preferred_element_type=F32)


def matmul_nt(left, right):
    return lax.dot_general(left, right, (((1,), (1,)), ((), ())), preferred_element_type=F32)


class Steps:
    def __init__(self, body=None, items=(), stages=()):
        self.body = body
        self.items = items
        self.stages = stages
        self.count = len(items) + stages[-1][0] if items else 0
        self.next = 0

    def run(self, n):
        if n >= self.count:
            return
        for offset, act in reversed(self.stages):
            if 0 <= n - offset < len(self.items):
                item = self.items[n - offset]
                act(item)
                self.body.done.append((act, item))

    def until(self, n):
        while self.next < n:
            self.run(self.next)
            self.next += 1

    def more(self, n):
        self.until(self.next + n)

    def finish(self):
        self.until(self.count)


class Slots:
    def __init__(self, rows, ff_tiles):
        self.rows = rows
        self.count = 0
        self.qkv = self.take(3 * rows)
        self.cq = self.take(rows)
        self.kv = self.take(2 * rows)
        self.pre = self.take(ff_tiles * rows)
        self.hid = self.take(ff_tiles * rows)
        self.att = self.take(rows)
        self.oc = self.take(rows)
        self.first = self.take(rows)
        self.second = self.take(rows)
        self.mem = self.take(rows)
        self.gmem = self.take(rows)
        self.gdown = self.take(rows)
        self.gout = self.take(rows)
        self.gcross = self.take(rows)
        self.stage = self.take(rows)
        self.dout = self.take(1)
        self.xhat = self.take(3 * rows)

    def take(self, n):
        at = self.count
        self.count += n
        return at


class Body:
    def __init__(self, inner, rows, dp, ff_tiles, refs):
        self.inner = inner
        self.rows = rows
        self.ff_tiles = ff_tiles
        self.at = Slots(rows, ff_tiles)
        names = ["emb_in", "cot", "lengths", "gain", "bias"]
        names += ["w_in", "w_out", "w_cross", "w_up", "w_down"]
        if not inner:
            names += ["w_memory"]
        names += ["result", "grad_in", "g_in", "g_out", "g_cross", "g_up", "g_down"]
        if not inner:
            names += ["g_memory"]
        names += ["g_gain", "g_bias", "spill"]
        names += ["emb", "emb_sem", "act", "probs", "res", "mask", "rstd", "gacc", "own_len", "src_len"]
        names += ["local_sem", "x_send", "x_recv"]
        if not inner:
            names += ["grad_sem"]
        if inner:
            names += ["wt", "wd", "x_shard", "x_grad", "r1", "r2", "r3", "gbuf", "grcv"]
            names += ["gown_sem", "gz_s", "gz_r", "gy_s", "gy_r", "gc_s", "gc_r"]
            names += ["a1_s", "a1_r", "a2_s", "a2_r", "a3_s", "a3_r"]
            names += ["away", "far", "fown_sem", "fa_s", "fa_r", "fz_s", "fz_r"]
            names += ["fy_s", "fy_r", "fx_s", "fx_r", "a4_s", "a4_r", "a5_s", "a5_r"]
            names += ["a6_s", "a6_r", "own_sem", "gs_s", "gs_r"]
        assert len(names) == len(refs), (len(names), len(refs))
        for name, ref in zip(names, refs):
            setattr(self, name, ref)
        self.sec = lax.axis_index("section")
        self.i = lax.axis_index("dp")
        self.across = (1 - self.sec, self.i)
        if inner:
            self.c = lax.rem(self.i, 2)
            self.y = lax.rem(self.i // 2, 2)
            self.z = self.i // 4
            self.core_dev = (self.sec, self.z * 4 + self.y * 2 + (1 - self.c))
            self.y_dev = (self.sec, self.z * 4 + (1 - self.y) * 2 + self.c)
            self.z_other = [lax.rem(self.z + d, LINE) for d in range(1, LINE)]
            self.z_dev = [(self.sec, zz * 4 + self.y * 2 + self.c) for zz in self.z_other]
        self.done = []
        self.draining = False
        self.encoding = True
        self.t_in = 0
        self.t_out = 3
        self.t_cross = 4
        self.t_up = 6
        self.t_down = 6 + ff_tiles
        self.t_all = 6 + 2 * ff_tiles
        self.t_mem = self.t_all
        self.w_memory_at = 6
        self.w_up_at = 8
        self.down_bands = TILE // down_columns
        self.far_at = self.w_up_at + ff_tiles + self.down_bands - far_count
        self.far_shift = far_count
        self.far_chunks = [self.far_at + self.far_shift + n for n in range(far_count)]
        self.feed_chunks = [self.w_up_at + n for n in range(ff_tiles + self.down_bands)]


    def remote(self, src, dst, send, recv, dev):
        return pltpu.make_async_remote_copy(
            src_ref=src, dst_ref=dst, send_sem=send, recv_sem=recv, device_id=dev, device_id_type=MESH
        )

    def send(self, src, dst, send, recv, dev):
        copy = self.remote(src, dst, send, recv, dev)
        if self.draining:
            copy.wait_send()
        else:
            copy.start()

    def drain(self):
        self.draining = True
        for act, item in self.done:
            act(item)
        self.draining = False
        self.done = []

    def barrier(self):
        sem = pltpu.get_barrier_semaphore()
        devs = [self.across]
        if self.inner:
            devs += [self.core_dev, self.y_dev] + self.z_dev
        for dev in devs:
            pl.semaphore_signal(sem, inc=1, device_id=dev, device_id_type=MESH)
        pl.semaphore_wait(sem, len(devs))


    def weight(self, k):
        if self.inner:
            return self.wt[k].reshape(TILE, TILE)
        if k < 3:
            return self.w_in[:, k * TILE : (k + 1) * TILE]
        if k == 3:
            return self.w_out[...]
        if k < 6:
            return self.w_cross[:, (k - 4) * TILE : (k - 3) * TILE]
        if k < 8:
            return self.w_memory[:, (k - 6) * TILE : (k - 5) * TILE]
        return self.w_up[:, (k - 8) * TILE : (k - 7) * TILE]

    def weight_up(self, t):
        if self.inner:
            return self.wt[self.w_up_at + t].reshape(TILE, TILE)
        start = t * TILE
        return self.w_up[:, pl.ds(start if isinstance(start, int) else pl.multiple_of(start, TILE), TILE)]

    def weight_down(self, t):
        if self.inner:
            return self.wd[t].reshape(TILE, TILE)
        return self.w_down[t * TILE : (t + 1) * TILE, :]

    def chunk_source(self, k):
        z, y, c = self.z, self.y, self.c
        down_at = self.w_up_at + self.ff_tiles
        if k < 3:
            src = self.w_in.at[:, pl.ds(k * TILE, TILE)]
        elif k == 3:
            src = self.w_out.at[...]
        elif k < 6:
            src = self.w_cross.at[:, pl.ds((k - 4) * TILE, TILE)]
        elif k < 8:
            src = self.x_shard.at[:, pl.ds((k - 6) * TILE, TILE)]
        elif k < down_at:
            src = self.w_up.at[:, pl.ds((k - 8) * TILE, TILE)]
        else:
            cols = pl.ds((k - down_at) * down_columns, down_columns)
            src = self.w_down.at[:, cols]
        if k < down_at:
            whole = self.wt.at[k]
            own = whole.at[z, y, c]
            line = whole.at[:, y, c]
            plane = whole.at[:, :, c]
        else:
            own = self.wd.at[z, y, c, :, cols]
            line = self.wd.at[:, y, c, :, cols]
            plane = self.wd.at[:, :, c, :, cols]
        return src, own, line, plane

    def gather1(self, k):
        if self.is_far(k):
            return self.far1(k)
        src, own, line, plane = self.chunk_source(k)
        if not self.draining:
            pltpu.make_async_copy(src, own, self.gown_sem.at[k]).start()
        for d in range(LINE - 1):
            self.send(src, own, self.gz_s.at[k, d], self.gz_r.at[k, d], self.z_dev[d])

    def gather2(self, k):
        if self.is_far(k):
            return self.far2(k)
        src, own, line, plane = self.chunk_source(k)
        if not self.draining:
            pltpu.make_async_copy(src, own, self.gown_sem.at[k]).wait()
        for d in range(0 if self.draining else LINE - 1):
            self.remote(src, own, self.gz_s.at[k, d], self.gz_r.at[k, d], self.z_dev[d]).wait_recv()
        self.send(line, line, self.gy_s.at[k], self.gy_r.at[k], self.y_dev)

    def gather3(self, k):
        if self.is_far(k) and not self.encoding:
            return self.far3(k)
        src, own, line, plane = self.chunk_source(k)
        if not self.draining:
            if self.is_far(k):
                n = k - self.far_at
                self.remote(plane, plane, self.fx_s.at[n], self.fx_r.at[n], self.across).wait_recv()
            else:
                self.remote(line, line, self.gy_s.at[k], self.gy_r.at[k], self.y_dev).wait_recv()
        self.send(plane, plane, self.gc_s.at[k], self.gc_r.at[k], self.core_dev)

    def gather4(self, k):
        if self.is_far(k) and not self.encoding:
            return
        src, own, line, plane = self.chunk_source(k)
        if not self.draining:
            self.remote(plane, plane, self.gc_s.at[k], self.gc_r.at[k], self.core_dev).wait_recv()


    def is_far(self, k):
        return k >= self.far_at + (0 if self.encoding else self.far_shift)

    def far_copy(self, n):
        cols = pl.ds((self.down_bands - far_count + n) * down_columns, down_columns)
        return self.remote(
            self.w_down.at[:, cols], self.away.at[n], self.fa_s.at[n], self.fa_r.at[n], self.across
        )

    def far1(self, k):
        if self.encoding:
            return
        n = k - self.far_at - self.far_shift
        src, own = self.away.at[n], self.far.at[n, self.z, self.y]
        if not self.draining:
            self.far_copy(n).wait_recv()
            pltpu.make_async_copy(src, own, self.fown_sem.at[n]).start()
        for d in range(LINE - 1):
            self.send(src, own, self.fz_s.at[n, d], self.fz_r.at[n, d], self.z_dev[d])

    def far2(self, k):
        if self.encoding:
            return
        n = k - self.far_at - self.far_shift
        src, own, line = self.away.at[n], self.far.at[n, self.z, self.y], self.far.at[n, :, self.y]
        if not self.draining:
            pltpu.make_async_copy(src, own, self.fown_sem.at[n]).wait()
            for d in range(LINE - 1):
                self.remote(
                    src, own, self.fz_s.at[n, d], self.fz_r.at[n, d], self.z_dev[d]
                ).wait_recv()
        self.send(line, line, self.fy_s.at[n], self.fy_r.at[n], self.y_dev)

    def far3(self, k):
        n = k - self.far_at - self.far_shift
        line = self.far.at[n, :, self.y]
        if not self.draining:
            self.remote(line, line, self.fy_s.at[n], self.fy_r.at[n], self.y_dev).wait_recv()
        src, own, near, plane = self.chunk_source(self.far_at + n)
        self.send(self.far.at[n], plane, self.fx_s.at[n], self.fx_r.at[n], self.across)

    def gather_steps(self, chunks):
        stages = [(0, self.gather1), (2, self.gather2), (4, self.gather3), (5, self.gather4)]
        return Steps(self, chunks, stages)


    def tile_slot(self, k):
        at, rows = self.at, self.rows
        if k < 3:
            return at.qkv + k * rows
        if k == 3:
            return at.gout
        if k == 4:
            return at.cq
        if k == 5:
            return at.gcross
        if k < self.t_down:
            return at.pre + (k - self.t_up) * rows
        if k < self.t_all:
            return at.hid + (k - self.t_down) * rows
        return at.kv + (k - self.t_mem) * rows

    def whole_grad(self, k, start=0, size=TILE):
        rows = pl.ds(start, size)

        def columns(ref, n):
            return ref.at[rows, pl.ds(n * TILE, TILE)]

        if k < 3:
            return columns(self.g_in, k)
        if k == 3:
            return columns(self.g_out, 0)
        if k < 6:
            return columns(self.g_cross, k - self.t_cross)
        if k < self.t_down:
            return columns(self.g_up, k - self.t_up)
        if k < self.t_all:
            return self.g_down.at[pl.ds((k - self.t_down) * TILE + start, size), :]
        return columns(self.g_memory, k - self.t_mem)

    def from_partner(self, k):
        return self.encoding and k in (self.t_cross, self.t_cross + 1)

    def block_at(self, c, y=0, z=0):
        return c * (TILE // 2) + y * (TILE // 4) + z * (TILE // 16)

    def reduce1(self, k):
        if self.from_partner(k):
            return
        slot = self.tile_slot(k)
        half = TILE // 2
        src = self.act.at[slot, pl.ds(self.block_at(1 - self.c), half)]
        self.send(src, self.r1.at[k], self.a1_s.at[k], self.a1_r.at[k], self.core_dev)

    def reduce2(self, k):
        if self.from_partner(k):
            return
        slot = self.tile_slot(k)
        half, quarter = TILE // 2, TILE // 4
        own = pl.ds(pl.multiple_of(self.block_at(self.c), half), half)
        src = self.act.at[slot, own]
        if not self.draining:
            self.remote(
                src, self.r1.at[k], self.a1_s.at[k], self.a1_r.at[k], self.core_dev
            ).wait_recv()
            total = self.act[slot, own].astype(F32) + self.r1[k].astype(F32)
            self.act[slot, own] = total.astype(BF16)
        src = self.act.at[slot, pl.ds(self.block_at(self.c, 1 - self.y), quarter)]
        self.send(src, self.r2.at[k], self.a2_s.at[k], self.a2_r.at[k], self.y_dev)

    def reduce3(self, k):
        if self.from_partner(k):
            return
        slot = self.tile_slot(k)
        quarter, part = TILE // 4, TILE // 16
        own = pl.ds(pl.multiple_of(self.block_at(self.c, self.y), quarter), quarter)
        src = self.act.at[slot, own]
        if not self.draining:
            self.remote(
                src, self.r2.at[k], self.a2_s.at[k], self.a2_r.at[k], self.y_dev
            ).wait_recv()
            total = self.act[slot, own].astype(F32) + self.r2[k].astype(F32)
            self.act[slot, own] = total.astype(BF16)
        for d in range(LINE - 1):
            src = self.act.at[slot, pl.ds(self.block_at(self.c, self.y, self.z_other[d]), part)]
            self.send(src, self.r3.at[k, d], self.a3_s.at[k, d], self.a3_r.at[k, d], self.z_dev[d])

    def reduce4(self, k):
        if self.from_partner(k):
            return self.reduce4_memory(k)
        slot = self.tile_slot(k)
        part = TILE // 16
        own = pl.ds(pl.multiple_of(self.block_at(self.c, self.y, self.z), part), part)
        src = self.act.at[slot, own]
        if not self.draining:
            total = self.act[slot, own].astype(F32)
            for d in range(LINE - 1):
                self.remote(
                    src, self.r3.at[k, d], self.a3_s.at[k, d], self.a3_r.at[k, d], self.z_dev[d]
                ).wait_recv()
                total = total + self.r3[k, d].astype(F32)
            self.act[slot, own] = total.astype(BF16)
        if k < self.t_all:
            self.spread(k, src)
        else:
            j = k - self.t_mem
            dst = self.x_grad.at[j]
            self.send(src, dst, self.x_send.at[6 + j], self.x_recv.at[6 + j], self.across)

    def spread(self, k, src):
        part = TILE // 16
        dst = self.whole_grad(k, self.block_at(self.c, self.y, self.z), part)
        if not self.draining:
            pltpu.make_async_copy(src, dst, self.own_sem.at[k]).start()
        for d in range(LINE - 1):
            self.send(src, dst, self.a4_s.at[k, d], self.a4_r.at[k, d], self.z_dev[d])

    def reduce4_memory(self, k):
        j = k - self.t_cross
        src = self.x_grad.at[j]
        if not self.draining:
            self.remote(
                src, src, self.x_send.at[6 + j], self.x_recv.at[6 + j], self.across
            ).wait_recv()
        self.spread(k, src)

    def reduce5(self, k):
        if k >= self.t_all:
            return
        quarter, part = TILE // 4, TILE // 16
        own = self.whole_grad(k, self.block_at(self.c, self.y, self.z), part)
        if not self.draining:
            pltpu.make_async_copy(own, own, self.own_sem.at[k]).wait()
        for d in range(0 if self.draining else LINE - 1):
            self.remote(
                own, own, self.a4_s.at[k, d], self.a4_r.at[k, d], self.z_dev[d]
            ).wait_recv()
        line = self.whole_grad(k, self.block_at(self.c, self.y), quarter)
        self.send(line, line, self.a5_s.at[k], self.a5_r.at[k], self.y_dev)

    def reduce6(self, k):
        if k >= self.t_all:
            return
        half, quarter = TILE // 2, TILE // 4
        line = self.whole_grad(k, self.block_at(self.c, self.y), quarter)
        if not self.draining:
            self.remote(line, line, self.a5_s.at[k], self.a5_r.at[k], self.y_dev).wait_recv()
        plane = self.whole_grad(k, self.block_at(self.c), half)
        self.send(plane, plane, self.a6_s.at[k], self.a6_r.at[k], self.core_dev)

    def reduce7(self, k):
        if k >= self.t_all:
            return
        plane = self.whole_grad(k, self.block_at(self.c), TILE // 2)
        if not self.draining:
            self.remote(plane, plane, self.a6_s.at[k], self.a6_r.at[k], self.core_dev).wait_recv()

    def small_steps(self):
        stages = [(0, self.small1), (1, self.small2), (2, self.small3), (3, self.small4)]
        return Steps(self, [0], stages)

    def small1(self, item):
        if not self.draining:
            for j in range(6):
                self.gbuf[0, pl.ds(j, 1), :] = jnp.sum(self.gacc[j], axis=0, keepdims=True)
            self.gbuf[0, pl.ds(6, 2), :] = jnp.zeros((2, TILE), F32)
        self.send(self.gbuf.at[0], self.grcv.at[0], self.gs_s.at[0], self.gs_r.at[0], self.core_dev)

    def small2(self, item):
        if not self.draining:
            self.remote(
                self.gbuf.at[0], self.grcv.at[0], self.gs_s.at[0], self.gs_r.at[0], self.core_dev
            ).wait_recv()
            self.gbuf[1] = self.gbuf[0] + self.grcv[0]
        self.send(self.gbuf.at[1], self.grcv.at[1], self.gs_s.at[1], self.gs_r.at[1], self.y_dev)

    def small3(self, item):
        if not self.draining:
            self.remote(
                self.gbuf.at[1], self.grcv.at[1], self.gs_s.at[1], self.gs_r.at[1], self.y_dev
            ).wait_recv()
            self.gbuf[2] = self.gbuf[1] + self.grcv[1]
        for d in range(LINE - 1):
            self.send(
                self.gbuf.at[2],
                self.grcv.at[2 + self.z],
                self.gs_s.at[2 + d],
                self.gs_r.at[2 + d],
                self.z_dev[d],
            )
        if not self.draining:
            self.grcv[2 + self.z] = self.gbuf[2]

    def small4(self, item):
        if self.draining:
            return
        for d in range(LINE - 1):
            self.remote(
                self.gbuf.at[2],
                self.grcv.at[2 + self.z],
                self.gs_s.at[2 + d],
                self.gs_r.at[2 + d],
                self.z_dev[d],
            ).wait_recv()
        total = self.grcv[2]
        for n in range(1, LINE):
            total = total + self.grcv[2 + n]
        self.g_gain[...] = total[0:3]
        self.g_bias[...] = total[3:6]


    def fill_mask(self, r, key_len, causal):
        lane = lax.broadcasted_iota(jnp.int32, (8, 128), 1)
        sub = lax.broadcasted_iota(jnp.int32, (8, 128), 0)

        def ends_of(ref):
            spans = jnp.broadcast_to(ref[pl.ds(r, 1), :], (8, 128))
            return jnp.sum(jnp.where(lane <= sub, spans, 0).astype(F32), axis=1, keepdims=True)

        ends = ends_of(key_len)
        flat = jnp.sum(jnp.where(lane == sub, ends, 0.0), axis=0, keepdims=True)
        flat = jnp.where(lane[:1] < 8, flat, 1e9)
        pos = lax.broadcasted_iota(jnp.int32, (TILE, 128), 0).astype(F32)
        key_ids = jnp.sum(jnp.where(pos >= flat, 1.0, 0.0), axis=1, keepdims=True)
        query_ends = ends_of(self.own_len)
        pos = lax.broadcasted_iota(jnp.int32, (8, TILE), 1).astype(F32)
        query_ids = jnp.sum(jnp.where(pos >= query_ends, 1.0, 0.0), axis=0, keepdims=True)
        step = 128
        for b in range(TILE // step):
            allowed = key_ids[b * step : (b + 1) * step] == query_ids
            if causal:
                k_pos = lax.broadcasted_iota(jnp.int32, (step, TILE), 0) + b * step
                q_pos = lax.broadcasted_iota(jnp.int32, (step, TILE), 1)
                allowed = allowed & (k_pos <= q_pos)
            self.mask[b * step : (b + 1) * step, :] = jnp.where(allowed, 0.0, masked_score)


    def attend(self, q, k, v, out, r, first=0, count=HEADS // 2):
        act = self.act
        low = lax.broadcasted_iota(jnp.int32, (1, 128), 1) < 64

        def pair(n, carry):
            hp = first + n
            cols = pl.ds(pl.multiple_of(hp * 128, 128), 128)
            qs, ks, vs = act[q, :, cols], act[k, :, cols], act[v, :, cols]
            scores = []
            for j in range(2):
                qm = jnp.where(low if j == 0 else ~low, qs, jnp.zeros_like(qs))
                s = matmul_nt(ks, qm) + self.mask[...]
                scores.append((s, jnp.max(s, axis=0, keepdims=True)))
            weights = []
            for j, (s, top) in enumerate(scores):
                raised = jnp.exp(s - top)
                raised = raised * (1.0 / jnp.sum(raised, axis=0, keepdims=True))
                weights.append(raised.astype(BF16))
                self.probs[r, hp * 2 + j] = weights[j]
            for j, probs in enumerate(weights):
                o = matmul_tn(vs, probs)[64 * j : 64 * j + 64]
                rows = pl.ds(pl.multiple_of(hp * 128 + 64 * j, 64), 64)
                act[out, rows, :] = o.astype(BF16)
            return carry

        lax.fori_loop(0, count, pair, 0)

    def attend_back(self, q, k, v, out, dout, r, first=0, count=HEADS // 2):
        act = self.act
        low = lax.broadcasted_iota(jnp.int32, (1, 128), 1) < 64

        def pair(n, carry):
            hp = first + n
            cols = pl.ds(pl.multiple_of(hp * 128, 128), 128)
            qs, ks, vs = act[q, :, cols], act[k, :, cols], act[v, :, cols]
            grads = []
            for j in range(2):
                rows = pl.ds(pl.multiple_of(hp * 128 + 64 * j, 64), 64)
                do = act[dout, rows, :]
                prod = do.astype(F32) * act[out, rows, :].astype(F32)
                delta = jnp.sum(prod, axis=0, keepdims=True)
                none = jnp.zeros_like(do)
                do = jnp.concatenate([do, none] if j == 0 else [none, do], axis=0)
                grads.append((do, delta, matmul_nn(vs, do)))
            scores = []
            for j, (do, delta, dp) in enumerate(grads):
                probs = self.probs[r, hp * 2 + j]
                scores.append((probs, (probs.astype(F32) * (dp - delta)).astype(BF16)))
            dq, dk, dv = [], None, None
            for j, (probs, ds) in enumerate(scores):
                qm = jnp.where(low if j == 0 else ~low, qs, jnp.zeros_like(qs))
                a, b = matmul_nt(probs, grads[j][0]), matmul_nn(ds, qm)
                dv, dk = (a, b) if j == 0 else (dv + a, dk + b)
                dq.append(matmul_tn(ks, ds)[64 * j : 64 * j + 64])
            dq = (jnp.concatenate(dq, axis=0) * 0.125).astype(BF16)
            act[q, :, cols] = dq.T
            act[k, :, cols] = dk.astype(BF16)
            act[v, :, cols] = dv.astype(BF16)
            return carry

        lax.fori_loop(0, count, pair, 0)


    def blocks(self, body):
        step = 128

        def one(b, carry):
            body(pl.ds(pl.multiple_of(b * step, step), step))
            return carry

        lax.fori_loop(0, TILE // step, one, 0, unroll=True)

    def norm(self, values, n, r, rows):
        center = jnp.mean(values, axis=-1, keepdims=True)
        shifted = values - center
        scale = lax.rsqrt(jnp.mean(shifted * shifted, axis=-1, keepdims=True) + norm_eps)
        hat = shifted * scale
        self.act[self.at.xhat + n * self.rows + r, rows] = hat.astype(BF16)
        self.rstd[r, rows, pl.ds(n, 1)] = scale
        return hat * self.gain[pl.ds(n, 1), :] + self.bias[pl.ds(n, 1), :]

    def norm_back(self, grad, n, r, rows):
        hat = self.act[self.at.xhat + n * self.rows + r, rows].astype(F32)
        scale = self.rstd[r, rows, pl.ds(n, 1)]
        count = grad.shape[0] // 8
        self.gacc[n] += jnp.sum((grad * hat).reshape(count, 8, TILE), axis=0)
        self.gacc[3 + n] += jnp.sum(grad.reshape(count, 8, TILE), axis=0)
        up = grad * self.gain[pl.ds(n, 1), :]
        first = jnp.mean(up, axis=-1, keepdims=True)
        second = jnp.mean(up * hat, axis=-1, keepdims=True)
        return (up - first - hat * second) * scale


    def row(self, r):
        start = r * TILE
        return pl.ds(start if isinstance(start, int) else pl.multiple_of(start, TILE), TILE)

    def loop(self, count, body):
        def one(n, carry):
            body(n)
            return carry

        lax.fori_loop(0, count, one, 0)

    def self_in(self, r):
        x = self.emb[self.row(r), :]
        for j in range(3):
            rows = matmul_nn(x, self.weight(j))
            if j == 0:
                rows = rows * query_scale
            self.act[self.at.qkv + j * self.rows + r] = rows.astype(BF16)

    def self_forward(self, causal, steps):
        at, rows = self.at, self.rows
        base = steps.next
        steps.next += 3 * rows

        def one(r):
            self.self_in(r)
            for n in range(rows):
                pl.when(r == n)(functools.partial(steps.run, base + 3 * n))
            self.fill_mask(r, self.own_len, causal)
            q, k, v = (at.qkv + j * rows + r for j in range(3))

            def half(h):
                self.attend(q, k, v, at.att + r, r, 2 * h, 2)
                for n in range(rows):
                    for m in range(2):
                        pl.when((r == n) & (h == m))(
                            functools.partial(steps.run, base + 3 * n + 1 + m)
                        )

            self.loop(HEADS // 4, half)
            if not self.encoding:
                self.spilled(r, False).start()
            self.self_out(r)

        self.loop(rows, one)

    def self_out(self, r):
        at = self.at
        x = self.emb[self.row(r), :].astype(F32)
        self.res[r] = x + matmul_tn(self.act[at.att + r], self.weight(3))

        def block(rows):
            out = self.norm(self.res[r, rows], 0, r, rows)
            self.res[r, rows] = out
            self.act[at.first + r, rows] = out.astype(BF16)

        self.blocks(block)

    def feed_up(self, x_slot, r, t):
        at = self.at
        pre = matmul_nn(self.act[x_slot], self.weight_up(t))
        hid = (pre / (1.0 + jnp.exp(-pre))).astype(BF16)
        self.act[at.pre + t * self.rows + r] = pre.astype(BF16)
        self.act[at.hid + t * self.rows + r] = hid

    def feed_down(self, r):
        total = self.res[r]
        for t in range(self.ff_tiles):
            hid = self.act[self.at.hid + t * self.rows + r]
            total = total + matmul_nn(hid, self.weight_down(t))
        self.res[r] = total

    def feed_back(self, r):
        at = self.at
        grad = self.act[at.gdown + r]
        total = None
        for t in range(self.ff_tiles):
            dh = matmul_nt(grad, self.weight_down(t))
            pre = self.act[at.pre + t * self.rows + r].astype(F32)
            s = 1.0 / (1.0 + jnp.exp(-pre))
            dp = (dh * (s * (1.0 + pre * (1.0 - s)))).astype(BF16)
            self.act[at.pre + t * self.rows + r] = dp
            part = matmul_nt(dp, self.weight_up(t))
            total = part if total is None else total + part
        self.res[r] += total

    def self_back(self, r, step):
        at = self.at
        self.act[at.dout] = matmul_nt(self.weight(3), self.act[at.gout + r]).astype(BF16)
        step(0)
        q, k, v = (at.qkv + j * self.rows + r for j in range(3))

        def half(h):
            self.attend_back(q, k, v, at.att + r, at.dout, r, 2 * h, 2)
            for m in range(2):
                pl.when(h == m)(functools.partial(step, 1 + m))

        self.loop(HEADS // 4, half)
        total = self.res[r]
        for j in range(3):
            total = total + matmul_nt(self.act[at.qkv + j * self.rows + r], self.weight(j))
        self.act[at.stage + r] = total.astype(BF16)
        step(3)
        self.store(at.stage + r, self.grad_in, r, 2 + r).start()

    def both(self, slot):
        return self.act[pl.ds(slot, self.rows)].reshape(self.rows * TILE, TILE)

    def weight_grad(self, slot, left, right):
        self.act[slot] = matmul_tn(left, right).astype(BF16)

    def out_grad(self, k, left, right):
        total = matmul_nn(self.act[left], self.act[right])
        for r in range(1, self.rows):
            total = total + matmul_nn(self.act[left + r], self.act[right + r])
        self.act[self.tile_slot(k)] = total.astype(BF16)

    def down_grads(self, steps):
        at, rows = self.at, self.rows
        grad = self.both(at.gdown)
        base = steps.next
        steps.next += self.ff_tiles

        def part(t):
            slot = at.hid + t * rows
            self.weight_grad(slot, self.both(slot), grad)
            for n in range(self.ff_tiles):
                pl.when(t == n)(functools.partial(steps.run, base + n))

        self.loop(self.ff_tiles, part)

    def up_grads(self, x_slot):
        at, rows = self.at, self.rows
        x = self.both(x_slot)

        def part(t):
            slot = at.pre + t * rows
            self.weight_grad(slot, x, self.both(slot))

        self.loop(self.ff_tiles, part)

    def self_grads(self):
        at = self.at
        x = self.emb[...]

        def part(j):
            slot = at.qkv + j * self.rows
            self.weight_grad(slot, x, self.both(slot))

        self.loop(3, part)
        self.out_grad(self.t_out, at.att, at.gout)


    def store(self, slot, out, r, sem):
        return pltpu.make_async_copy(
            self.act.at[slot], out.at[self.row(r), :], self.local_sem.at[sem]
        )

    def spilled(self, r, back):
        a, b = self.probs.at[r], self.spill.at[r]
        return pltpu.make_async_copy(*((b, a) if back else (a, b)), self.local_sem.at[4 + r])

    def upstream(self, slot, r):
        return pltpu.make_async_copy(
            self.cot.at[self.row(r), :], self.act.at[slot], self.local_sem.at[6 + r]
        )

    def x_copy(self, slot, r, sem):
        ref = self.act.at[slot + r]
        return self.remote(ref, ref, self.x_send.at[sem + r], self.x_recv.at[sem + r], self.across)

    def length_copy(self):
        return self.remote(
            self.own_len, self.src_len, self.x_send.at[4], self.x_recv.at[4], self.across
        )

    def shard_copy(self):
        return self.remote(
            self.w_cross, self.x_shard, self.x_send.at[5], self.x_recv.at[5], self.across
        )


    def run(self):
        rows_in = pltpu.make_async_copy(self.emb_in, self.emb, self.emb_sem.at[0])
        rows_in.start()
        self.gacc[...] = jnp.zeros(self.gacc.shape, F32)
        self.own_len[...] = jnp.zeros(self.own_len.shape, jnp.int32)
        self.own_len[pl.ds(0, self.rows), pl.ds(0, self.lengths.shape[1])] = self.lengths[...]
        self.barrier()
        rows_in.wait()

        @pl.when(self.sec == 0)
        def first():
            self.encoding = True
            self.encoder()

        @pl.when(self.sec == 1)
        def second():
            self.encoding = False
            self.decoder()

    def encoder(self):
        at, rows = self.at, self.rows
        self.length_copy().start()
        for r in range(rows):
            self.upstream(at.cq + r, r).start()
        steps = Steps()
        if self.inner:
            self.shard_copy().start()
            for n in range(far_count):
                self.far_copy(n).start()
            steps = self.gather_steps([0, 1, 2, 3] + self.feed_chunks)
            steps.until(8)
        self.self_forward(False, steps)
        steps.finish()

        def send(r):
            for t in range(self.ff_tiles):
                self.feed_up(at.first + r, r, t)
            self.feed_down(r)

            def block(b):
                second = self.norm(self.res[r, b], 1, r, b)
                self.act[at.mem + r, b] = self.norm(second, 2, r, b).astype(BF16)

            self.blocks(block)
            pl.when(r > 0)(lambda: self.x_copy(at.mem, r - 1, 0).wait_send())
            self.x_copy(at.mem, r, 0).start()
            self.store(at.mem + r, self.result, r, r).start()

        self.loop(rows, send)
        steps = Steps()
        if self.inner:
            feed = list(range(self.t_down, self.t_all)) + list(range(self.t_up, self.t_down))
            steps = self.reduce_steps(feed + [4, 5, 3, 0, 1, 2])

        def back(r):
            self.x_copy(at.gmem, r, 2).wait_recv()
            self.upstream(at.cq + r, r).wait()

            def block(b):
                up = self.act[at.cq + r, b]
                grad = up.astype(F32) + self.act[at.gmem + r, b].astype(F32)
                grad = self.norm_back(self.norm_back(grad, 2, r, b), 1, r, b)
                self.res[r, b] = grad
                self.act[at.gdown + r, b] = grad.astype(BF16)

            self.blocks(block)

            @pl.when(r == rows - 1)
            def down():
                self.down_grads(steps)

            self.feed_back(r)

            def block(b):
                grad = self.norm_back(self.res[r, b], 0, r, b)
                self.res[r, b] = grad
                self.act[at.gout + r, b] = grad.astype(BF16)

            self.blocks(block)

            @pl.when(r == rows - 1)
            def up():
                self.up_grads(at.first)
                steps.more(1)

            base = steps.next
            steps.next += 4

            def step(n):
                pl.when(r == rows - 1)(functools.partial(steps.run, base + n))

            self.self_back(r, step)

        self.loop(rows, back)
        small = Steps()
        if self.inner:
            small = self.small_steps()
            small.more(1)
        self.self_grads()
        small.more(1)
        steps.more(2)
        small.more(1)
        steps.finish()
        small.finish()
        self.length_copy().wait_send()
        if self.inner:
            self.shard_copy().wait_send()
            for n in range(far_count):
                self.far_copy(n).wait_send()
            self.drain()
        self.x_copy(at.mem, rows - 1, 0).wait_send()
        for r in range(rows):
            self.store(at.mem + r, self.result, r, r).wait()
            self.store(at.stage + r, self.grad_in, r, 2 + r).wait()
        if not self.inner:
            self.keep_grads()

    def reduce_steps(self, tiles):
        stages = [(0, self.reduce1), (2, self.reduce2), (4, self.reduce3), (6, self.reduce4)]
        stages += [(8, self.reduce5), (10, self.reduce6), (11, self.reduce7)]
        return Steps(self, tiles, stages)

    def keep_grads(self):
        tiles = list(range(self.t_all))
        if self.encoding:
            tiles = [k for k in tiles if not self.from_partner(k)]
        else:
            tiles += [self.t_mem, self.t_mem + 1]
        copies = [
            pltpu.make_async_copy(
                self.act.at[self.tile_slot(k)], self.whole_grad(k), self.grad_sem.at[k]
            )
            for k in tiles
        ]
        for copy in copies:
            copy.start()
        for copy in copies:
            copy.wait()
        for j in range(3):
            self.g_gain[pl.ds(j, 1), :] = jnp.sum(self.gacc[j], axis=0, keepdims=True)
            self.g_bias[pl.ds(j, 1), :] = jnp.sum(self.gacc[3 + j], axis=0, keepdims=True)

    def decoder(self):
        at, rows = self.at, self.rows
        for r in range(rows):
            self.upstream(at.gcross + r, r).start()
        steps = Steps()
        if self.inner:
            steps = self.gather_steps([0, 1, 2, 3] + self.far_chunks + [4, 5, 6, 7] + self.feed_chunks)
            self.shard_copy().wait_recv()
            steps.until(8)
        self.self_forward(True, steps)
        steps.until(13 + far_count)

        def ask(r):
            queries = matmul_nn(self.act[at.first + r], self.weight(4)) * query_scale
            self.act[at.cq + r] = queries.astype(BF16)

        self.loop(rows, ask)
        steps.until(steps.count - 4)
        self.length_copy().wait_recv()
        base = steps.next
        steps.next = steps.count

        def middle(r):
            def rest(first, last):
                @pl.when(r == 0)
                def some():
                    for n in range(first, last):
                        steps.run(n)

            self.fill_mask(r, self.src_len, False)
            self.spilled(r, False).wait()
            self.x_copy(at.mem, r, 0).wait_recv()
            for j in range(2):
                self.act[at.kv + j * rows + r] = matmul_nn(
                    self.act[at.mem + r], self.weight(self.w_memory_at + j)
                ).astype(BF16)
            rest(base, base + 2)
            k, v = at.kv + r, at.kv + rows + r
            self.attend(at.cq + r, k, v, at.oc + r, r)
            rest(base + 2, steps.count)
            self.res[r] += matmul_tn(self.act[at.oc + r], self.weight(5))

            def block(b):
                out = self.norm(self.res[r, b], 1, r, b)
                self.res[r, b] = out
                self.act[at.second + r, b] = out.astype(BF16)

            self.blocks(block)
            for t in range(self.ff_tiles):
                self.feed_up(at.second + r, r, t)
            self.feed_down(r)
            self.upstream(at.gcross + r, r).wait()

            def block(b):
                out = self.norm(self.res[r, b], 2, r, b)
                self.act[at.stage + r, b] = out.astype(BF16)
                up = self.act[at.gcross + r, b]
                grad = self.norm_back(up.astype(F32), 2, r, b)
                self.res[r, b] = grad
                self.act[at.gdown + r, b] = grad.astype(BF16)

            self.blocks(block)
            self.store(at.stage + r, self.result, r, r).start()
            self.feed_back(r)

            def block(b):
                grad = self.norm_back(self.res[r, b], 1, r, b)
                self.res[r, b] = grad
                self.act[at.gcross + r, b] = grad.astype(BF16)

            self.blocks(block)
            self.act[at.dout] = matmul_nt(self.weight(5), self.act[at.gcross + r]).astype(BF16)
            self.attend_back(at.cq + r, k, v, at.oc + r, at.dout, r)
            total = matmul_nt(self.act[k], self.weight(self.w_memory_at))
            total = total + matmul_nt(self.act[v], self.weight(self.w_memory_at + 1))
            self.act[at.gmem + r] = total.astype(BF16)
            self.x_copy(at.gmem, r, 2).start()
            self.spilled(r, True).start()
            self.res[r] += matmul_nt(self.act[at.cq + r], self.weight(4))

            def block(b):
                grad = self.norm_back(self.res[r, b], 0, r, b)
                self.res[r, b] = grad
                self.act[at.gout + r, b] = grad.astype(BF16)

            self.blocks(block)

        self.loop(rows, middle)
        steps, small = Steps(), Steps()
        x = self.both(at.mem)

        def memory_grad(j):
            slot = at.kv + j * rows
            self.weight_grad(slot, x, self.both(slot))

        self.loop(2, memory_grad)
        if self.inner:
            feed = list(range(self.t_down, self.t_all)) + list(range(self.t_up, self.t_down))
            steps = self.reduce_steps([self.t_mem, self.t_mem + 1] + feed + [4, 5, 3, 0, 1, 2])
            small = self.small_steps()
        steps.more(2)
        self.down_grads(steps)
        small.more(1)
        self.up_grads(at.second)
        steps.more(1)
        self.weight_grad(at.cq, self.both(at.first), self.both(at.cq))
        self.out_grad(self.t_cross + 1, at.oc, at.gcross)
        base = steps.next
        steps.next += 2 * rows

        def back(r):
            self.spilled(r, True).wait()
            self.store(at.stage + r, self.result, r, r).wait()

            def step(n):
                if n % 2 == 0:
                    for m in range(rows):
                        pl.when(r == m)(functools.partial(steps.run, base + 2 * m + n // 2))

            self.self_back(r, step)

        self.loop(rows, back)
        small.more(1)
        self.self_grads()
        small.more(1)
        steps.finish()
        small.finish()
        if self.inner:
            self.drain()
        for r in range(rows):
            self.x_copy(at.gmem, r, 2).wait_send()
            self.store(at.stage + r, self.grad_in, r, 2 + r).wait()
        if not self.inner:
            self.keep_grads()


def both_layers(inner, dp, call, emb, cot, lengths, gain, bias, weights):
    rows = lengths.shape[0]
    model = emb.shape[1]
    ff_tiles = weights[3].shape[1] // TILE
    tiles = 6 + 2 * ff_tiles
    sums = tiles + 2
    vmem = pl.BlockSpec(memory_space=pltpu.VMEM)
    anywhere = pl.BlockSpec(memory_space=pl.ANY)
    dma = pltpu.SemaphoreType.DMA
    square = (TILE, TILE)
    scratch = [
        pltpu.VMEM(emb.shape, BF16),
        dma((1,)),
        pltpu.VMEM((Slots(rows, ff_tiles).count,) + square, BF16),
        pltpu.VMEM((rows, HEADS) + square, BF16),
        pltpu.VMEM((rows,) + square, F32),
        pltpu.VMEM(square, F32),
        pltpu.VMEM((rows, TILE, 128), F32),
        pltpu.VMEM((6, 8, model), F32),
        pltpu.VMEM((8, 128), jnp.int32),
        pltpu.VMEM((8, 128), jnp.int32),
        dma((8,)),
        dma((8,)),
        dma((8,)),
    ]
    if inner:
        part = TILE // 16
        chunks = 8 + ff_tiles + TILE // down_columns
        scratch += [
            pltpu.VMEM((8 + ff_tiles, LINE, 2, 2, part, TILE), BF16),
            pltpu.VMEM((LINE, 2, 2, weights[4].shape[0], TILE), BF16),
            pltpu.VMEM((part, 2 * TILE), BF16),
            pltpu.VMEM((2, part, TILE), BF16),
            pltpu.VMEM((sums, TILE // 2, TILE), BF16),
            pltpu.VMEM((sums, TILE // 4, TILE), BF16),
            pltpu.VMEM((sums, LINE - 1, part, TILE), BF16),
            pltpu.VMEM((3, 8, model), F32),
            pltpu.VMEM((2 + LINE, 8, model), F32),
        ]
        line = (LINE - 1,)
        scratch += [dma((chunks,))] + [dma((chunks,) + line)] * 2 + [dma((chunks,))] * 4
        scratch += [dma((sums,))] * 4 + [dma((sums,) + line)] * 2
        shard = weights[4].shape[0]
        scratch += [
            pltpu.VMEM((far_count, shard, down_columns), BF16),
            pltpu.VMEM((far_count, LINE, 2, shard, down_columns), BF16),
        ]
        scratch += [dma((far_count,))] * 3 + [dma((far_count,) + line)] * 2 + [dma((far_count,))] * 4
        scratch += [dma((sums,) + line)] * 2
        scratch += [dma((sums,))] * 4 + [dma((sums,)), dma((2 + LINE,)), dma((2 + LINE,))]
    else:
        scratch += [dma((sums,))]

    hidden = ff_tiles * TILE
    grads = [(model, 3 * TILE), square, (model, 2 * TILE), (model, hidden), (hidden, model)]
    if not inner:
        grads += [(model, 2 * TILE)]

    def kernel(*refs):
        Body(inner, rows, dp, ff_tiles, refs).run()

    return pl.pallas_call(
        kernel,
        out_shape=(
            jax.ShapeDtypeStruct(emb.shape, BF16),
            jax.ShapeDtypeStruct(emb.shape, BF16),
            *(jax.ShapeDtypeStruct(shape, BF16) for shape in grads),
            jax.ShapeDtypeStruct(gain.shape, F32),
            jax.ShapeDtypeStruct(bias.shape, F32),
            jax.ShapeDtypeStruct((rows, HEADS) + square, BF16),
        ),
        in_specs=[anywhere] * 2 + [vmem] * 3 + [anywhere if inner else vmem] * len(weights),
        out_specs=(anywhere,) * (2 + len(grads)) + (vmem, vmem, anywhere),
        scratch_shapes=scratch,
        compiler_params=pltpu.CompilerParams(
            collective_id=call, has_side_effects=True, vmem_limit_bytes=62 * 2**20
        ),
        name="layers",
    )(emb, cot, lengths, gain, bias, *weights)


def passed_along(shard, axis, by):
    count = lax.axis_size(axis)
    pairs = [(i, i + by) for i in range(count) if 0 <= i + by < count]
    return lax.ppermute(shard, axis, pairs)


def local(
    embedded,
    lengths,
    cotangent,
    attn_in,
    attn_out,
    cross_weight,
    up_weight,
    down_weight,
    norm_gain,
    norm_bias,
):
    dp = lax.axis_size("dp")
    rows = lengths.shape[1]
    shards = tuple(w[0] for w in (attn_in, attn_out, cross_weight, up_weight, down_weight))
    inner = dp == 4 * LINE and rows <= CALL_ROWS
    args = (embedded[0], cotangent[0], lengths[0], norm_gain[0], norm_bias[0])
    if inner:
        result, grad_in, *grads, gain, bias, spill = both_layers(inner, dp, 0, *args, shards)
        grads = [grad.astype(F32) for grad in grads]
    else:
        weights = tuple(lax.all_gather(w, "dp", axis=0, tiled=True) for w in shards)
        weights += (passed_along(weights[2], "section", 1),)
        parts = []
        for call in range(0, rows, CALL_ROWS):
            span = slice(call * TILE, min(rows, call + CALL_ROWS) * TILE)
            lens = args[2][call : call + CALL_ROWS]
            parts.append(
                both_layers(
                    inner, dp, call // CALL_ROWS, args[0][span], args[1][span], lens, *args[3:], weights
                )
            )
        result = jnp.concatenate([part[0] for part in parts], axis=0)
        grad_in = jnp.concatenate([part[1] for part in parts], axis=0)
        sums = [sum(part[n].astype(F32) for part in parts) for n in range(2, 10)]
        *grads, memory, gain, bias = lax.psum(tuple(sums), "dp")
        is_first = lax.axis_index("section") == 0
        grads[2] = jnp.where(is_first, passed_along(memory, "section", -1), grads[2])
    return tuple(out[None] for out in (result, grad_in, *grads, gain, bias))


def solution(mesh):
    rows = P("section", "dp", None)
    whole = P("section", None, None)
    in_specs = (rows,) * 8 + (whole,) * 2
    out_specs = (rows,) * 2 + (whole,) * 7
    return jax.shard_map(local, mesh=mesh, in_specs=in_specs, out_specs=out_specs, check_vma=False)
```

```python
import functools

import jax
import jax.numpy as jnp
from jax import lax
from jax.experimental import pallas as pl
from jax.experimental.pallas import tpu as pltpu
from jax.sharding import PartitionSpec as P

HEADS = 8

norm_eps = 1e-06
masked_score = -1e30
F32 = jnp.float32
BF16 = jnp.bfloat16
MESH = pl.DeviceIdType.MESH
far_count = 1
down_columns = 128
query_scale = 0.125
LINE = 4
CALL_ROWS = 2
TILE = 512


def matmul_nn(left, right):
    return jnp.dot(left, right, preferred_element_type=F32)


def matmul_tn(left, right):
    return lax.dot_general(left, right, (((0,), (0,)), ((), ())), preferred_element_type=F32)


def matmul_nt(left, right):
    return lax.dot_general(left, right, (((1,), (1,)), ((), ())), preferred_element_type=F32)


class Steps:
    def __init__(self, body=None, items=(), stages=()):
        self.body = body
        self.items = items
        self.stages = stages
        self.count = len(items) + stages[-1][0] if items else 0
        self.next = 0

    def run(self, n):
        if n >= self.count:
            return
        for offset, act in reversed(self.stages):
            if 0 <= n - offset < len(self.items):
                item = self.items[n - offset]
                act(item)
                self.body.done.append((act, item))

    def until(self, n):
        while self.next < n:
            self.run(self.next)
            self.next += 1

    def more(self, n):
        self.until(self.next + n)

    def finish(self):
        self.until(self.count)


class Slots:
    def __init__(self, rows, ff_tiles):
        self.rows = rows
        self.count = 0
        self.qkv = self.take(3 * rows)
        self.cq = self.take(rows)
        self.kv = self.take(2 * rows)
        self.pre = self.take(ff_tiles * rows)
        self.hid = self.take(ff_tiles * rows)
        self.att = self.take(rows)
        self.oc = self.take(rows)
        self.first = self.take(rows)
        self.second = self.take(rows)
        self.mem = self.take(rows)
        self.gmem = self.take(rows)
        self.gdown = self.take(rows)
        self.gout = self.take(rows)
        self.gcross = self.take(rows)
        self.stage = self.take(rows)
        self.dout = self.take(1)
        self.xhat = self.take(3 * rows)

    def take(self, n):
        at = self.count
        self.count += n
        return at


class Body:
    def __init__(self, inner, rows, dp, ff_tiles, refs):
        self.inner = inner
        self.rows = rows
        self.ff_tiles = ff_tiles
        self.at = Slots(rows, ff_tiles)
        names = ["emb_in", "cot", "lengths", "gain", "bias"]
        names += ["w_in", "w_out", "w_cross", "w_up", "w_down"]
        if not inner:
            names += ["w_memory"]
        names += ["result", "grad_in", "g_in", "g_out", "g_cross", "g_up", "g_down"]
        if not inner:
            names += ["g_memory"]
        names += ["g_gain", "g_bias", "spill"]
        names += ["emb", "emb_sem", "act", "probs", "res", "mask", "rstd", "gacc", "own_len", "src_len"]
        names += ["local_sem", "x_send", "x_recv"]
        if not inner:
            names += ["grad_sem"]
        if inner:
            names += ["wt", "wd", "x_shard", "x_grad", "r1", "r2", "r3", "gbuf", "grcv"]
            names += ["gown_sem", "gz_s", "gz_r", "gy_s", "gy_r", "gc_s", "gc_r"]
            names += ["a1_s", "a1_r", "a2_s", "a2_r", "a3_s", "a3_r"]
            names += ["away", "far", "fown_sem", "fa_s", "fa_r", "fz_s", "fz_r"]
            names += ["fy_s", "fy_r", "fx_s", "fx_r", "a4_s", "a4_r", "a5_s", "a5_r"]
            names += ["a6_s", "a6_r", "own_sem", "gs_s", "gs_r"]
        assert len(names) == len(refs), (len(names), len(refs))
        for name, ref in zip(names, refs):
            setattr(self, name, ref)
        self.sec = lax.axis_index("section")
        self.i = lax.axis_index("dp")
        self.across = (1 - self.sec, self.i)
        if inner:
            self.c = lax.rem(self.i, 2)
            self.y = lax.rem(self.i // 2, 2)
            self.z = self.i // 4
            self.core_dev = (self.sec, self.z * 4 + self.y * 2 + (1 - self.c))
            self.y_dev = (self.sec, self.z * 4 + (1 - self.y) * 2 + self.c)
            self.z_other = [lax.rem(self.z + d, LINE) for d in range(1, LINE)]
            self.z_dev = [(self.sec, zz * 4 + self.y * 2 + self.c) for zz in self.z_other]
        self.done = []
        self.draining = False
        self.encoding = True
        self.t_in = 0
        self.t_out = 3
        self.t_cross = 4
        self.t_up = 6
        self.t_down = 6 + ff_tiles
        self.t_all = 6 + 2 * ff_tiles
        self.t_mem = self.t_all
        self.w_memory_at = 6
        self.w_up_at = 8
        self.down_bands = TILE // down_columns
        self.far_at = self.w_up_at + ff_tiles + self.down_bands - far_count
        self.far_shift = far_count
        self.far_chunks = [self.far_at + self.far_shift + n for n in range(far_count)]
        self.feed_chunks = [self.w_up_at + n for n in range(ff_tiles + self.down_bands)]


    def remote(self, src, dst, send, recv, dev):
        return pltpu.make_async_remote_copy(
            src_ref=src, dst_ref=dst, send_sem=send, recv_sem=recv, device_id=dev, device_id_type=MESH
        )

    def send(self, src, dst, send, recv, dev):
        copy = self.remote(src, dst, send, recv, dev)
        if self.draining:
            copy.wait_send()
        else:
            copy.start()

    def drain(self):
        self.draining = True
        for act, item in self.done:
            act(item)
        self.draining = False
        self.done = []

    def barrier(self):
        sem = pltpu.get_barrier_semaphore()
        devs = [self.across]
        if self.inner:
            devs += [self.core_dev, self.y_dev] + self.z_dev
        for dev in devs:
            pl.semaphore_signal(sem, inc=1, device_id=dev, device_id_type=MESH)
        pl.semaphore_wait(sem, len(devs))


    def weight(self, k):
        if self.inner:
            return self.wt[k].reshape(TILE, TILE)
        if k < 3:
            return self.w_in[:, k * TILE : (k + 1) * TILE]
        if k == 3:
            return self.w_out[...]
        if k < 6:
            return self.w_cross[:, (k - 4) * TILE : (k - 3) * TILE]
        if k < 8:
            return self.w_memory[:, (k - 6) * TILE : (k - 5) * TILE]
        return self.w_up[:, (k - 8) * TILE : (k - 7) * TILE]

    def weight_up(self, t):
        if self.inner:
            return self.wt[self.w_up_at + t].reshape(TILE, TILE)
        start = t * TILE
        return self.w_up[:, pl.ds(start if isinstance(start, int) else pl.multiple_of(start, TILE), TILE)]

    def weight_down(self, t):
        if self.inner:
            return self.wd[t].reshape(TILE, TILE)
        return self.w_down[t * TILE : (t + 1) * TILE, :]

    def chunk_source(self, k):
        z, y, c = self.z, self.y, self.c
        down_at = self.w_up_at + self.ff_tiles
        if k < 3:
            src = self.w_in.at[:, pl.ds(k * TILE, TILE)]
        elif k == 3:
            src = self.w_out.at[...]
        elif k < 6:
            src = self.w_cross.at[:, pl.ds((k - 4) * TILE, TILE)]
        elif k < 8:
            src = self.x_shard.at[:, pl.ds((k - 6) * TILE, TILE)]
        elif k < down_at:
            src = self.w_up.at[:, pl.ds((k - 8) * TILE, TILE)]
        else:
            cols = pl.ds((k - down_at) * down_columns, down_columns)
            src = self.w_down.at[:, cols]
        if k < down_at:
            whole = self.wt.at[k]
            own = whole.at[z, y, c]
            line = whole.at[:, y, c]
            plane = whole.at[:, :, c]
        else:
            own = self.wd.at[z, y, c, :, cols]
            line = self.wd.at[:, y, c, :, cols]
            plane = self.wd.at[:, :, c, :, cols]
        return src, own, line, plane

    def gather1(self, k):
        if self.is_far(k):
            return self.far1(k)
        src, own, line, plane = self.chunk_source(k)
        if not self.draining:
            pltpu.make_async_copy(src, own, self.gown_sem.at[k]).start()
        for d in range(LINE - 1):
            self.send(src, own, self.gz_s.at[k, d], self.gz_r.at[k, d], self.z_dev[d])

    def gather2(self, k):
        if self.is_far(k):
            return self.far2(k)
        src, own, line, plane = self.chunk_source(k)
        if not self.draining:
            pltpu.make_async_copy(src, own, self.gown_sem.at[k]).wait()
        for d in range(0 if self.draining else LINE - 1):
            self.remote(src, own, self.gz_s.at[k, d], self.gz_r.at[k, d], self.z_dev[d]).wait_recv()
        self.send(line, line, self.gy_s.at[k], self.gy_r.at[k], self.y_dev)

    def gather3(self, k):
        if self.is_far(k) and not self.encoding:
            return self.far3(k)
        src, own, line, plane = self.chunk_source(k)
        if not self.draining:
            if self.is_far(k):
                n = k - self.far_at
                self.remote(plane, plane, self.fx_s.at[n], self.fx_r.at[n], self.across).wait_recv()
            else:
                self.remote(line, line, self.gy_s.at[k], self.gy_r.at[k], self.y_dev).wait_recv()
        self.send(plane, plane, self.gc_s.at[k], self.gc_r.at[k], self.core_dev)

    def gather4(self, k):
        if self.is_far(k) and not self.encoding:
            return
        src, own, line, plane = self.chunk_source(k)
        if not self.draining:
            self.remote(plane, plane, self.gc_s.at[k], self.gc_r.at[k], self.core_dev).wait_recv()


    def is_far(self, k):
        return k >= self.far_at + (0 if self.encoding else self.far_shift)

    def far_copy(self, n):
        cols = pl.ds((self.down_bands - far_count + n) * down_columns, down_columns)
        return self.remote(
            self.w_down.at[:, cols], self.away.at[n], self.fa_s.at[n], self.fa_r.at[n], self.across
        )

    def far1(self, k):
        if self.encoding:
            return
        n = k - self.far_at - self.far_shift
        src, own = self.away.at[n], self.far.at[n, self.z, self.y]
        if not self.draining:
            self.far_copy(n).wait_recv()
            pltpu.make_async_copy(src, own, self.fown_sem.at[n]).start()
        for d in range(LINE - 1):
            self.send(src, own, self.fz_s.at[n, d], self.fz_r.at[n, d], self.z_dev[d])

    def far2(self, k):
        if self.encoding:
            return
        n = k - self.far_at - self.far_shift
        src, own, line = self.away.at[n], self.far.at[n, self.z, self.y], self.far.at[n, :, self.y]
        if not self.draining:
            pltpu.make_async_copy(src, own, self.fown_sem.at[n]).wait()
            for d in range(LINE - 1):
                self.remote(
                    src, own, self.fz_s.at[n, d], self.fz_r.at[n, d], self.z_dev[d]
                ).wait_recv()
        self.send(line, line, self.fy_s.at[n], self.fy_r.at[n], self.y_dev)

    def far3(self, k):
        n = k - self.far_at - self.far_shift
        line = self.far.at[n, :, self.y]
        if not self.draining:
            self.remote(line, line, self.fy_s.at[n], self.fy_r.at[n], self.y_dev).wait_recv()
        src, own, near, plane = self.chunk_source(self.far_at + n)
        self.send(self.far.at[n], plane, self.fx_s.at[n], self.fx_r.at[n], self.across)

    def gather_steps(self, chunks):
        stages = [(0, self.gather1), (2, self.gather2), (4, self.gather3), (5, self.gather4)]
        return Steps(self, chunks, stages)


    def tile_slot(self, k):
        at, rows = self.at, self.rows
        if k < 3:
            return at.qkv + k * rows
        if k == 3:
            return at.gout
        if k == 4:
            return at.cq
        if k == 5:
            return at.gcross
        if k < self.t_down:
            return at.pre + (k - self.t_up) * rows
        if k < self.t_all:
            return at.hid + (k - self.t_down) * rows
        return at.kv + (k - self.t_mem) * rows

    def whole_grad(self, k, start=0, size=TILE):
        rows = pl.ds(start, size)

        def columns(ref, n):
            return ref.at[rows, pl.ds(n * TILE, TILE)]

        if k < 3:
            return columns(self.g_in, k)
        if k == 3:
            return columns(self.g_out, 0)
        if k < 6:
            return columns(self.g_cross, k - self.t_cross)
        if k < self.t_down:
            return columns(self.g_up, k - self.t_up)
        if k < self.t_all:
            return self.g_down.at[pl.ds((k - self.t_down) * TILE + start, size), :]
        return columns(self.g_memory, k - self.t_mem)

    def from_partner(self, k):
        return self.encoding and k in (self.t_cross, self.t_cross + 1)

    def block_at(self, c, y=0, z=0):
        return c * (TILE // 2) + y * (TILE // 4) + z * (TILE // 16)

    def reduce1(self, k):
        if self.from_partner(k):
            return
        slot = self.tile_slot(k)
        half = TILE // 2
        src = self.act.at[slot, pl.ds(self.block_at(1 - self.c), half)]
        self.send(src, self.r1.at[k], self.a1_s.at[k], self.a1_r.at[k], self.core_dev)

    def reduce2(self, k):
        if self.from_partner(k):
            return
        slot = self.tile_slot(k)
        half, quarter = TILE // 2, TILE // 4
        own = pl.ds(pl.multiple_of(self.block_at(self.c), half), half)
        src = self.act.at[slot, own]
        if not self.draining:
            self.remote(
                src, self.r1.at[k], self.a1_s.at[k], self.a1_r.at[k], self.core_dev
            ).wait_recv()
            total = self.act[slot, own].astype(F32) + self.r1[k].astype(F32)
            self.act[slot, own] = total.astype(BF16)
        src = self.act.at[slot, pl.ds(self.block_at(self.c, 1 - self.y), quarter)]
        self.send(src, self.r2.at[k], self.a2_s.at[k], self.a2_r.at[k], self.y_dev)

    def reduce3(self, k):
        if self.from_partner(k):
            return
        slot = self.tile_slot(k)
        quarter, part = TILE // 4, TILE // 16
        own = pl.ds(pl.multiple_of(self.block_at(self.c, self.y), quarter), quarter)
        src = self.act.at[slot, own]
        if not self.draining:
            self.remote(
                src, self.r2.at[k], self.a2_s.at[k], self.a2_r.at[k], self.y_dev
            ).wait_recv()
            total = self.act[slot, own].astype(F32) + self.r2[k].astype(F32)
            self.act[slot, own] = total.astype(BF16)
        for d in range(LINE - 1):
            src = self.act.at[slot, pl.ds(self.block_at(self.c, self.y, self.z_other[d]), part)]
            self.send(src, self.r3.at[k, d], self.a3_s.at[k, d], self.a3_r.at[k, d], self.z_dev[d])

    def reduce4(self, k):
        if self.from_partner(k):
            return self.reduce4_memory(k)
        slot = self.tile_slot(k)
        part = TILE // 16
        own = pl.ds(pl.multiple_of(self.block_at(self.c, self.y, self.z), part), part)
        src = self.act.at[slot, own]
        if not self.draining:
            total = self.act[slot, own].astype(F32)
            for d in range(LINE - 1):
                self.remote(
                    src, self.r3.at[k, d], self.a3_s.at[k, d], self.a3_r.at[k, d], self.z_dev[d]
                ).wait_recv()
                total = total + self.r3[k, d].astype(F32)
            self.act[slot, own] = total.astype(BF16)
        if k < self.t_all:
            self.spread(k, src)
        else:
            j = k - self.t_mem
            dst = self.x_grad.at[j]
            self.send(src, dst, self.x_send.at[6 + j], self.x_recv.at[6 + j], self.across)

    def spread(self, k, src):
        part = TILE // 16
        dst = self.whole_grad(k, self.block_at(self.c, self.y, self.z), part)
        if not self.draining:
            pltpu.make_async_copy(src, dst, self.own_sem.at[k]).start()
        for d in range(LINE - 1):
            self.send(src, dst, self.a4_s.at[k, d], self.a4_r.at[k, d], self.z_dev[d])

    def reduce4_memory(self, k):
        j = k - self.t_cross
        src = self.x_grad.at[j]
        if not self.draining:
            self.remote(
                src, src, self.x_send.at[6 + j], self.x_recv.at[6 + j], self.across
            ).wait_recv()
        self.spread(k, src)

    def reduce5(self, k):
        if k >= self.t_all:
            return
        quarter, part = TILE // 4, TILE // 16
        own = self.whole_grad(k, self.block_at(self.c, self.y, self.z), part)
        if not self.draining:
            pltpu.make_async_copy(own, own, self.own_sem.at[k]).wait()
        for d in range(0 if self.draining else LINE - 1):
            self.remote(
                own, own, self.a4_s.at[k, d], self.a4_r.at[k, d], self.z_dev[d]
            ).wait_recv()
        line = self.whole_grad(k, self.block_at(self.c, self.y), quarter)
        self.send(line, line, self.a5_s.at[k], self.a5_r.at[k], self.y_dev)

    def reduce6(self, k):
        if k >= self.t_all:
            return
        half, quarter = TILE // 2, TILE // 4
        line = self.whole_grad(k, self.block_at(self.c, self.y), quarter)
        if not self.draining:
            self.remote(line, line, self.a5_s.at[k], self.a5_r.at[k], self.y_dev).wait_recv()
        plane = self.whole_grad(k, self.block_at(self.c), half)
        self.send(plane, plane, self.a6_s.at[k], self.a6_r.at[k], self.core_dev)

    def reduce7(self, k):
        if k >= self.t_all:
            return
        plane = self.whole_grad(k, self.block_at(self.c), TILE // 2)
        if not self.draining:
            self.remote(plane, plane, self.a6_s.at[k], self.a6_r.at[k], self.core_dev).wait_recv()

    def small_steps(self):
        stages = [(0, self.small1), (1, self.small2), (2, self.small3), (3, self.small4)]
        return Steps(self, [0], stages)

    def small1(self, item):
        if not self.draining:
            for j in range(6):
                self.gbuf[0, pl.ds(j, 1), :] = jnp.sum(self.gacc[j], axis=0, keepdims=True)
            self.gbuf[0, pl.ds(6, 2), :] = jnp.zeros((2, TILE), F32)
        self.send(self.gbuf.at[0], self.grcv.at[0], self.gs_s.at[0], self.gs_r.at[0], self.core_dev)

    def small2(self, item):
        if not self.draining:
            self.remote(
                self.gbuf.at[0], self.grcv.at[0], self.gs_s.at[0], self.gs_r.at[0], self.core_dev
            ).wait_recv()
            self.gbuf[1] = self.gbuf[0] + self.grcv[0]
        self.send(self.gbuf.at[1], self.grcv.at[1], self.gs_s.at[1], self.gs_r.at[1], self.y_dev)

    def small3(self, item):
        if not self.draining:
            self.remote(
                self.gbuf.at[1], self.grcv.at[1], self.gs_s.at[1], self.gs_r.at[1], self.y_dev
            ).wait_recv()
            self.gbuf[2] = self.gbuf[1] + self.grcv[1]
        for d in range(LINE - 1):
            self.send(
                self.gbuf.at[2],
                self.grcv.at[2 + self.z],
                self.gs_s.at[2 + d],
                self.gs_r.at[2 + d],
                self.z_dev[d],
            )
        if not self.draining:
            self.grcv[2 + self.z] = self.gbuf[2]

    def small4(self, item):
        if self.draining:
            return
        for d in range(LINE - 1):
            self.remote(
                self.gbuf.at[2],
                self.grcv.at[2 + self.z],
                self.gs_s.at[2 + d],
                self.gs_r.at[2 + d],
                self.z_dev[d],
            ).wait_recv()
        total = self.grcv[2]
        for n in range(1, LINE):
            total = total + self.grcv[2 + n]
        self.g_gain[...] = total[0:3]
        self.g_bias[...] = total[3:6]


    def fill_mask(self, r, key_len, causal):
        lane = lax.broadcasted_iota(jnp.int32, (8, 128), 1)
        sub = lax.broadcasted_iota(jnp.int32, (8, 128), 0)

        def ends_of(ref):
            spans = jnp.broadcast_to(ref[pl.ds(r, 1), :], (8, 128))
            return jnp.sum(jnp.where(lane <= sub, spans, 0).astype(F32), axis=1, keepdims=True)

        ends = ends_of(key_len)
        flat = jnp.sum(jnp.where(lane == sub, ends, 0.0), axis=0, keepdims=True)
        flat = jnp.where(lane[:1] < 8, flat, 1e9)
        pos = lax.broadcasted_iota(jnp.int32, (TILE, 128), 0).astype(F32)
        key_ids = jnp.sum(jnp.where(pos >= flat, 1.0, 0.0), axis=1, keepdims=True)
        query_ends = ends_of(self.own_len)
        pos = lax.broadcasted_iota(jnp.int32, (8, TILE), 1).astype(F32)
        query_ids = jnp.sum(jnp.where(pos >= query_ends, 1.0, 0.0), axis=0, keepdims=True)
        step = 128
        for b in range(TILE // step):
            allowed = key_ids[b * step : (b + 1) * step] == query_ids
            if causal:
                k_pos = lax.broadcasted_iota(jnp.int32, (step, TILE), 0) + b * step
                q_pos = lax.broadcasted_iota(jnp.int32, (step, TILE), 1)
                allowed = allowed & (k_pos <= q_pos)
            self.mask[b * step : (b + 1) * step, :] = jnp.where(allowed, 0.0, masked_score)


    def attend(self, q, k, v, out, r, first=0, count=HEADS // 2):
        act = self.act
        low = lax.broadcasted_iota(jnp.int32, (1, 128), 1) < 64

        def pair(n, carry):
            hp = first + n
            cols = pl.ds(pl.multiple_of(hp * 128, 128), 128)
            qs, ks, vs = act[q, :, cols], act[k, :, cols], act[v, :, cols]
            scores = []
            for j in range(2):
                qm = jnp.where(low if j == 0 else ~low, qs, jnp.zeros_like(qs))
                s = matmul_nt(ks, qm) + self.mask[...]
                scores.append((s, jnp.max(s, axis=0, keepdims=True)))
            weights = []
            for j, (s, top) in enumerate(scores):
                raised = jnp.exp(s - top)
                raised = raised * (1.0 / jnp.sum(raised, axis=0, keepdims=True))
                weights.append(raised.astype(BF16))
                self.probs[r, hp * 2 + j] = weights[j]
            for j, probs in enumerate(weights):
                o = matmul_tn(vs, probs)[64 * j : 64 * j + 64]
                rows = pl.ds(pl.multiple_of(hp * 128 + 64 * j, 64), 64)
                act[out, rows, :] = o.astype(BF16)
            return carry

        lax.fori_loop(0, count, pair, 0)

    def attend_back(self, q, k, v, out, dout, r, first=0, count=HEADS // 2):
        act = self.act
        low = lax.broadcasted_iota(jnp.int32, (1, 128), 1) < 64

        def pair(n, carry):
            hp = first + n
            cols = pl.ds(pl.multiple_of(hp * 128, 128), 128)
            qs, ks, vs = act[q, :, cols], act[k, :, cols], act[v, :, cols]
            grads = []
            for j in range(2):
                rows = pl.ds(pl.multiple_of(hp * 128 + 64 * j, 64), 64)
                do = act[dout, rows, :]
                prod = do.astype(F32) * act[out, rows, :].astype(F32)
                delta = jnp.sum(prod, axis=0, keepdims=True)
                none = jnp.zeros_like(do)
                do = jnp.concatenate([do, none] if j == 0 else [none, do], axis=0)
                grads.append((do, delta, matmul_nn(vs, do)))
            scores = []
            for j, (do, delta, dp) in enumerate(grads):
                probs = self.probs[r, hp * 2 + j]
                scores.append((probs, (probs.astype(F32) * (dp - delta)).astype(BF16)))
            dq, dk, dv = [], None, None
            for j, (probs, ds) in enumerate(scores):
                qm = jnp.where(low if j == 0 else ~low, qs, jnp.zeros_like(qs))
                a, b = matmul_nt(probs, grads[j][0]), matmul_nn(ds, qm)
                dv, dk = (a, b) if j == 0 else (dv + a, dk + b)
                dq.append(matmul_tn(ks, ds)[64 * j : 64 * j + 64])
            dq = (jnp.concatenate(dq, axis=0) * 0.125).astype(BF16)
            act[q, :, cols] = dq.T
            act[k, :, cols] = dk.astype(BF16)
            act[v, :, cols] = dv.astype(BF16)
            return carry

        lax.fori_loop(0, count, pair, 0)


    def blocks(self, body):
        step = 128

        def one(b, carry):
            body(pl.ds(pl.multiple_of(b * step, step), step))
            return carry

        lax.fori_loop(0, TILE // step, one, 0, unroll=True)

    def norm(self, values, n, r, rows):
        center = jnp.mean(values, axis=-1, keepdims=True)
        shifted = values - center
        scale = lax.rsqrt(jnp.mean(shifted * shifted, axis=-1, keepdims=True) + norm_eps)
        hat = shifted * scale
        self.act[self.at.xhat + n * self.rows + r, rows] = hat.astype(BF16)
        self.rstd[r, rows, pl.ds(n, 1)] = scale
        return hat * self.gain[pl.ds(n, 1), :] + self.bias[pl.ds(n, 1), :]

    def norm_back(self, grad, n, r, rows):
        hat = self.act[self.at.xhat + n * self.rows + r, rows].astype(F32)
        scale = self.rstd[r, rows, pl.ds(n, 1)]
        count = grad.shape[0] // 8
        self.gacc[n] += jnp.sum((grad * hat).reshape(count, 8, TILE), axis=0)
        self.gacc[3 + n] += jnp.sum(grad.reshape(count, 8, TILE), axis=0)
        up = grad * self.gain[pl.ds(n, 1), :]
        first = jnp.mean(up, axis=-1, keepdims=True)
        second = jnp.mean(up * hat, axis=-1, keepdims=True)
        return (up - first - hat * second) * scale


    def row(self, r):
        start = r * TILE
        return pl.ds(start if isinstance(start, int) else pl.multiple_of(start, TILE), TILE)

    def loop(self, count, body):
        def one(n, carry):
            body(n)
            return carry

        lax.fori_loop(0, count, one, 0)

    def self_in(self, r):
        x = self.emb[self.row(r), :]
        for j in range(3):
            rows = matmul_nn(x, self.weight(j))
            if j == 0:
                rows = rows * query_scale
            self.act[self.at.qkv + j * self.rows + r] = rows.astype(BF16)

    def self_forward(self, causal, steps):
        at, rows = self.at, self.rows
        base = steps.next
        steps.next += 3 * rows

        def one(r):
            self.self_in(r)
            for n in range(rows):
                pl.when(r == n)(functools.partial(steps.run, base + 3 * n))
            self.fill_mask(r, self.own_len, causal)
            q, k, v = (at.qkv + j * rows + r for j in range(3))

            def half(h):
                self.attend(q, k, v, at.att + r, r, 2 * h, 2)
                for n in range(rows):
                    for m in range(2):
                        pl.when((r == n) & (h == m))(
                            functools.partial(steps.run, base + 3 * n + 1 + m)
                        )

            self.loop(HEADS // 4, half)
            if not self.encoding:
                self.spilled(r, False).start()
            self.self_out(r)

        self.loop(rows, one)

    def self_out(self, r):
        at = self.at
        x = self.emb[self.row(r), :].astype(F32)
        self.res[r] = x + matmul_tn(self.act[at.att + r], self.weight(3))

        def block(rows):
            out = self.norm(self.res[r, rows], 0, r, rows)
            self.res[r, rows] = out
            self.act[at.first + r, rows] = out.astype(BF16)

        self.blocks(block)

    def feed_up(self, x_slot, r, t):
        at = self.at
        pre = matmul_nn(self.act[x_slot], self.weight_up(t))
        hid = (pre / (1.0 + jnp.exp(-pre))).astype(BF16)
        self.act[at.pre + t * self.rows + r] = pre.astype(BF16)
        self.act[at.hid + t * self.rows + r] = hid

    def feed_down(self, r):
        total = self.res[r]
        for t in range(self.ff_tiles):
            hid = self.act[self.at.hid + t * self.rows + r]
            total = total + matmul_nn(hid, self.weight_down(t))
        self.res[r] = total

    def feed_back(self, r):
        at = self.at
        grad = self.act[at.gdown + r]
        total = None
        for t in range(self.ff_tiles):
            dh = matmul_nt(grad, self.weight_down(t))
            pre = self.act[at.pre + t * self.rows + r].astype(F32)
            s = 1.0 / (1.0 + jnp.exp(-pre))
            dp = (dh * (s * (1.0 + pre * (1.0 - s)))).astype(BF16)
            self.act[at.pre + t * self.rows + r] = dp
            part = matmul_nt(dp, self.weight_up(t))
            total = part if total is None else total + part
        self.res[r] += total

    def self_back(self, r, step):
        at = self.at
        self.act[at.dout] = matmul_nt(self.weight(3), self.act[at.gout + r]).astype(BF16)
        step(0)
        q, k, v = (at.qkv + j * self.rows + r for j in range(3))

        def half(h):
            self.attend_back(q, k, v, at.att + r, at.dout, r, 2 * h, 2)
            for m in range(2):
                pl.when(h == m)(functools.partial(step, 1 + m))

        self.loop(HEADS // 4, half)
        total = self.res[r]
        for j in range(3):
            total = total + matmul_nt(self.act[at.qkv + j * self.rows + r], self.weight(j))
        self.act[at.stage + r] = total.astype(BF16)
        step(3)
        self.store(at.stage + r, self.grad_in, r, 2 + r).start()

    def both(self, slot):
        return self.act[pl.ds(slot, self.rows)].reshape(self.rows * TILE, TILE)

    def weight_grad(self, slot, left, right):
        self.act[slot] = matmul_tn(left, right).astype(BF16)

    def out_grad(self, k, left, right):
        total = matmul_nn(self.act[left], self.act[right])
        for r in range(1, self.rows):
            total = total + matmul_nn(self.act[left + r], self.act[right + r])
        self.act[self.tile_slot(k)] = total.astype(BF16)

    def down_grads(self, steps):
        at, rows = self.at, self.rows
        grad = self.both(at.gdown)
        base = steps.next
        steps.next += self.ff_tiles

        def part(t):
            slot = at.hid + t * rows
            self.weight_grad(slot, self.both(slot), grad)
            for n in range(self.ff_tiles):
                pl.when(t == n)(functools.partial(steps.run, base + n))

        self.loop(self.ff_tiles, part)

    def up_grads(self, x_slot):
        at, rows = self.at, self.rows
        x = self.both(x_slot)

        def part(t):
            slot = at.pre + t * rows
            self.weight_grad(slot, x, self.both(slot))

        self.loop(self.ff_tiles, part)

    def self_grads(self):
        at = self.at
        x = self.emb[...]

        def part(j):
            slot = at.qkv + j * self.rows
            self.weight_grad(slot, x, self.both(slot))

        self.loop(3, part)
        self.out_grad(self.t_out, at.att, at.gout)


    def store(self, slot, out, r, sem):
        return pltpu.make_async_copy(
            self.act.at[slot], out.at[self.row(r), :], self.local_sem.at[sem]
        )

    def spilled(self, r, back):
        a, b = self.probs.at[r], self.spill.at[r]
        return pltpu.make_async_copy(*((b, a) if back else (a, b)), self.local_sem.at[4 + r])

    def upstream(self, slot, r):
        return pltpu.make_async_copy(
            self.cot.at[self.row(r), :], self.act.at[slot], self.local_sem.at[6 + r]
        )

    def x_copy(self, slot, r, sem):
        ref = self.act.at[slot + r]
        return self.remote(ref, ref, self.x_send.at[sem + r], self.x_recv.at[sem + r], self.across)

    def length_copy(self):
        return self.remote(
            self.own_len, self.src_len, self.x_send.at[4], self.x_recv.at[4], self.across
        )

    def shard_copy(self):
        return self.remote(
            self.w_cross, self.x_shard, self.x_send.at[5], self.x_recv.at[5], self.across
        )


    def run(self):
        rows_in = pltpu.make_async_copy(self.emb_in, self.emb, self.emb_sem.at[0])
        rows_in.start()
        self.gacc[...] = jnp.zeros(self.gacc.shape, F32)
        self.own_len[...] = jnp.zeros(self.own_len.shape, jnp.int32)
        self.own_len[pl.ds(0, self.rows), pl.ds(0, self.lengths.shape[1])] = self.lengths[...]
        self.barrier()
        rows_in.wait()

        @pl.when(self.sec == 0)
        def first():
            self.encoding = True
            self.encoder()

        @pl.when(self.sec == 1)
        def second():
            self.encoding = False
            self.decoder()

    def encoder(self):
        at, rows = self.at, self.rows
        self.length_copy().start()
        for r in range(rows):
            self.upstream(at.cq + r, r).start()
        steps = Steps()
        if self.inner:
            self.shard_copy().start()
            for n in range(far_count):
                self.far_copy(n).start()
            steps = self.gather_steps([0, 1, 2, 3] + self.feed_chunks)
            steps.until(8)
        self.self_forward(False, steps)
        steps.finish()

        def send(r):
            for t in range(self.ff_tiles):
                self.feed_up(at.first + r, r, t)
            self.feed_down(r)

            def block(b):
                second = self.norm(self.res[r, b], 1, r, b)
                self.act[at.mem + r, b] = self.norm(second, 2, r, b).astype(BF16)

            self.blocks(block)
            pl.when(r > 0)(lambda: self.x_copy(at.mem, r - 1, 0).wait_send())
            self.x_copy(at.mem, r, 0).start()
            self.store(at.mem + r, self.result, r, r).start()

        self.loop(rows, send)
        steps = Steps()
        if self.inner:
            feed = list(range(self.t_down, self.t_all)) + list(range(self.t_up, self.t_down))
            steps = self.reduce_steps(feed + [4, 5, 3, 0, 1, 2])

        def back(r):
            self.x_copy(at.gmem, r, 2).wait_recv()
            self.upstream(at.cq + r, r).wait()

            def block(b):
                up = self.act[at.cq + r, b]
                grad = up.astype(F32) + self.act[at.gmem + r, b].astype(F32)
                grad = self.norm_back(self.norm_back(grad, 2, r, b), 1, r, b)
                self.res[r, b] = grad
                self.act[at.gdown + r, b] = grad.astype(BF16)

            self.blocks(block)

            @pl.when(r == rows - 1)
            def down():
                self.down_grads(steps)

            self.feed_back(r)

            def block(b):
                grad = self.norm_back(self.res[r, b], 0, r, b)
                self.res[r, b] = grad
                self.act[at.gout + r, b] = grad.astype(BF16)

            self.blocks(block)

            @pl.when(r == rows - 1)
            def up():
                self.up_grads(at.first)
                steps.more(1)

            base = steps.next
            steps.next += 4

            def step(n):
                pl.when(r == rows - 1)(functools.partial(steps.run, base + n))

            self.self_back(r, step)

        self.loop(rows, back)
        small = Steps()
        if self.inner:
            small = self.small_steps()
            small.more(1)
        self.self_grads()
        small.more(1)
        steps.more(2)
        small.more(1)
        steps.finish()
        small.finish()
        self.length_copy().wait_send()
        if self.inner:
            self.shard_copy().wait_send()
            for n in range(far_count):
                self.far_copy(n).wait_send()
            self.drain()
        self.x_copy(at.mem, rows - 1, 0).wait_send()
        for r in range(rows):
            self.store(at.mem + r, self.result, r, r).wait()
            self.store(at.stage + r, self.grad_in, r, 2 + r).wait()
        if not self.inner:
            self.keep_grads()

    def reduce_steps(self, tiles):
        stages = [(0, self.reduce1), (2, self.reduce2), (4, self.reduce3), (6, self.reduce4)]
        stages += [(8, self.reduce5), (10, self.reduce6), (11, self.reduce7)]
        return Steps(self, tiles, stages)

    def keep_grads(self):
        tiles = list(range(self.t_all))
        if self.encoding:
            tiles = [k for k in tiles if not self.from_partner(k)]
        else:
            tiles += [self.t_mem, self.t_mem + 1]
        copies = [
            pltpu.make_async_copy(
                self.act.at[self.tile_slot(k)], self.whole_grad(k), self.grad_sem.at[k]
            )
            for k in tiles
        ]
        for copy in copies:
            copy.start()
        for copy in copies:
            copy.wait()
        for j in range(3):
            self.g_gain[pl.ds(j, 1), :] = jnp.sum(self.gacc[j], axis=0, keepdims=True)
            self.g_bias[pl.ds(j, 1), :] = jnp.sum(self.gacc[3 + j], axis=0, keepdims=True)

    def decoder(self):
        at, rows = self.at, self.rows
        for r in range(rows):
            self.upstream(at.gcross + r, r).start()
        steps = Steps()
        if self.inner:
            steps = self.gather_steps([0, 1, 2, 3] + self.far_chunks + [4, 5, 6, 7] + self.feed_chunks)
            self.shard_copy().wait_recv()
            steps.until(8)
        self.self_forward(True, steps)
        steps.until(13 + far_count)

        def ask(r):
            queries = matmul_nn(self.act[at.first + r], self.weight(4)) * query_scale
            self.act[at.cq + r] = queries.astype(BF16)

        self.loop(rows, ask)
        steps.until(steps.count - 4)
        self.length_copy().wait_recv()
        base = steps.next
        steps.next = steps.count

        def middle(r):
            def rest(first, last):
                @pl.when(r == 0)
                def some():
                    for n in range(first, last):
                        steps.run(n)

            self.fill_mask(r, self.src_len, False)
            self.spilled(r, False).wait()
            self.x_copy(at.mem, r, 0).wait_recv()
            for j in range(2):
                self.act[at.kv + j * rows + r] = matmul_nn(
                    self.act[at.mem + r], self.weight(self.w_memory_at + j)
                ).astype(BF16)
            rest(base, base + 2)
            k, v = at.kv + r, at.kv + rows + r
            self.attend(at.cq + r, k, v, at.oc + r, r)
            rest(base + 2, steps.count)
            self.res[r] += matmul_tn(self.act[at.oc + r], self.weight(5))

            def block(b):
                out = self.norm(self.res[r, b], 1, r, b)
                self.res[r, b] = out
                self.act[at.second + r, b] = out.astype(BF16)

            self.blocks(block)
            for t in range(self.ff_tiles):
                self.feed_up(at.second + r, r, t)
            self.feed_down(r)
            self.upstream(at.gcross + r, r).wait()

            def block(b):
                out = self.norm(self.res[r, b], 2, r, b)
                self.act[at.stage + r, b] = out.astype(BF16)
                up = self.act[at.gcross + r, b]
                grad = self.norm_back(up.astype(F32), 2, r, b)
                self.res[r, b] = grad
                self.act[at.gdown + r, b] = grad.astype(BF16)

            self.blocks(block)
            self.store(at.stage + r, self.result, r, r).start()
            self.feed_back(r)

            def block(b):
                grad = self.norm_back(self.res[r, b], 1, r, b)
                self.res[r, b] = grad
                self.act[at.gcross + r, b] = grad.astype(BF16)

            self.blocks(block)
            self.act[at.dout] = matmul_nt(self.weight(5), self.act[at.gcross + r]).astype(BF16)
            self.attend_back(at.cq + r, k, v, at.oc + r, at.dout, r)
            total = matmul_nt(self.act[k], self.weight(self.w_memory_at))
            total = total + matmul_nt(self.act[v], self.weight(self.w_memory_at + 1))
            self.act[at.gmem + r] = total.astype(BF16)
            self.x_copy(at.gmem, r, 2).start()
            self.spilled(r, True).start()

        self.loop(rows, middle)
        steps, small = Steps(), Steps()
        x = self.both(at.mem)

        def memory_grad(j):
            slot = at.kv + j * rows
            self.weight_grad(slot, x, self.both(slot))

        self.loop(2, memory_grad)
        if self.inner:
            feed = list(range(self.t_down, self.t_all)) + list(range(self.t_up, self.t_down))
            steps = self.reduce_steps([self.t_mem, self.t_mem + 1] + feed + [4, 5, 3, 0, 1, 2])
            small = self.small_steps()
        steps.more(2)
        self.down_grads(steps)

        def first_norm(r):
            self.res[r] += matmul_nt(self.act[at.cq + r], self.weight(4))

            def block(b):
                grad = self.norm_back(self.res[r, b], 0, r, b)
                self.res[r, b] = grad
                self.act[at.gout + r, b] = grad.astype(BF16)

            self.blocks(block)

        self.loop(rows, first_norm)
        small.more(1)
        self.up_grads(at.second)
        steps.more(1)
        self.weight_grad(at.cq, self.both(at.first), self.both(at.cq))
        self.out_grad(self.t_cross + 1, at.oc, at.gcross)
        base = steps.next
        steps.next += 2 * rows

        def back(r):
            self.spilled(r, True).wait()
            self.store(at.stage + r, self.result, r, r).wait()

            def step(n):
                if n % 2 == 0:
                    for m in range(rows):
                        pl.when(r == m)(functools.partial(steps.run, base + 2 * m + n // 2))

            self.self_back(r, step)

        self.loop(rows, back)
        small.more(1)
        self.self_grads()
        small.more(1)
        steps.finish()
        small.finish()
        if self.inner:
            self.drain()
        for r in range(rows):
            self.x_copy(at.gmem, r, 2).wait_send()
            self.store(at.stage + r, self.grad_in, r, 2 + r).wait()
        if not self.inner:
            self.keep_grads()


def both_layers(inner, dp, call, emb, cot, lengths, gain, bias, weights):
    rows = lengths.shape[0]
    model = emb.shape[1]
    ff_tiles = weights[3].shape[1] // TILE
    tiles = 6 + 2 * ff_tiles
    sums = tiles + 2
    vmem = pl.BlockSpec(memory_space=pltpu.VMEM)
    anywhere = pl.BlockSpec(memory_space=pl.ANY)
    dma = pltpu.SemaphoreType.DMA
    square = (TILE, TILE)
    scratch = [
        pltpu.VMEM(emb.shape, BF16),
        dma((1,)),
        pltpu.VMEM((Slots(rows, ff_tiles).count,) + square, BF16),
        pltpu.VMEM((rows, HEADS) + square, BF16),
        pltpu.VMEM((rows,) + square, F32),
        pltpu.VMEM(square, F32),
        pltpu.VMEM((rows, TILE, 128), F32),
        pltpu.VMEM((6, 8, model), F32),
        pltpu.VMEM((8, 128), jnp.int32),
        pltpu.VMEM((8, 128), jnp.int32),
        dma((8,)),
        dma((8,)),
        dma((8,)),
    ]
    if inner:
        part = TILE // 16
        chunks = 8 + ff_tiles + TILE // down_columns
        scratch += [
            pltpu.VMEM((8 + ff_tiles, LINE, 2, 2, part, TILE), BF16),
            pltpu.VMEM((LINE, 2, 2, weights[4].shape[0], TILE), BF16),
            pltpu.VMEM((part, 2 * TILE), BF16),
            pltpu.VMEM((2, part, TILE), BF16),
            pltpu.VMEM((sums, TILE // 2, TILE), BF16),
            pltpu.VMEM((sums, TILE // 4, TILE), BF16),
            pltpu.VMEM((sums, LINE - 1, part, TILE), BF16),
            pltpu.VMEM((3, 8, model), F32),
            pltpu.VMEM((2 + LINE, 8, model), F32),
        ]
        line = (LINE - 1,)
        scratch += [dma((chunks,))] + [dma((chunks,) + line)] * 2 + [dma((chunks,))] * 4
        scratch += [dma((sums,))] * 4 + [dma((sums,) + line)] * 2
        shard = weights[4].shape[0]
        scratch += [
            pltpu.VMEM((far_count, shard, down_columns), BF16),
            pltpu.VMEM((far_count, LINE, 2, shard, down_columns), BF16),
        ]
        scratch += [dma((far_count,))] * 3 + [dma((far_count,) + line)] * 2 + [dma((far_count,))] * 4
        scratch += [dma((sums,) + line)] * 2
        scratch += [dma((sums,))] * 4 + [dma((sums,)), dma((2 + LINE,)), dma((2 + LINE,))]
    else:
        scratch += [dma((sums,))]

    hidden = ff_tiles * TILE
    grads = [(model, 3 * TILE), square, (model, 2 * TILE), (model, hidden), (hidden, model)]
    if not inner:
        grads += [(model, 2 * TILE)]

    def kernel(*refs):
        Body(inner, rows, dp, ff_tiles, refs).run()

    return pl.pallas_call(
        kernel,
        out_shape=(
            jax.ShapeDtypeStruct(emb.shape, BF16),
            jax.ShapeDtypeStruct(emb.shape, BF16),
            *(jax.ShapeDtypeStruct(shape, BF16) for shape in grads),
            jax.ShapeDtypeStruct(gain.shape, F32),
            jax.ShapeDtypeStruct(bias.shape, F32),
            jax.ShapeDtypeStruct((rows, HEADS) + square, BF16),
        ),
        in_specs=[anywhere] * 2 + [vmem] * 3 + [anywhere if inner else vmem] * len(weights),
        out_specs=(anywhere,) * (2 + len(grads)) + (vmem, vmem, anywhere),
        scratch_shapes=scratch,
        compiler_params=pltpu.CompilerParams(
            collective_id=call, has_side_effects=True, vmem_limit_bytes=62 * 2**20
        ),
        name="layers",
    )(emb, cot, lengths, gain, bias, *weights)


def passed_along(shard, axis, by):
    count = lax.axis_size(axis)
    pairs = [(i, i + by) for i in range(count) if 0 <= i + by < count]
    return lax.ppermute(shard, axis, pairs)


def local(
    embedded,
    lengths,
    cotangent,
    attn_in,
    attn_out,
    cross_weight,
    up_weight,
    down_weight,
    norm_gain,
    norm_bias,
):
    dp = lax.axis_size("dp")
    rows = lengths.shape[1]
    shards = tuple(w[0] for w in (attn_in, attn_out, cross_weight, up_weight, down_weight))
    inner = dp == 4 * LINE and rows <= CALL_ROWS
    args = (embedded[0], cotangent[0], lengths[0], norm_gain[0], norm_bias[0])
    if inner:
        result, grad_in, *grads, gain, bias, spill = both_layers(inner, dp, 0, *args, shards)
        grads = [grad.astype(F32) for grad in grads]
    else:
        weights = tuple(lax.all_gather(w, "dp", axis=0, tiled=True) for w in shards)
        weights += (passed_along(weights[2], "section", 1),)
        parts = []
        for call in range(0, rows, CALL_ROWS):
            span = slice(call * TILE, min(rows, call + CALL_ROWS) * TILE)
            lens = args[2][call : call + CALL_ROWS]
            parts.append(
                both_layers(
                    inner, dp, call // CALL_ROWS, args[0][span], args[1][span], lens, *args[3:], weights
                )
            )
        result = jnp.concatenate([part[0] for part in parts], axis=0)
        grad_in = jnp.concatenate([part[1] for part in parts], axis=0)
        sums = [sum(part[n].astype(F32) for part in parts) for n in range(2, 10)]
        *grads, memory, gain, bias = lax.psum(tuple(sums), "dp")
        is_first = lax.axis_index("section") == 0
        grads[2] = jnp.where(is_first, passed_along(memory, "section", -1), grads[2])
    return tuple(out[None] for out in (result, grad_in, *grads, gain, bias))


def solution(mesh):
    rows = P("section", "dp", None)
    whole = P("section", None, None)
    in_specs = (rows,) * 8 + (whole,) * 2
    out_specs = (rows,) * 2 + (whole,) * 7
    return jax.shard_map(local, mesh=mesh, in_specs=in_specs, out_specs=out_specs, check_vma=False)
```
